256 devices in a mesh: rows: 64 (over z, x, core), ch: 4 (over y).
Axes of the slice: x: 4, y: 4, z: 8, core: 2. Of those that a mesh axis runs over, the one named last changes fastest.
Arguments:
- features: bfloat16 [256, 64, 2048], P('rows', None, 'ch'), may hold values from -6 to 6
- low_level: bfloat16 [1024, 256, 256], P('rows'), may hold values from -6 to 6
- labels: int32 [1024, 256], P('rows'), may hold values from 0 to 20
- crop_rows: int32 [8], replicated, may hold values from 1 to 144, 256 in all
- w_one: bfloat16 [2048, 256], P('rows', 'ch'), may hold values from -0.125 to 0.125
- w_atrous: bfloat16 [2048, 3, 3, 3, 256], P('rows', None, None, None, 'ch'), may hold values from -0.046875 to 0.046875
- w_pool: bfloat16 [2048, 256], P('rows', 'ch'), may hold values from -0.125 to 0.125
- w_proj: bfloat16 [1280, 256], P('rows', 'ch'), may hold values from -0.15625 to 0.15625
- w_low: bfloat16 [256, 48], P('rows', 'ch'), may hold values from -0.375 to 0.375
- w_unite_up: bfloat16 [256, 3, 3, 256], P('rows', None, None, 'ch'), may hold values from -0.109375 to 0.109375
- w_unite_low: bfloat16 [48, 3, 3, 256], P(None, None, None, 'ch'), may hold values from -0.109375 to 0.109375
- w_refine: bfloat16 [256, 3, 3, 256], P('rows', None, None, 'ch'), may hold values from -0.125 to 0.125
- w_classes: bfloat16 [256, 21], P('ch'), may hold values from -1 to 1
- b_classes: float32 [21], replicated, may hold values from -3 to 3
- gain_aspp: float32 [5, 256], P(None, 'ch'), may hold values from 0.1 to 1.9
- shift_aspp: float32 [5, 256], P(None, 'ch'), may hold values from -3 to 3
- gain_proj: float32 [256], P('ch'), may hold values from 0.1 to 1.9
- shift_proj: float32 [256], P('ch'), may hold values from -3 to 3
- gain_low: float32 [48], P('ch'), may hold values from 0.1 to 1.9
- shift_low: float32 [48], P('ch'), may hold values from -3 to 3
- gain_dec: float32 [2, 256], P(None, 'ch'), may hold values from 0.1 to 1.9
- shift_dec: float32 [2, 256], P(None, 'ch'), may hold values from -3 to 3
Outputs:
- loss: float32 [], replicated
- grad_features: float32 [256, 64, 2048], P('rows', None, 'ch')
- grad_low_level: float32 [1024, 256, 256], P('rows', 'ch')
- grad_w_one: float32 [2048, 256], P('rows', 'ch')
- grad_w_atrous: float32 [2048, 3, 3, 3, 256], P('rows', None, None, None, 'ch')
- grad_w_pool: float32 [2048, 256], P('rows', 'ch')
- grad_w_proj: float32 [1280, 256], P('rows', 'ch')
- grad_w_low: float32 [256, 48], P('rows', 'ch')
- grad_w_unite_up: float32 [256, 3, 3, 256], P('rows', None, None, 'ch')
- grad_w_unite_low: float32 [48, 3, 3, 256], P(None, None, None, 'ch')
- grad_w_refine: float32 [256, 3, 3, 256], P('rows', None, None, 'ch')
- grad_w_classes: float32 [256, 21], P('ch')
- grad_b_classes: float32 [21], replicated
- grad_gain_aspp: float32 [5, 256], P(None, 'ch')
- grad_shift_aspp: float32 [5, 256], P(None, 'ch')
- grad_gain_proj: float32 [256], P('ch')
- grad_shift_proj: float32 [256], P('ch')
- grad_gain_low: float32 [48], P('ch')
- grad_shift_low: float32 [48], P('ch')
- grad_gain_dec: float32 [2, 256], P(None, 'ch')
- grad_shift_dec: float32 [2, 256], P(None, 'ch')
The draws below stay inside these ranges and needn't reach their ends.
Inputs may be any that keep to these rules, and one draw needn't show every extreme that they name: `crop_rows`: the crops' rows in order along rows; they sum to 256.
All inputs are finite; a program needn't handle non-finite values.
Results may differ from the reference program's by a relative error of at most 0.028.
Values may be sent and summed in bfloat16 or wider, within the bound.
No kernel may reach another device: no remote copies, remote signals or barrier semaphores. Data moves between devices by JAX's collectives and lax.ppermute only.
A program may use at most 256 MiB of HBM per device.

```python
import math
import jax
import jax.numpy as jnp
import numpy as np
from jax import lax

CHANNELS_IN = 2048
BRANCH = 256
LOW_CHANNELS = 256
LOW_OUT = 48
CLASSES = 21
COLUMNS = 64
CROP = 32
RATE_SMALL = 6
RATE_MIDDLE = 12
RATE_LARGE = 18
TOTAL_ROWS = 256
FINE_ROWS = 1024
FINE_COLUMNS = 256
IMAGES = 8


def touch_ends(array, key, least, top_value):
    index_at = [jax.random.randint(jax.random.fold_in(key, axis), (), 0, length) for axis, length in enumerate(array.shape)]
    widest = array.shape.index(max(array.shape))
    next_to = index_at[:widest] + [(index_at[widest] + 1) % array.shape[widest]] + index_at[widest + 1:]
    return array.at[tuple(index_at)].set(least).at[tuple(next_to)].set(top_value)


def levels(stream_key, dims, shards, least, largest):
    level, own = 1.0, jax.random.fold_in(stream_key, 6)
    for position, shards_of in shards:
        steps = jnp.exp(jax.random.uniform(jax.random.fold_in(own, position), (shards_of,), jnp.float32, least / len(shards), largest / len(shards)))
        level = level * jnp.repeat(steps, dims[position] // shards_of).reshape([-1 if axis == position else 1 for axis in range(len(dims))])
    return level


def length_profile(amount, total, bound, slope):
    portions = [(1 << 20) // math.isqrt(rank ** slope) + 1 for rank in range(2, amount + 1)]
    rest, given = total - bound - (amount - 1), [1] * (amount - 1)
    while rest > 0:
        free = [i for i in range(amount - 1) if given[i] < bound]
        pool, budget = sum([portions[i] for i in free]), rest
        for i in free:
            addition = min(bound - given[i], max(1, budget * portions[i] // pool), rest)
            given[i] = given[i] + addition
            rest = rest - addition
    return np.array([bound] + given)


def uneven(key, amount, total, bound, slope):
    if amount == 2:
        one = jax.random.randint(key, (), max(1, total - bound), min(bound, total - 1) + 1)
        return jnp.stack([one, total - one])
    sizes = jnp.asarray(length_profile(amount, total, bound, slope), jnp.int32)
    pairs = (amount - 1) // 2
    source_of, receiver = sizes[1:1 + 2 * pairs:2], sizes[2:2 + 2 * pairs:2]
    room = jnp.minimum(source_of - 1, bound - receiver)
    shifted = jax.random.randint(jax.random.fold_in(key, 1), (pairs,), 0, 1 << 20) % (room + 1)
    sizes = sizes.at[1:1 + 2 * pairs:2].set(source_of - shifted).at[2:2 + 2 * pairs:2].set(receiver + shifted)
    return sizes[jax.random.permutation(jax.random.fold_in(key, 2), amount)]


def bell_draw(key, shape, deviation, bound, cuts=(), kind=jnp.bfloat16):
    drawn = deviation * jax.random.normal(key, shape, jnp.float32)
    if cuts:
        drawn = drawn * levels(key, shape, cuts, -0.22, 0.18)
    return jnp.clip(drawn, -bound, bound).astype(kind)


def setup_inputs(seed: int = 0) -> dict:
    seeds = jax.random.split(jax.random.key(seed), 23)
    features = bell_draw(seeds[0], (TOTAL_ROWS, COLUMNS, CHANNELS_IN), 1.0, 6.0, ((0, 64), (2, 4)))
    low_level = bell_draw(seeds[1], (FINE_ROWS, LOW_CHANNELS, FINE_COLUMNS), 1.0, 6.0, ((0, 64),))
    labels = touch_ends(jax.random.randint(seeds[2], (FINE_ROWS, FINE_COLUMNS), 0, CLASSES), jax.random.fold_in(seeds[2], 1), 0, CLASSES - 1).astype(jnp.int32)
    crop_rows = uneven(seeds[3], IMAGES, TOTAL_ROWS, TOTAL_ROWS - (IMAGES - 1) * CROP // 2, 0).astype(jnp.int32)
    w_one = bell_draw(seeds[4], (CHANNELS_IN, BRANCH), CHANNELS_IN ** -0.5, 0.125, ((0, 64), (1, 4)))
    w_atrous = bell_draw(seeds[5], (CHANNELS_IN, 3, 3, 3, BRANCH), (9 * CHANNELS_IN) ** -0.5, 0.046875, ((0, 64), (4, 4)))
    w_pool = bell_draw(seeds[6], (CHANNELS_IN, BRANCH), CHANNELS_IN ** -0.5, 0.125, ((0, 64), (1, 4)))
    w_proj = bell_draw(seeds[7], (5 * BRANCH, BRANCH), (5 * BRANCH) ** -0.5, 0.15625, ((0, 64), (1, 4)))
    w_low = bell_draw(seeds[8], (LOW_CHANNELS, LOW_OUT), LOW_CHANNELS ** -0.5, 0.375, ((0, 64), (1, 4)))
    w_unite_up = bell_draw(seeds[9], (BRANCH, 3, 3, BRANCH), (9 * (BRANCH + LOW_OUT)) ** -0.5, 0.109375, ((0, 64), (3, 4)))
    w_unite_low = bell_draw(seeds[10], (LOW_OUT, 3, 3, BRANCH), (9 * (BRANCH + LOW_OUT)) ** -0.5, 0.109375, ((3, 4),))
    w_refine = bell_draw(seeds[11], (BRANCH, 3, 3, BRANCH), (9 * BRANCH) ** -0.5, 0.125, ((0, 64), (3, 4)))
    w_classes = bell_draw(seeds[12], (BRANCH, CLASSES), (BRANCH // 8) ** -0.5, 1.0, ((0, 4),))
    b_classes = bell_draw(seeds[13], (CLASSES,), 0.5, 3.0, (), jnp.float32)
    gain_aspp = jnp.clip(1.0 + 0.18 * jax.random.normal(seeds[14], (5, BRANCH), jnp.float32), 0.1, 1.9)
    shift_aspp = bell_draw(seeds[15], (5, BRANCH), 0.5, 3.0, ((1, 4),), jnp.float32)
    gain_proj = jnp.clip(1.0 + 0.18 * jax.random.normal(seeds[16], (BRANCH,), jnp.float32), 0.1, 1.9)
    shift_proj = bell_draw(seeds[17], (BRANCH,), 0.5, 3.0, ((0, 4),), jnp.float32)
    gain_low = jnp.clip(1.0 + 0.18 * jax.random.normal(seeds[18], (LOW_OUT,), jnp.float32), 0.1, 1.9)
    shift_low = bell_draw(seeds[19], (LOW_OUT,), 0.5, 3.0, ((0, 4),), jnp.float32)
    gain_dec = jnp.clip(1.0 + 0.18 * jax.random.normal(seeds[20], (2, BRANCH), jnp.float32), 0.1, 1.9)
    shift_dec = bell_draw(seeds[21], (2, BRANCH), 0.5, 3.0, ((1, 4),), jnp.float32)
    return {"features": features, "low_level": low_level, "labels": labels, "crop_rows": crop_rows, "w_one": w_one, "w_atrous": w_atrous, "w_pool": w_pool, "w_proj": w_proj, "w_low": w_low, "w_unite_up": w_unite_up, "w_unite_low": w_unite_low, "w_refine": w_refine, "w_classes": w_classes, "b_classes": b_classes, "gain_aspp": gain_aspp, "shift_aspp": shift_aspp, "gain_proj": gain_proj, "shift_proj": shift_proj, "gain_low": gain_low, "shift_low": shift_low, "gain_dec": gain_dec, "shift_dec": shift_dec}


PRECISE = lax.Precision.HIGHEST
EPSILON = 1e-05

@jax.custom_vjp
def low(v):
    return lax.optimization_barrier(v.astype(jnp.bfloat16)).astype(jnp.float32)

@jax.custom_vjp
def low_back(v):
    return v

def low_keep(v):
    return (low(v), None)

def low_pass(kept, grad):
    return (grad,)

def back_keep(v):
    return (v, None)

def back_low(kept, grad):
    return (low(grad),)
low.defvjp(low_keep, low_pass)
low_back.defvjp(back_keep, back_low)

def image_of(row_ids, image_ends):
    return lax.optimization_barrier(jnp.sum((row_ids[:, None] >= image_ends[None, :]).astype(jnp.int32), axis=1))

def same_image(row_ids, offset, image_ends, extent):
    neighbour = row_ids + offset
    inside = (row_ids >= 0) & (row_ids < extent) & (neighbour >= 0) & (neighbour < extent)
    return (inside & (image_of(row_ids, image_ends) == image_of(neighbour, image_ends))).astype(jnp.float32)

def blend_shares(fine_ids, image_ends, extent):
    source = fine_ids // 4
    quarter = fine_ids % 4
    weight = jnp.where((quarter == 0) | (quarter == 3), 0.375, 0.125).astype(jnp.float32)
    upper_share = weight * (quarter < 2).astype(jnp.float32) * same_image(source, -1, image_ends, extent)
    lower_share = weight * (quarter >= 2).astype(jnp.float32) * same_image(source, 1, image_ends, extent)
    return (upper_share, lower_share)

def stretch(values, upper_share, lower_share):
    shape = (-1,) + (1,) * (values.ndim - 1)
    own_rows = jnp.repeat(values, 4, axis=0)
    upper_rows = jnp.repeat(jnp.concatenate([values[:1], values[:-1]], axis=0), 4, axis=0)
    lower_rows = jnp.repeat(jnp.concatenate([values[1:], values[-1:]], axis=0), 4, axis=0)
    return (1.0 - upper_share - lower_share).reshape(shape) * own_rows + upper_share.reshape(shape) * upper_rows + lower_share.reshape(shape) * lower_rows

def coarse_mix(product, dilation):
    extent = product.shape[1]
    padded = jnp.pad(product, ((0, 0), (dilation, dilation), (0, 0), (0, 0)))
    return padded[:, 0:extent, 0] + padded[:, dilation:dilation + extent, 1] + padded[:, 2 * dilation:2 * dilation + extent, 2]

def shift_columns(values, step):
    extent = values.shape[-1]
    padded = jnp.pad(values, ((0, 0), (0, 0), (1, 1)))
    return padded[:, :, 1 + step:1 + step + extent]

def coarse_conv(values, weight, dilation, image_ends):
    total_rows = values.shape[0]
    row_ids = jnp.arange(total_rows, dtype=jnp.int32)
    padded = jnp.pad(values, ((dilation, dilation), (0, 0), (0, 0)))
    summed = jnp.zeros(values.shape[:2] + (weight.shape[-1],), jnp.float32)
    for row_tap in range(3):
        offset = (row_tap - 1) * dilation
        window = padded[dilation + offset:dilation + offset + total_rows]
        product = jnp.einsum('rwc,cjo->rwjo', window, weight[:, row_tap], precision=PRECISE)
        keep_rows = same_image(row_ids, offset, image_ends, total_rows)
        summed = summed + keep_rows[:, None, None] * coarse_mix(product, dilation)
    return summed

def fine_conv(values, weight, image_ends):
    total_rows = values.shape[0]
    row_ids = jnp.arange(total_rows, dtype=jnp.int32)
    padded = jnp.pad(values, ((1, 1), (0, 0), (0, 0)))
    summed = jnp.zeros((total_rows, weight.shape[-1], values.shape[2]), jnp.float32)
    for row_tap in range(3):
        window = padded[row_tap:row_tap + total_rows]
        keep_rows = same_image(row_ids, row_tap - 1, image_ends, total_rows)[:, None, None]
        for col_tap in range(3):
            product = jnp.einsum('fcv,co->fov', window, weight[:, row_tap, col_tap], precision=PRECISE)
            summed = summed + keep_rows * shift_columns(product, col_tap - 1)
    return summed

def batch_norm(values, gain, shift, axes):
    average = lax.optimization_barrier(jnp.mean(values, axis=axes, keepdims=True))
    variance = lax.optimization_barrier(jnp.mean(jnp.square(values - average), axis=axes, keepdims=True))
    return jax.nn.silu((values - average) * lax.rsqrt(variance + EPSILON) * gain + shift)

def reference(features, low_level, labels, crop_rows, w_one, w_atrous, w_pool, w_proj, w_low, w_unite_up, w_unite_low, w_refine, w_classes, b_classes, gain_aspp, shift_aspp, gain_proj, shift_proj, gain_low, shift_low, gain_dec, shift_dec):
    image_ends = jnp.cumsum(crop_rows.astype(jnp.int32)).astype(jnp.int32)
    fine_ends = (4 * image_ends).astype(jnp.int32)
    total_rows = features.shape[0]
    fine_total = low_level.shape[0]
    row_ids = jnp.arange(total_rows, dtype=jnp.int32)
    fine_ids = jnp.arange(fine_total, dtype=jnp.int32)
    member = (image_of(row_ids, image_ends)[:, None] == jnp.arange(IMAGES, dtype=jnp.int32)[None, :]).astype(jnp.float32)
    counts_all = crop_rows.astype(jnp.float32) * float(COLUMNS)
    upper_rows, lower_rows = blend_shares(fine_ids, image_ends, total_rows)
    column_ids = jnp.arange(FINE_COLUMNS, dtype=jnp.int32)
    upper_cols, lower_cols = blend_shares(column_ids, jnp.zeros((1,), jnp.int32), COLUMNS)
    one_hot = (labels[:, None, :] == jnp.arange(CLASSES, dtype=jnp.int32)[None, :, None]).astype(jnp.float32)
    dilations = (RATE_SMALL, RATE_MIDDLE, RATE_LARGE)
    coarse_checked = jax.checkpoint(coarse_conv, static_argnums=(2,))
    fine_checked = jax.checkpoint(fine_conv)

    def forward(feats, lowf, one_w, atrous_w, pool_w, proj_w, shrink_w, unite_up_w, unite_low_w, refine_w, classes_w, classes_b, gain_a, shift_a, gain_p, shift_p, gain_l, shift_l, gain_d, shift_d):
        spatial = [low_back(jnp.einsum('rwc,co->rwo', feats, one_w, precision=PRECISE))]
        for branch_index in range(3):
            spatial.append(low_back(coarse_checked(feats, atrous_w[:, branch_index], dilations[branch_index], image_ends)))
        act_spatial = batch_norm(jnp.stack(spatial, axis=2), gain_a[:4], shift_a[:4], (0, 1))
        pooled = jnp.dot(member.T, lax.optimization_barrier(jnp.sum(feats, axis=1)), precision=PRECISE) / counts_all[:, None]
        pool_act = batch_norm(low_back(jnp.dot(low(pooled), pool_w, precision=PRECISE)), gain_a[4], shift_a[4], (0,))
        pool_map = jnp.dot(member, pool_act, precision=PRECISE)
        joined = jnp.concatenate([act_spatial, jnp.broadcast_to(pool_map[:, None, None, :], act_spatial.shape[:2] + (1, pool_map.shape[1]))], axis=2)
        joined = low(joined.reshape(joined.shape[0], joined.shape[1], -1))
        aspp_out = low(batch_norm(low_back(jnp.einsum('rwc,co->rwo', joined, proj_w, precision=PRECISE)), gain_p, shift_p, (0, 1)))
        tall = stretch(aspp_out, upper_rows, lower_rows)
        wide = stretch(jnp.transpose(tall, (1, 0, 2)), upper_cols, lower_cols)
        upsampled = low_back(low(jnp.transpose(wide, (1, 2, 0))))
        low_z = low_back(jnp.einsum('fcv,co->fov', lowf, shrink_w, precision=PRECISE))
        low_act = low(batch_norm(low_z, gain_l[None, :, None], shift_l[None, :, None], (0, 2)))
        united_in = jnp.concatenate([upsampled, low_act], axis=1)
        united_weight = jnp.concatenate([unite_up_w, unite_low_w], axis=0)
        united_z = low_back(fine_checked(united_in, united_weight, fine_ends))
        hidden = low(batch_norm(united_z, gain_d[0][None, :, None], shift_d[0][None, :, None], (0, 2)))
        refine_z = low_back(fine_checked(hidden, refine_w, fine_ends))
        refined = low(batch_norm(refine_z, gain_d[1][None, :, None], shift_d[1][None, :, None], (0, 2)))
        logits = low_back(jnp.einsum('fcv,ck->fkv', refined, classes_w, precision=PRECISE) + classes_b[None, :, None])
        entropy = jax.nn.logsumexp(logits, axis=1) - lax.optimization_barrier(jnp.sum(logits * one_hot, axis=1))
        return jnp.sum(entropy) / IMAGES
    loss_value, pullback = jax.vjp(forward, features.astype(jnp.float32), low_level.astype(jnp.float32), w_one.astype(jnp.float32), w_atrous.astype(jnp.float32), w_pool.astype(jnp.float32), w_proj.astype(jnp.float32), w_low.astype(jnp.float32), w_unite_up.astype(jnp.float32), w_unite_low.astype(jnp.float32), w_refine.astype(jnp.float32), w_classes.astype(jnp.float32), b_classes.astype(jnp.float32), gain_aspp.astype(jnp.float32), shift_aspp.astype(jnp.float32), gain_proj.astype(jnp.float32), shift_proj.astype(jnp.float32), gain_low.astype(jnp.float32), shift_low.astype(jnp.float32), gain_dec.astype(jnp.float32), shift_dec.astype(jnp.float32))
    grad_features, grad_low_level, grad_one, grad_atrous, grad_pool, grad_proj, grad_shrink, grad_unite_up, grad_unite_low, grad_refine, grad_classes, grad_bias, grad_gain_a, grad_shift_a, grad_gain_p, grad_shift_p, grad_gain_l, grad_shift_l, grad_gain_d, grad_shift_d = pullback(jnp.ones((), jnp.float32))
    return (loss_value, grad_features, grad_low_level, grad_one, grad_atrous, grad_pool, grad_proj, grad_shrink, grad_unite_up, grad_unite_low, grad_refine, grad_classes, grad_bias, grad_gain_a, grad_shift_a, grad_gain_p, grad_shift_p, grad_gain_l, grad_shift_l, grad_gain_d, grad_shift_d)
```

```python
import jax
import jax.numpy as jnp
from jax import lax
from jax.sharding import Mesh
from jax.sharding import PartitionSpec as P

DILATIONS = (6, 12, 18)
REACH = 18
EPSILON = 1e-05
PRECISE = lax.Precision.HIGHEST
BF = jnp.bfloat16
F32 = jnp.float32

ROWS = ("z", "x", "core")
ALL = ("z", "x", "core", "y")
STRIP = ("z", "x")
GROUP = ("core", "y")


def hop(block, axes, distance):
    n = lax.axis_size(axes)
    return lax.ppermute(block, axes, [(i, (i + distance) % n) for i in range(n)])


def hop_open(block, axes, distance):
    n = lax.axis_size(axes)
    route = [(i, i + distance) for i in range(n) if 0 <= i + distance < n]
    return lax.ppermute(block, axes, route)


def summed_over(values, groups):
    for axes in groups:
        n = lax.axis_size(axes)
        copies = jnp.broadcast_to(values[None], (n,) + values.shape)
        values = jnp.sum(lax.all_to_all(copies, axes, 0, 0, tiled=True), axis=0)
    return values


def total_of(elements, groups):
    flat = jnp.concatenate([jnp.ravel(e) for e in elements])
    size = flat.shape[0]
    padded = jnp.pad(flat, (0, -size % 128)).reshape(-1, 128)
    out = summed_over(padded, groups).reshape(-1)
    results, at = [], 0
    for e in elements:
        results.append(out[at : at + e.size].reshape(e.shape))
        at += e.size
    return results


def total_all(elements):
    return total_of(elements, (("x", "core", "y"), ("z",)))


def scattered(pieces, axis):
    n = lax.axis_size(axis)
    me = lax.axis_index(axis)
    own = lax.dynamic_index_in_dim(pieces, me, 0, keepdims=False).astype(F32)
    low = pieces.astype(BF)
    for k in range(1, n):
        piece = lax.dynamic_index_in_dim(low, (me + k) % n, 0, keepdims=False)
        own = own + hop(piece, axis, k).astype(F32)
    return own


def gathered(block, axis):
    n = lax.axis_size(axis)
    me = lax.axis_index(axis)
    out = jnp.zeros((n,) + block.shape, block.dtype)
    out = lax.dynamic_update_index_in_dim(out, block, me, 0)
    for k in range(1, n):
        out = lax.dynamic_update_index_in_dim(out, hop(block, axis, k), (me - k) % n, 0)
    return out


def image_of(row_ids, image_ends):
    return jnp.sum((row_ids[:, None] >= image_ends[None, :]).astype(jnp.int32), axis=1)


def same_image(row_ids, offset, image_ends, extent):
    neighbour = row_ids + offset
    inside = (row_ids >= 0) & (row_ids < extent) & (neighbour >= 0) & (neighbour < extent)
    return (inside & (image_of(row_ids, image_ends) == image_of(neighbour, image_ends))).astype(F32)


def blend_matrix(fine_ids, coarse_ids, image_ends, extent):
    source = fine_ids // 4
    quarter = fine_ids % 4
    weight = jnp.where((quarter == 0) | (quarter == 3), 0.375, 0.125).astype(F32)
    upper = weight * (quarter < 2).astype(F32) * same_image(source, -1, image_ends, extent)
    lower = weight * (quarter >= 2).astype(F32) * same_image(source, 1, image_ends, extent)
    target = coarse_ids[None, :]
    centre = source[:, None]
    return (
        (target == centre).astype(F32) * (1.0 - upper - lower)[:, None]
        + (target == centre - 1).astype(F32) * upper[:, None]
        + (target == centre + 1).astype(F32) * lower[:, None]
    )


def shifted(values, step, axis):
    if step == 0:
        return values
    extent = values.shape[axis]
    pads = [(0, 0)] * values.ndim
    pads[axis] = (max(-step, 0), max(step, 0))
    padded = jnp.pad(values, pads)
    start = max(step, 0)
    return lax.slice_in_dim(padded, start, start + extent, axis=axis)


def silu_slope(pre):
    gate = jax.nn.sigmoid(pre)
    return gate * (1.0 + pre * (1.0 - gate))


def moments(sums, squares, count):
    average = sums / count
    return average, lax.rsqrt(squares / count - jnp.square(average) + EPSILON)


def split_two(values):
    high = values.astype(BF)
    return high, (values - high.astype(F32)).astype(BF)


def taps(values, sign):
    return jnp.concatenate([shifted(values, sign * b, 2) for b in (-1, 0, 1)], axis=1)


def dot(spec, a, b):
    return jnp.einsum(spec, a, b, preferred_element_type=F32)


def on_device(
    features,
    low_level,
    labels,
    crop_rows,
    w_one,
    w_atrous,
    w_pool,
    w_proj,
    w_low,
    w_unite_up,
    w_unite_low,
    w_refine,
    w_classes,
    b_classes,
    gain_aspp,
    shift_aspp,
    gain_proj,
    shift_proj,
    gain_low,
    shift_low,
    gain_dec,
    shift_dec,
):
    n_y, n_z, n_x = lax.axis_size("y"), lax.axis_size("z"), lax.axis_size("x")
    core, yi, xi, zi = (lax.axis_index(a) for a in ("core", "y", "x", "z"))
    strip = lax.axis_index(STRIP)
    row = lax.axis_index(ALL)
    groups = lax.axis_size(ROWS)
    rows_in, columns, c_part = features.shape
    total_rows = rows_in * groups
    c_in = c_part * n_y
    fine_strip, c_low, fine_columns = low_level.shape
    fine_total = fine_strip * groups
    branch = w_proj.shape[1] * n_y
    o_part = w_one.shape[1]
    half = o_part // 2
    low_out = w_low.shape[1] * n_y
    classes = w_classes.shape[1]
    images = crop_rows.shape[0]
    pixels = float(total_rows * columns)
    fine_pixels = float(fine_total * fine_columns)
    image_ends = jnp.cumsum(crop_rows)
    fine_ends = 4 * image_ends
    counts = crop_rows.astype(F32) * float(columns)
    tall = 2 * rows_in
    rows8 = strip * tall + jnp.arange(tall, dtype=jnp.int32)

    feats = lax.all_gather(features, GROUP, axis=0, tiled=False)
    feats = feats.reshape(2, n_y, rows_in, columns, c_part).transpose(0, 2, 3, 1, 4)
    feats = feats.reshape(tall * columns, c_in)

    atrous = w_atrous.transpose(0, 1, 3, 2, 4).reshape(w_one.shape[0], 27, o_part)
    own = jnp.concatenate([atrous, w_one[:, None], w_pool[:, None]], axis=1)
    paired = lax.all_to_all(own, "core", 2, 0, tiled=True)
    weights = lax.all_gather(paired.reshape(paired.shape[0], -1), STRIP, axis=0, tiled=True)

    vectors = [gain_dec, shift_dec, gain_proj, shift_proj, gain_low, shift_low]
    flat = jnp.concatenate([jnp.ravel(v) for v in vectors])
    flat = gathered(jnp.pad(flat, (0, -flat.shape[0] % 128)).reshape(-1, 128), "y").reshape(n_y, -1)
    whole, at = [], 0
    for v in vectors:
        piece = flat[:, at : at + v.size].reshape((n_y,) + v.shape)
        whole.append(jnp.moveaxis(piece, 0, -2).reshape(v.shape[:-1] + (-1,)))
        at += v.size
    gain_dec_all, shift_dec_all, gain_p, shift_p, gain_l, shift_l = whole
    gain_a = lax.dynamic_slice_in_dim(gain_aspp, core * half, half, 1)
    shift_a = lax.dynamic_slice_in_dim(shift_aspp, core * half, half, 1)

    def beside(block):
        parts = gathered(block.reshape(-1, 128), "y").reshape((n_y,) + block.shape)
        return jnp.moveaxis(parts, 0, -2).reshape(block.shape[:-1] + (-1,))

    k_row = w_refine.shape[0]
    up_all, refine_all, proj_w, shrink = (
        lax.all_gather(block, ROWS, axis=0, tiled=True)
        for block in (
            beside(w_unite_up).reshape(k_row, -1),
            beside(w_refine).reshape(k_row, -1),
            beside(w_proj),
            lax.all_gather(w_low, "y", axis=1, tiled=True),
        )
    )

    def whole_conv(block):
        return block.reshape(-1, 3, 3, branch).transpose(1, 2, 0, 3)

    up_w = whole_conv(up_all)
    refine_w = whole_conv(refine_all).reshape(3, 3 * branch, branch)
    low_w9 = whole_conv(beside(w_unite_low.reshape(-1, o_part)))
    unite_w = jnp.concatenate([up_w, low_w9], axis=2).reshape(3, -1, branch)
    classes_w = gathered(w_classes, "y").reshape(branch, classes)

    low_own = lax.dynamic_slice_in_dim(low_level, yi * 4, 4, 0)
    labels_own = lax.dynamic_slice_in_dim(labels, yi * 4, 4, 0)
    low_z = dot("fcv,co->fov", low_own, shrink)
    low_above = hop_open(low_z[2:], ALL, 1)
    low_below = hop_open(low_z[:2], ALL, -1)
    low_sums = [jnp.sum(low_z, axis=(0, 2)), jnp.sum(jnp.square(low_z), axis=(0, 2))]

    product = jnp.dot(feats, weights, preferred_element_type=F32).reshape(tall, columns, 29, half)
    centre, minus, plus = [], [], []
    for k, d in enumerate(DILATIONS):
        at = 9 * k
        mixed = (
            product[:, :, at + 3 : at + 6]
            + shifted(product[:, :, at : at + 3], -d, 1)
            + shifted(product[:, :, at + 6 : at + 9], d, 1)
        )
        centre.append(mixed[:, :, 1])
        minus.append(mixed[:, :, 0])
        plus.append(mixed[:, :, 2])
    pool_rows = jnp.sum(product[:, :, 28], axis=1)
    minus = [m.astype(BF) for m in minus]
    plus = [m.astype(BF) for m in plus]

    def packed(parts):
        return jnp.concatenate(parts, axis=0)

    p1 = hop_open(packed([plus[0][0:6], plus[1][4:8]]), STRIP, -1)
    p2 = hop_open(packed([plus[1][0:4], plus[2][2:8]]), STRIP, -2)
    p3 = hop_open(plus[2][0:2], STRIP, -3)
    m1 = hop_open(packed([minus[0][2:8], minus[1][0:4]]), STRIP, 1)
    m2 = hop_open(packed([minus[1][4:8], minus[2][0:6]]), STRIP, 2)
    m3 = hop_open(minus[2][6:8], STRIP, 3)
    from_plus = [
        packed([plus[0][6:8], p1[0:6]]),
        packed([p1[6:10], p2[0:4]]),
        packed([p2[4:10], p3]),
    ]
    from_minus = [
        packed([m1[0:6], minus[0][0:2]]),
        packed([m2[0:4], m1[6:10]]),
        packed([m3, m2[4:10]]),
    ]
    spatial = [product[:, :, 27]]
    for k, d in enumerate(DILATIONS):
        up = same_image(rows8, -d, image_ends, total_rows)[:, None, None]
        down = same_image(rows8, d, image_ends, total_rows)[:, None, None]
        spatial.append(
            centre[k] + up * from_minus[k].astype(F32) + down * from_plus[k].astype(F32)
        )
    spatial = jnp.concatenate(spatial, axis=2)
    member = (
        image_of(rows8, image_ends)[:, None] == jnp.arange(images, dtype=jnp.int32)[None, :]
    ).astype(F32)
    pool_part = jnp.dot(member.T, pool_rows, precision=PRECISE)
    sum_sp, square_sp, pool_sum = total_of(
        [jnp.sum(spatial, axis=(0, 1)), jnp.sum(jnp.square(spatial), axis=(0, 1)), pool_part],
        (STRIP,),
    )
    mean_sp, inverse_sp = moments(sum_sp, square_sp, pixels)
    gain_sp = gain_a[:4].reshape(-1)
    normed_sp = (spatial - mean_sp) * inverse_sp
    pre_sp = normed_sp * gain_sp + shift_a[:4].reshape(-1)
    act_sp = jax.nn.silu(pre_sp).astype(BF)
    pool_z = pool_sum / counts[:, None]
    pool_mean = jnp.mean(pool_z, axis=0, keepdims=True)
    pool_inverse = lax.rsqrt(
        jnp.mean(jnp.square(pool_z - pool_mean), axis=0, keepdims=True) + EPSILON
    )
    pool_normed = (pool_z - pool_mean) * pool_inverse
    pool_pre = pool_normed * gain_a[4] + shift_a[4]
    pool_act = jnp.dot(member, jax.nn.silu(pool_pre), precision=PRECISE).astype(BF)

    lanes = 4 * half
    extra = jnp.pad(pool_act[:, None], ((0, 0), (0, 15), (0, lanes - half)))
    payload = jnp.concatenate([act_sp, extra], axis=1)
    landed = lax.all_to_all(payload, GROUP, 0, 0, tiled=True)
    joined = landed[:, :columns].transpose(1, 0, 2).reshape(columns, -1)
    pool_in = landed[:, columns, :half].reshape(-1)
    main_w = proj_w[: 4 * branch].reshape(4, n_y, 2, half, branch).transpose(2, 1, 0, 3, 4)
    main_w = main_w.reshape(-1, branch)
    pool_w = proj_w[4 * branch :].reshape(n_y, 2, half, branch).transpose(1, 0, 2, 3)
    pool_w = pool_w.reshape(-1, branch)
    proj_z = jnp.dot(joined, main_w, preferred_element_type=F32) + jnp.dot(
        pool_in[None], pool_w, preferred_element_type=F32
    )
    proj_above = hop_open(proj_z, ALL, 1)
    proj_below = hop_open(proj_z, ALL, -1)
    sum_p, square_p, sum_l, square_l = total_all(
        [jnp.sum(proj_z, axis=0), jnp.sum(jnp.square(proj_z), axis=0)] + low_sums
    )
    mean_p, inverse_p = moments(sum_p, square_p, pixels)
    proj_ext = jnp.stack([proj_above, proj_z, proj_below])
    aspp = jax.nn.silu((proj_ext - mean_p) * inverse_p * gain_p + shift_p).astype(BF)

    rows3 = row - 1 + jnp.arange(3, dtype=jnp.int32)
    fine8 = 4 * row - 2 + jnp.arange(8, dtype=jnp.int32)
    row_blend = blend_matrix(fine8, rows3, image_ends, total_rows)
    column_blend = blend_matrix(
        jnp.arange(fine_columns, dtype=jnp.int32),
        jnp.arange(columns, dtype=jnp.int32),
        jnp.zeros((1,), jnp.int32),
        columns,
    ).astype(BF)
    up_rows = sum(
        row_blend[:, k][:, None, None] * aspp[k].astype(F32)[None] for k in range(3)
    )
    up_high, up_low = split_two(up_rows)
    upsampled = (
        dot("fwc,vw->fcv", up_high, column_blend) + dot("fwc,vw->fcv", up_low, column_blend)
    ).astype(BF)
    mean_l, inverse_l = moments(sum_l, square_l, fine_pixels)
    low_ext = jnp.concatenate([low_above, low_z, low_below], axis=0)
    normed_l = (low_ext - mean_l[:, None]) * inverse_l[:, None]
    pre_l = normed_l * gain_l[:, None] + shift_l[:, None]
    low_act = jax.nn.silu(pre_l).astype(BF)
    inside8 = ((fine8 >= 0) & (fine8 < fine_total))[:, None, None]
    united = jnp.where(inside8, jnp.concatenate([upsampled, low_act], axis=1), 0)
    united_t = taps(united, 1)

    fine6 = 4 * row - 1 + jnp.arange(6, dtype=jnp.int32)
    fine4 = 4 * row + jnp.arange(4, dtype=jnp.int32)

    def conv(tapped, weight, ids):
        height = ids.shape[0]
        out = None
        for a in range(3):
            keep = same_image(ids, a - 1, fine_ends, fine_total)[:, None, None]
            part = keep * dot("fkv,ko->fov", tapped[a : a + height], weight[a])
            out = part if out is None else out + part
        return out

    united_z = conv(united_t, unite_w, fine6)
    own_1 = united_z[1:5]
    sum_1, square_1 = total_all([jnp.sum(own_1, axis=(0, 2)), jnp.sum(jnp.square(own_1), axis=(0, 2))])
    mean_1, inverse_1 = moments(sum_1, square_1, fine_pixels)
    normed_1 = (united_z - mean_1[:, None]) * inverse_1[:, None]
    pre_1 = normed_1 * gain_dec_all[0][:, None] + shift_dec_all[0][:, None]
    inside6 = ((fine6 >= 0) & (fine6 < fine_total))[:, None, None]
    hidden = jnp.where(inside6, jax.nn.silu(pre_1).astype(BF), 0)
    hidden_t = taps(hidden, 1)
    refine_z = conv(hidden_t, refine_w, fine4)
    sum_2, square_2 = total_all(
        [jnp.sum(refine_z, axis=(0, 2)), jnp.sum(jnp.square(refine_z), axis=(0, 2))]
    )
    mean_2, inverse_2 = moments(sum_2, square_2, fine_pixels)
    normed_2 = (refine_z - mean_2[:, None]) * inverse_2[:, None]
    pre_2 = normed_2 * gain_dec_all[1][:, None] + shift_dec_all[1][:, None]
    refined = jax.nn.silu(pre_2).astype(BF)

    logits = dot("fcv,ck->fkv", refined, classes_w) + b_classes[None, :, None]
    highest = jnp.max(logits, axis=1, keepdims=True)
    exponent = jnp.exp(logits - highest)
    exp_total = jnp.sum(exponent, axis=1, keepdims=True)
    one_hot = (labels_own[:, None, :] == jnp.arange(classes, dtype=jnp.int32)[None, :, None]).astype(F32)
    entropy = jnp.log(exp_total[:, 0]) + highest[:, 0] - jnp.sum(logits * one_hot, axis=1)
    grad_logits = ((exponent / exp_total - one_hot) / images).astype(BF)
    classes_part = dot("fcv,fkv->ck", refined, grad_logits)
    bias_part = jnp.sum(grad_logits, axis=(0, 2), dtype=F32)
    loss_part = jnp.sum(entropy)
    grad_refined = dot("fkv,ck->fcv", grad_logits, classes_w)

    def back_sums(gp, normed):
        return [jnp.sum(gp * normed, axis=(0, 2)), jnp.sum(gp, axis=(0, 2))]

    def grad_z_of(gp, normed, gain, inverse, grad_gain, grad_shift):
        scale = (gain * inverse)[:, None]
        return (
            scale
            * (gp - (grad_shift[:, None] + normed * grad_gain[:, None]) / fine_pixels)
        ).astype(BF)

    gp_2 = grad_refined * silu_slope(pre_2)
    edge_2 = jnp.stack([gp_2, normed_2], axis=1).astype(BF)
    edge_above = hop_open(edge_2[3:], ALL, 1)
    edge_below = hop_open(edge_2[:1], ALL, -1)
    gain_grad_2, shift_grad_2, grad_bias, loss_sum = total_all(
        back_sums(gp_2, normed_2) + [bias_part, loss_part]
    )
    loss_value = loss_sum / images
    gp_2_ext = jnp.concatenate(
        [edge_above[:, 0].astype(F32), gp_2, edge_below[:, 0].astype(F32)], axis=0
    )
    normed_2_ext = jnp.concatenate(
        [edge_above[:, 1].astype(F32), normed_2, edge_below[:, 1].astype(F32)], axis=0
    )
    grad_refine_z = grad_z_of(
        gp_2_ext, normed_2_ext, gain_dec_all[1], inverse_2, gain_grad_2, shift_grad_2
    )
    grad_refine_z = jnp.where(inside6, grad_refine_z, 0)

    def conv_back(grad_ext, weight, channels):
        grad_t = taps(grad_ext, -1)
        out = None
        for a in range(3):
            start = 2 - a
            keep = same_image(fine4 - (a - 1), a - 1, fine_ends, fine_total)[:, None, None]
            part = keep * dot("fkv,kc->fcv", grad_t[start : start + 4], weight[a])
            out = part if out is None else out + part
        return out

    def turned(weight, channels):
        return weight.reshape(3, 3, channels, branch).transpose(0, 1, 3, 2).reshape(3, -1, channels)

    def conv_weight(tapped, start, grad_own):
        parts = []
        for a in range(3):
            keep = same_image(fine4, a - 1, fine_ends, fine_total)[:, None, None]
            masked = jnp.where(keep > 0, grad_own, jnp.zeros_like(grad_own))
            parts.append(dot("fkv,fov->ko", tapped[start + a : start + a + 4], masked))
        return jnp.stack(parts).reshape(3, 3, -1, n_y, o_part)

    grad_hidden = conv_back(grad_refine_z, turned(refine_w, branch), branch)
    refine_part = conv_weight(hidden_t, 0, grad_refine_z[1:5])

    own_normed_1 = normed_1[1:5]
    gp_1 = grad_hidden * silu_slope(pre_1[1:5])
    edge_1 = gp_1.astype(BF)
    edge_1_above = hop_open(edge_1[3:], ALL, 1)
    edge_1_below = hop_open(edge_1[:1], ALL, -1)
    gain_grad_1, shift_grad_1 = total_all(back_sums(gp_1, own_normed_1))
    gp_1_ext = jnp.concatenate([edge_1_above.astype(F32), gp_1, edge_1_below.astype(F32)], axis=0)
    grad_united_z = grad_z_of(
        gp_1_ext, normed_1, gain_dec_all[0], inverse_1, gain_grad_1, shift_grad_1
    )
    grad_united_z = jnp.where(inside6, grad_united_z, 0)
    grad_united = conv_back(grad_united_z, turned(unite_w, branch + low_out), branch + low_out)
    unite_part = conv_weight(united_t, 1, grad_united_z[1:5])

    grad_up = grad_united[:, :branch].astype(BF)
    grad_cols = dot("fcv,vw->fwc", grad_up, column_blend)
    back_blend = row_blend[2:6]
    to_row = [
        sum(back_blend[f, k] * grad_cols[f] for f in range(4)) for k in range(3)
    ]
    to_above = hop_open(to_row[0], ALL, -1)
    to_below = hop_open(to_row[2], ALL, 1)
    grad_aspp = to_row[1] + to_above + to_below
    normed_p = (proj_z - mean_p) * inverse_p
    pre_p = normed_p * gain_p + shift_p
    gp_p = grad_aspp * silu_slope(pre_p)
    gp_l = grad_united[:, branch:] * silu_slope(pre_l[2:6])
    own_normed_l = normed_l[2:6]
    gain_grad_p, shift_grad_p, gain_grad_l, shift_grad_l = total_all(
        [jnp.sum(gp_p * normed_p, axis=0), jnp.sum(gp_p, axis=0)] + back_sums(gp_l, own_normed_l)
    )
    grad_proj_z = (
        gain_p * inverse_p * (gp_p - (shift_grad_p + normed_p * gain_grad_p) / pixels)
    ).astype(BF)

    grad_sum = jnp.sum(grad_proj_z.astype(F32), axis=0)
    grad_joined = dot("wo,ko->wk", grad_proj_z, main_w)
    grad_joined = grad_joined.reshape(columns, 2 * n_y, lanes).transpose(1, 0, 2).astype(BF)
    pool_high, pool_low = split_two(
        jnp.dot(pool_w.astype(F32), grad_sum, precision=PRECISE).reshape(2 * n_y, half)
    )
    extra = jnp.stack([pool_high, pool_low], axis=1)
    extra = jnp.pad(extra, ((0, 0), (0, 14), (0, lanes - half)))
    back = lax.all_to_all(jnp.concatenate([grad_joined, extra], axis=1), GROUP, 0, 0, tiled=True)
    grad_act = back[:, :columns].astype(F32)
    pool_grad_rows = back[:, columns, :half].astype(F32) + back[:, columns + 1, :half].astype(F32)
    pool_grad_part = jnp.dot(member.T, pool_grad_rows, precision=PRECISE)
    gp_sp = grad_act * silu_slope(pre_sp)
    gain_grad_sp, shift_grad_sp, pool_grad = total_of(
        [jnp.sum(gp_sp * normed_sp, axis=(0, 1)), jnp.sum(gp_sp, axis=(0, 1)), pool_grad_part],
        (STRIP,),
    )
    grad_sp = (
        gain_sp * inverse_sp * (gp_sp - (shift_grad_sp + normed_sp * gain_grad_sp) / pixels)
    ).astype(BF)
    pool_gp = pool_grad * silu_slope(pool_pre)
    pool_gain_grad = jnp.sum(pool_gp * pool_normed, axis=0)
    pool_shift_grad = jnp.sum(pool_gp, axis=0)
    grad_pool_z = (
        gain_a[4]
        * pool_inverse
        * (pool_gp - (pool_shift_grad + pool_normed * pool_gain_grad) / images)
    )

    group_rows = n_x * tall
    wide = gathered(grad_sp, "x").reshape(group_rows, columns, lanes)
    reach_above = hop_open(wide[group_rows - REACH :], "z", 1)
    reach_below = hop_open(wide[:REACH], "z", -1)
    reach = jnp.concatenate([reach_above, wide, reach_below], axis=0)
    ids = zi * group_rows + jnp.arange(group_rows, dtype=jnp.int32)
    spread = []
    for k, d in enumerate(DILATIONS):
        lane = half * (k + 1)
        for b in (-1, 0, 1):
            for a in (-1, 0, 1):
                start = REACH - a * d
                window = reach[start : start + group_rows, :, lane : lane + half]
                keep = same_image(ids - a * d, a * d, image_ends, total_rows)[:, None, None]
                window = jnp.where(keep > 0, window, jnp.zeros_like(window))
                spread.append(shifted(window, -b * d, 1))
    spread.append(wide[:, :, :half])
    member_group = (
        image_of(ids, image_ends)[:, None] == jnp.arange(images, dtype=jnp.int32)[None, :]
    ).astype(F32)
    pool_window = jnp.dot(member_group, grad_pool_z / counts[:, None], precision=PRECISE).astype(BF)
    spread.append(jnp.broadcast_to(pool_window[:, None], (group_rows, columns, half)))
    spread = jnp.concatenate(spread, axis=2)

    own_spread = lax.dynamic_slice_in_dim(spread, xi * tall, tall, 0)
    grad_feats = dot("pk,ck->pc", own_spread.reshape(tall * columns, -1), weights)
    grad_feats = grad_feats.reshape(2, rows_in, columns, c_in)
    grad_feats = scattered(grad_feats, "core")
    grad_feats = jnp.moveaxis(grad_feats.reshape(rows_in, columns, n_y, c_part), 2, 0)
    grad_features = scattered(grad_feats, "y")

    digits = features.reshape(rows_in, columns, c_part // (n_x * o_part), n_x, o_part)
    by_x = lax.all_to_all(jnp.moveaxis(digits, 3, 0), "x", 0, 0, tiled=True)
    feats_x = lax.all_gather(by_x, GROUP, axis=0, tiled=False)
    feats_x = feats_x.reshape((2, n_y, n_x, rows_in, columns) + digits.shape[2:3] + (o_part,))
    feats_x = feats_x.transpose(2, 0, 3, 4, 1, 5, 6).reshape(group_rows * columns, -1)
    aspp_part = dot("pc,pk->ck", feats_x, spread.reshape(group_rows * columns, -1))
    aspp_part = scattered(aspp_part.reshape(n_z, o_part, -1), "z")
    aspp_part = aspp_part.reshape(2, half, 29, half)
    mine = lax.dynamic_index_in_dim(aspp_part, core, 0, keepdims=False)
    theirs = hop(lax.dynamic_index_in_dim(aspp_part, 1 - core, 0, keepdims=False).astype(BF), "core", 1)
    theirs = theirs.astype(F32)
    first = jnp.where(core == 0, mine, theirs)
    second = jnp.where(core == 0, theirs, mine)
    aspp_grad = jnp.concatenate([first, second], axis=2)
    grad_one = aspp_grad[:, 27]
    grad_pool = aspp_grad[:, 28]
    grad_atrous = aspp_grad[:, :27].reshape(-1, 3, 3, 3, o_part).transpose(0, 1, 3, 2, 4)

    grad_low_z = grad_z_of(gp_l, own_normed_l, gain_l, inverse_l, gain_grad_l, shift_grad_l)
    shrink_part = dot("fcv,fov->co", low_own, grad_low_z)
    grad_low_all = gathered(grad_low_z, "y").reshape(fine_strip, low_out, fine_columns)
    shrink_own = lax.dynamic_slice_in_dim(shrink, yi * (c_low // n_y), c_low // n_y, 0)
    grad_low_level = dot("fov,co->fcv", grad_low_all, shrink_own)

    def owned(part):
        return jnp.sum(lax.all_to_all(part.astype(BF), ROWS, 0, 0, tiled=True).astype(F32), axis=0)

    def by_group(part):
        return scattered(jnp.moveaxis(part, -2, 0), "y")

    def conv_pieces(part):
        return by_group(part).transpose(2, 0, 1, 3).reshape(part.shape[2], -1)

    refine_sum = conv_pieces(refine_part)
    unite_sum = conv_pieces(unite_part)
    class_sum = scattered(classes_part.reshape(n_y, -1, classes), "y")
    decoder_sum = owned(
        jnp.concatenate(
            [
                refine_sum.reshape(groups, -1),
                unite_sum[:branch].reshape(groups, -1),
                unite_sum[branch:].reshape(groups, -1),
                class_sum.reshape(groups, -1),
            ],
            axis=1,
        )
    )
    size_9 = k_row * 9 * o_part
    grad_refine = decoder_sum[:size_9].reshape(w_refine.shape)
    grad_unite_up = decoder_sum[size_9 : 2 * size_9].reshape(w_unite_up.shape)
    rest = decoder_sum[2 * size_9 :]
    size_low = low_out * 9 * o_part // groups
    rest = lax.all_to_all(
        jnp.broadcast_to(rest[None], (groups,) + rest.shape), ROWS, 0, 0, tiled=True
    )
    grad_unite_low = rest[:, :size_low].reshape(w_unite_low.shape)
    grad_classes = rest[:, size_low:].reshape(w_classes.shape)
    main_part = dot("wk,wo->ko", joined, grad_proj_z)
    main_part = main_part.reshape(2, n_y, 4, half, branch).transpose(2, 1, 0, 3, 4)
    pool_part_w = (pool_in.astype(F32)[:, None] * grad_sum[None]).reshape(2, n_y, half, branch)
    pool_part_w = pool_part_w.transpose(1, 0, 2, 3)
    proj_part = jnp.concatenate([main_part.reshape(-1, branch), pool_part_w.reshape(-1, branch)])
    proj_sum = by_group(proj_part.reshape(-1, n_y, o_part))
    shrink_sum = by_group(shrink_part.reshape(c_low, n_y, -1))
    late_sum = owned(
        jnp.concatenate([proj_sum.reshape(groups, -1), shrink_sum.reshape(groups, -1)], axis=1)
    )
    size_p = w_proj.size
    grad_proj = late_sum[:size_p].reshape(w_proj.shape)
    grad_shrink = late_sum[size_p:].reshape(w_low.shape)

    both = jnp.stack(
        [
            jnp.concatenate([gain_grad_sp.reshape(4, half), pool_gain_grad[None]]),
            jnp.concatenate([shift_grad_sp.reshape(4, half), pool_shift_grad[None]]),
        ]
    )
    both = gathered(both, "core")
    both = both.transpose(1, 2, 0, 3).reshape(2, 5, o_part)

    def own_channels(vector):
        size = vector.shape[-1] // n_y
        return lax.dynamic_slice_in_dim(vector, yi * size, size, vector.ndim - 1)

    return (
        loss_value,
        grad_features,
        grad_low_level,
        grad_one,
        grad_atrous,
        grad_pool,
        grad_proj,
        grad_shrink,
        grad_unite_up,
        grad_unite_low,
        grad_refine,
        grad_classes,
        grad_bias,
        both[0],
        both[1],
        own_channels(gain_grad_p),
        own_channels(shift_grad_p),
        own_channels(gain_grad_l),
        own_channels(shift_grad_l),
        own_channels(jnp.stack([gain_grad_1, gain_grad_2])),
        own_channels(jnp.stack([shift_grad_1, shift_grad_2])),
    )


def solution(mesh):
    torus = Mesh(mesh.devices.reshape(8, 4, 2, mesh.shape["ch"]), ALL)
    in_specs = (
        P(ROWS, None, "y"),
        P(ROWS, None, None),
        P(ROWS, None),
        P(),
        P(ROWS, "y"),
        P(ROWS, None, None, None, "y"),
        P(ROWS, "y"),
        P(ROWS, "y"),
        P(ROWS, "y"),
        P(ROWS, None, None, "y"),
        P(None, None, None, "y"),
        P(ROWS, None, None, "y"),
        P("y", None),
        P(),
        P(None, "y"),
        P(None, "y"),
        P("y"),
        P("y"),
        P("y"),
        P("y"),
        P(None, "y"),
        P(None, "y"),
    )
    out_specs = (
        P(),
        P(ROWS, None, "y"),
        P(ROWS, "y", None),
        P(ROWS, "y"),
        P(ROWS, None, None, None, "y"),
        P(ROWS, "y"),
        P(ROWS, "y"),
        P(ROWS, "y"),
        P(ROWS, None, None, "y"),
        P(None, None, None, "y"),
        P(ROWS, None, None, "y"),
        P("y", None),
        P(),
        P(None, "y"),
        P(None, "y"),
        P("y"),
        P("y"),
        P("y"),
        P("y"),
        P(None, "y"),
        P(None, "y"),
    )
    return jax.shard_map(
        on_device, mesh=torus, in_specs=in_specs, out_specs=out_specs, check_vma=False
    )
```

```python
import functools

import jax
import jax.numpy as jnp
from jax import lax
from jax.experimental import pallas as pl
from jax.experimental.pallas import tpu as pltpu
from jax.sharding import Mesh
from jax.sharding import PartitionSpec as P

DILATIONS = (6, 12, 18)
REACH = 18
EPSILON = 1e-05
PRECISE = lax.Precision.HIGHEST
BF = jnp.bfloat16
F32 = jnp.float32

ROWS = ("z", "x", "core")
ALL = ("z", "x", "core", "y")
STRIP = ("z", "x")
GROUP = ("core", "y")


def hop(block, axes, distance):
    n = lax.axis_size(axes)
    return lax.ppermute(block, axes, [(i, (i + distance) % n) for i in range(n)])


def hop_open(block, axes, distance):
    n = lax.axis_size(axes)
    route = [(i, i + distance) for i in range(n) if 0 <= i + distance < n]
    return lax.ppermute(block, axes, route)


def summed_over(values, groups):
    for axes in groups:
        n = lax.axis_size(axes)
        copies = jnp.broadcast_to(values[None], (n,) + values.shape)
        values = jnp.sum(lax.all_to_all(copies, axes, 0, 0, tiled=True), axis=0)
    return values


def total_of(elements, groups):
    flat = jnp.concatenate([jnp.ravel(e) for e in elements])
    size = flat.shape[0]
    padded = jnp.pad(flat, (0, -size % 128)).reshape(-1, 128)
    out = summed_over(padded, groups).reshape(-1)
    results, at = [], 0
    for e in elements:
        results.append(out[at : at + e.size].reshape(e.shape))
        at += e.size
    return results


def total_all(elements):
    return total_of(elements, (("x", "core", "y"), ("z",)))


def scattered(pieces, axis):
    n = lax.axis_size(axis)
    me = lax.axis_index(axis)
    own = lax.dynamic_index_in_dim(pieces, me, 0, keepdims=False).astype(F32)
    low = pieces.astype(BF)
    for k in range(1, n):
        piece = lax.dynamic_index_in_dim(low, (me + k) % n, 0, keepdims=False)
        own = own + hop(piece, axis, k).astype(F32)
    return own


def gathered(block, axis):
    n = lax.axis_size(axis)
    me = lax.axis_index(axis)
    out = jnp.zeros((n,) + block.shape, block.dtype)
    out = lax.dynamic_update_index_in_dim(out, block, me, 0)
    for k in range(1, n):
        out = lax.dynamic_update_index_in_dim(out, hop(block, axis, k), (me - k) % n, 0)
    return out


def image_of(row_ids, image_ends):
    return jnp.sum((row_ids[:, None] >= image_ends[None, :]).astype(jnp.int32), axis=1)


def same_image(row_ids, offset, image_ends, extent):
    neighbour = row_ids + offset
    inside = (row_ids >= 0) & (row_ids < extent) & (neighbour >= 0) & (neighbour < extent)
    return (inside & (image_of(row_ids, image_ends) == image_of(neighbour, image_ends))).astype(F32)


def blend_matrix(fine_ids, coarse_ids, image_ends, extent):
    source = fine_ids // 4
    quarter = fine_ids % 4
    weight = jnp.where((quarter == 0) | (quarter == 3), 0.375, 0.125).astype(F32)
    upper = weight * (quarter < 2).astype(F32) * same_image(source, -1, image_ends, extent)
    lower = weight * (quarter >= 2).astype(F32) * same_image(source, 1, image_ends, extent)
    target = coarse_ids[None, :]
    centre = source[:, None]
    return (
        (target == centre).astype(F32) * (1.0 - upper - lower)[:, None]
        + (target == centre - 1).astype(F32) * upper[:, None]
        + (target == centre + 1).astype(F32) * lower[:, None]
    )


def shifted(values, step, axis):
    if step == 0:
        return values
    extent = values.shape[axis]
    pads = [(0, 0)] * values.ndim
    pads[axis] = (max(-step, 0), max(step, 0))
    padded = jnp.pad(values, pads)
    start = max(step, 0)
    return lax.slice_in_dim(padded, start, start + extent, axis=axis)


def silu_slope(pre):
    gate = jax.nn.sigmoid(pre)
    return gate * (1.0 + pre * (1.0 - gate))


def moments(sums, squares, count):
    average = sums / count
    return average, lax.rsqrt(squares / count - jnp.square(average) + EPSILON)


def split_two(values):
    high = values.astype(BF)
    return high, (values - high.astype(F32)).astype(BF)


def taps(values, sign):
    return jnp.concatenate([shifted(values, sign * b, 2) for b in (-1, 0, 1)], axis=1)


def dot(spec, a, b):
    return jnp.einsum(spec, a, b, preferred_element_type=F32)


VMEM = pltpu.VMEM
SMEM = pltpu.SMEM


def mm(a, b):
    return lax.dot_general(a, b, (((1,), (0,)), ((), ())), preferred_element_type=F32)


def mm_nt(a, b):
    return lax.dot_general(a, b, (((1,), (1,)), ((), ())), preferred_element_type=F32)


def mm_tn(a, b):
    return lax.dot_general(a, b, (((0,), (0,)), ((), ())), preferred_element_type=F32)


def run_kernel(body, scalars, arrays, outs, scratch=(), limit=40):
    return pl.pallas_call(
        body,
        out_shape=[jax.ShapeDtypeStruct(shape, kind) for shape, kind in outs],
        in_specs=[pl.BlockSpec(memory_space=SMEM)] * len(scalars)
        + [pl.BlockSpec(memory_space=VMEM)] * len(arrays),
        out_specs=[pl.BlockSpec(memory_space=VMEM)] * len(outs),
        scratch_shapes=[VMEM(shape, kind) for shape, kind in scratch],
        compiler_params=pltpu.CompilerParams(vmem_limit_bytes=limit * 2**20),
    )(*scalars, *arrays)


def tap_rows(values, step):
    if step == 0:
        return values
    extent = values.shape[0]
    ids = lax.broadcasted_iota(jnp.int32, values.shape, 0)
    moved = pltpu.roll(values, (-step) % extent, 0)
    return jnp.where((ids + step >= 0) & (ids + step < extent), moved, 0.0)


def column_sum(values):
    return jnp.sum(values, axis=0, keepdims=True)


def norm_of(total, count):
    mean = total[0:1] / count
    return mean, lax.rsqrt(total[1:2] / count - jnp.square(mean) + EPSILON)


def silu(pre):
    return pre * jax.nn.sigmoid(pre)


def slot_mask(shape, slot):
    lanes = lax.broadcasted_iota(jnp.int32, shape, len(shape) - 1)
    return (lanes >= 32 * slot) & (lanes < 32 * slot + 32)


def lane_roll(values, shift):
    shift = shift % 128
    return values if shift == 0 else pltpu.roll(values, shift, values.ndim - 1)


def product_kernel(
    x_ref, w_ref, pad_ref, a0_ref, a1_ref, a2_ref, p1, p2, p3, m1, m2, m3, acc
):
    rows = x_ref.shape[1]
    depth = x_ref.shape[2]
    n_y = w_ref.shape[0] // depth
    for g in range(9):
        pad_ref[:, 128 * g : 128 * g + 96] = w_ref[:, 96 * g : 96 * g + 96]
        at = {1: 864, 4: 896}.get(g)
        if at is None:
            pad_ref[:, 128 * g + 96 : 128 * g + 128] = jnp.zeros((w_ref.shape[0], 32), BF)
        else:
            pad_ref[:, 128 * g + 96 : 128 * g + 128] = w_ref[:, at : at + 32]
    acc[...] = jnp.zeros_like(acc)

    @pl.loop(0, 2 * n_y)
    def _(i):
        part = pl.ds(pl.multiple_of((i // n_y) * rows, rows), rows)
        deep = pl.ds(pl.multiple_of((i % n_y) * depth, depth), depth)
        acc[part, :] += mm(x_ref[i], pad_ref[deep, :])

    outs = (a0_ref, a1_ref, a2_ref)
    shape = a0_ref.shape
    columns = lax.broadcasted_iota(jnp.int32, shape, 1)
    for k, d in enumerate(DILATIONS):
        left, own, right = (
            acc[:, 128 * (3 * k + j) : 128 * (3 * k + j) + 128].reshape(shape) for j in range(3)
        )
        outs[k][...] = (
            own
            + jnp.where(columns >= d, pltpu.roll(left, d, 1), 0.0)
            + jnp.where(columns < shape[1] - d, pltpu.roll(right, shape[1] - d, 1), 0.0)
        )
    p1[0:6] = a0_ref[0:6].astype(BF)
    p1[6:10] = a1_ref[4:8].astype(BF)
    p2[0:4] = a1_ref[0:4].astype(BF)
    p2[4:10] = a2_ref[2:8].astype(BF)
    p3[...] = a2_ref[0:2].astype(BF)
    m1[0:6] = a0_ref[2:8].astype(BF)
    m1[6:10] = a1_ref[0:4].astype(BF)
    m2[0:4] = a1_ref[4:8].astype(BF)
    m2[4:10] = a2_ref[0:6].astype(BF)
    m3[...] = a2_ref[6:8].astype(BF)


def spatial_kernel(
    up, down, member, a0, a1, a2, p1, p2, p3, m1, m2, m3, out_ref, payload_ref
):
    own = (a0, a1, a2)
    shape = out_ref.shape[1:]
    masks = [slot_mask(shape, slot) for slot in range(4)]

    def plus_of(k, r):
        if k == 0:
            return a0[6 + r] if r < 2 else p1[r - 2].astype(F32)
        if k == 1:
            return p1[6 + r].astype(F32) if r < 4 else p2[r - 4].astype(F32)
        return p2[4 + r].astype(F32) if r < 6 else p3[r - 6].astype(F32)

    def minus_of(k, r):
        if k == 0:
            return m1[r].astype(F32) if r < 6 else a0[r - 6]
        if k == 1:
            return m2[r].astype(F32) if r < 4 else m1[2 + r].astype(F32)
        return m3[r].astype(F32) if r < 2 else m2[2 + r].astype(F32)

    sums = jnp.zeros((1, 128), F32)
    squares = jnp.zeros((1, 128), F32)
    pools = []
    for r in range(out_ref.shape[0]):
        total = jnp.where(masks[0], lane_roll(a0[r], 32), 0.0)
        for k in range(3):
            term = (
                lane_roll(own[k][r], 32 * k)
                + up[k, r] * lane_roll(minus_of(k, r), 32 * (k + 1))
                + down[k, r] * lane_roll(plus_of(k, r), 32 * (k - 1))
            )
            total = jnp.where(masks[k + 1], term, total)
        out_ref[r] = total
        sums = sums + column_sum(total)
        squares = squares + column_sum(total * total)
        pools.append(lane_roll(column_sum(a1[r]), 32))
    first = slot_mask((1, 128), 0)
    packed = [jnp.zeros((1, 128), F32), jnp.zeros((1, 128), F32)]
    for m in range(8):
        part = sum(member[r, m] * pools[r] for r in range(len(pools)))
        packed[m // 4] = packed[m // 4] + lane_roll(jnp.where(first, part, 0.0), 32 * (m % 4))
    payload = jnp.concatenate([sums, squares] + packed, axis=0)
    payload_ref[...] = jnp.broadcast_to(payload[None], payload_ref.shape)


def pool_rows_of(total, slot_rows):
    first = slot_mask((1, 128), 0)
    rows = []
    for m in range(8):
        row = total[slot_rows + m // 4 : slot_rows + m // 4 + 1]
        rows.append(jnp.where(first, lane_roll(row, -32 * (m % 4)), 0.0))
    return rows


def pool_norm(total, counts, gains):
    rows = pool_rows_of(total, 2)
    z = jnp.concatenate([rows[m] / counts[m] for m in range(8)], axis=0)
    mean = jnp.mean(z, axis=0, keepdims=True)
    inverse = lax.rsqrt(jnp.mean(jnp.square(z - mean), axis=0, keepdims=True) + EPSILON)
    normed = (z - mean) * inverse
    return normed, inverse, normed * gains[2:3] + gains[3:4]


def act_kernel(pixels, counts, member, spatial_ref, landed_ref, gains_ref, out_ref):
    total = jnp.sum(landed_ref[...], axis=0)
    gains = gains_ref[...]
    mean, inverse = norm_of(total, pixels)
    _, _, pre = pool_norm(total, counts, gains)
    act = silu(pre)
    columns = spatial_ref.shape[1]
    first_row = lax.broadcasted_iota(jnp.int32, (16, 128), 0) == 0
    for r in range(spatial_ref.shape[0]):
        normed = (spatial_ref[r] - mean) * inverse
        out_ref[r, 0:columns] = silu(normed * gains[0:1] + gains[1:2]).astype(BF)
        row = sum(member[r, m] * act[m : m + 1] for m in range(8))
        row = jnp.where(slot_mask((1, 128), 0), row, 0.0)
        out_ref[r, columns : columns + 16] = jnp.where(first_row, row, 0.0).astype(BF)


def proj_kernel(landed_ref, main_ref, pool_ref, low_ref, out_ref, payload_ref):
    columns = out_ref.shape[0]
    acc = jnp.zeros(out_ref.shape, F32)
    extra = jnp.zeros((16, out_ref.shape[1]), F32)
    for s in range(landed_ref.shape[0]):
        acc = acc + mm(landed_ref[s, 0:columns], main_ref[s])
        extra = extra + mm(landed_ref[s, columns : columns + 16], pool_ref[s])
    z = acc + extra[0:1]
    out_ref[...] = z
    payload = jnp.concatenate([column_sum(z), column_sum(z * z), low_ref[...]], axis=0)
    payload_ref[...] = jnp.broadcast_to(payload[None], payload_ref.shape)


def unite_kernel(
    counts,
    blend,
    keep,
    inside,
    own_ref,
    above_ref,
    below_ref,
    landed_ref,
    gain_ref,
    low_ref,
    low_above_ref,
    low_below_ref,
    low_gain_ref,
    columns_ref,
    up_w_ref,
    low_w_ref,
    z_ref,
    up_ref,
    act_ref,
    payload_ref,
    moments_ref,
    taps_ref,
    low_taps_ref,
    coarse_ref,
    low_all_ref,
):
    total = jnp.sum(landed_ref[...], axis=0)
    mean, inverse = norm_of(total, counts[0])
    mean_l, inverse_l = norm_of(total[2:4, 0:128], counts[1])
    moments_ref[0:1] = mean
    moments_ref[1:2] = inverse
    moments_ref[2:3] = total[2:3] / counts[1]
    moments_ref[3:4] = lax.rsqrt(
        total[3:4] / counts[1] - jnp.square(total[2:3] / counts[1]) + EPSILON
    )
    gain = gain_ref[...]
    low_gain = low_gain_ref[...]
    for k, ref in enumerate((above_ref, own_ref, below_ref)):
        pre = (ref[...] - mean) * inverse * gain[0:1] + gain[1:2]
        coarse_ref[k] = silu(pre).astype(BF).astype(F32)
    low_all_ref[0:2] = low_above_ref[...].astype(F32)
    low_all_ref[2:6] = low_ref[...]
    low_all_ref[6:8] = low_below_ref[...].astype(F32)
    width = z_ref.shape[1]

    @pl.loop(0, 8)
    def _(f):
        row = (
            blend[f, 0] * coarse_ref[0] + blend[f, 1] * coarse_ref[1] + blend[f, 2] * coarse_ref[2]
        )
        high = row.astype(BF)
        rest = (row - high.astype(F32)).astype(BF)
        grown = mm(columns_ref[...], jnp.concatenate([high, rest], axis=0)) * inside[f]
        taps_ref[f] = grown.astype(BF)
        pre = (low_all_ref[f] - mean_l) * inverse_l * low_gain[0:1] + low_gain[1:2]
        act = silu(pre).astype(BF).astype(F32) * inside[f]
        pair = tap_rows(act, -1) + pltpu.roll(act, 64, 1)
        low_taps_ref[f] = jnp.concatenate([pair, tap_rows(act, 1)], axis=1).astype(BF)

        @pl.when((f >= 1) & (f <= 6))
        def _():
            up_ref[f - 1] = grown[width : 2 * width].astype(BF)
            act_ref[f - 1] = act.astype(BF)

    payload_ref[...] = jnp.zeros_like(payload_ref)

    @pl.loop(0, 6)
    def _(f):
        acc = jnp.zeros(z_ref.shape[1:], F32)
        for a in range(3):
            part = mm(low_taps_ref[f + a], low_w_ref[a])
            for b in range(3):
                t = 3 * a + b
                part = part + mm(
                    taps_ref[f + a, b * width : (b + 1) * width, :],
                    up_w_ref[:, 256 * t : 256 * t + 256],
                )
            acc = acc + keep[f, a] * part
        z_ref[f] = acc

        @pl.when((f >= 1) & (f <= 4))
        def _():
            both = jnp.concatenate([column_sum(acc), column_sum(acc * acc)], axis=0)
            payload_ref[...] += jnp.broadcast_to(both[None], payload_ref.shape)


def refine_kernel(
    counts,
    keep,
    inside,
    z_in_ref,
    landed_ref,
    gain_ref,
    w_ref,
    hidden_ref,
    z_ref,
    payload_ref,
    moments_ref,
    taps_ref,
):
    total = jnp.sum(landed_ref[...], axis=0)
    mean, inverse = norm_of(total, counts[1])
    moments_ref[0:1] = mean
    moments_ref[1:2] = inverse
    gain = gain_ref[...]
    width = z_ref.shape[1]

    @pl.loop(0, 6)
    def _(f):
        pre = (z_in_ref[f] - mean) * inverse * gain[0:1] + gain[1:2]
        hidden = silu(pre).astype(BF).astype(F32) * inside[f + 1]
        hidden_ref[f] = hidden.astype(BF)
        for b in range(3):
            taps_ref[f, b * width : (b + 1) * width, :] = tap_rows(hidden, b - 1).astype(BF)

    payload_ref[...] = jnp.zeros_like(payload_ref)

    @pl.loop(0, 4)
    def _(f):
        acc = jnp.zeros(z_ref.shape[1:], F32)
        for a in range(3):
            part = None
            for b in range(3):
                t = 3 * a + b
                term = mm(
                    taps_ref[f + a, b * width : (b + 1) * width, :],
                    w_ref[:, 256 * t : 256 * t + 256],
                )
                part = term if part is None else part + term
            acc = acc + keep[f + 1, a] * part
        z_ref[f] = acc
        both = jnp.concatenate([column_sum(acc), column_sum(acc * acc)], axis=0)
        payload_ref[...] += jnp.broadcast_to(both[None], payload_ref.shape)


def classes_kernel(
    images,
    classes,
    counts,
    z_ref,
    landed_ref,
    gain_ref,
    labels_ref,
    w_ref,
    bias_ref,
    gp_ref,
    payload_ref,
    moments_ref,
    top_ref,
    bottom_ref,
    part_ref,
):
    total = jnp.sum(landed_ref[...], axis=0)
    mean, inverse = norm_of(total, counts[1])
    moments_ref[0:1] = mean
    moments_ref[1:2] = inverse
    gain = gain_ref[...]
    weight = w_ref[...]
    width = z_ref.shape[1]
    shape = (weight.shape[0], width)
    ids = lax.broadcasted_iota(jnp.int32, shape, 0)
    ones = jnp.ones((8, width), BF)
    rows = [jnp.zeros((1, 256), F32) for _ in range(4)]
    part_ref[...] = jnp.zeros_like(part_ref)
    for f in range(4):
        normed = (z_ref[f] - mean) * inverse
        pre = normed * gain[0:1] + gain[1:2]
        gate = jax.nn.sigmoid(pre)
        refined = (pre * gate).astype(BF)
        logits = mm_nt(weight, refined) + bias_ref[:, 0:1]
        valid = ids < classes
        logits = jnp.where(valid, logits, -1e30)
        highest = jnp.max(logits, axis=0, keepdims=True)
        exponent = jnp.exp(logits - highest)
        exp_total = jnp.sum(exponent, axis=0, keepdims=True)
        one_hot = ids == labels_ref[f : f + 1, :]
        picked = jnp.sum(jnp.where(one_hot, logits, 0.0), axis=0, keepdims=True)
        rows[3] = rows[3] + jnp.log(exp_total) + highest - picked
        share = exponent / exp_total - jnp.where(one_hot, 1.0, 0.0)
        grad = jnp.where(valid, share / images, 0.0).astype(BF)
        part_ref[...] += mm(grad, refined)
        counted = mm_nt(ones, grad)[0:1]
        rows[2] = rows[2] + jnp.concatenate(
            [counted, jnp.zeros((1, 256 - shape[0]), F32)], axis=1
        )
        gp = mm_tn(grad, weight) * (gate * (1.0 + pre * (1.0 - gate)))
        gp_ref[f] = gp
        rows[0] = rows[0] + column_sum(gp * normed)
        rows[1] = rows[1] + column_sum(gp)
        if f == 0:
            bottom_ref[0] = gp.astype(BF)
            bottom_ref[1] = normed.astype(BF)
        if f == 3:
            top_ref[0] = gp.astype(BF)
            top_ref[1] = normed.astype(BF)
    payload = jnp.concatenate(rows, axis=0)
    payload_ref[...] = jnp.broadcast_to(payload[None], payload_ref.shape)


def grad_z(gp, normed, scale, total, count):
    return (scale * (gp - (total[1:2] + normed * total[0:1]) / count)).astype(BF)


def store_taps(ref, f, values):
    width = values.shape[0]
    wide = values.astype(F32)
    for b in range(3):
        ref[f, b * width : (b + 1) * width, :] = tap_rows(wide, 1 - b).astype(BF)


def refine_back_kernel(
    counts,
    keep,
    inside,
    gp_ref,
    z_ref,
    above_ref,
    below_ref,
    landed_ref,
    moments_ref,
    gain_ref,
    w_ref,
    z1_ref,
    moments1_ref,
    gain1_ref,
    out_ref,
    taps_ref,
    payload_ref,
    top_ref,
    bottom_ref,
    ends_ref,
):
    total = jnp.sum(landed_ref[...], axis=0)
    mean, inverse = moments_ref[0:1], moments_ref[1:2]
    scale = gain_ref[0:1] * inverse
    count = counts[1]
    for ref, at, f in ((above_ref, 0, 0), (below_ref, 1, 5)):
        edge = grad_z(ref[0].astype(F32), ref[1].astype(F32), scale, total, count)
        store_taps(ends_ref, at, edge.astype(F32) * inside[f + 1])

    @pl.loop(0, 4)
    def _(f):
        normed = (z_ref[f] - mean) * inverse
        store_taps(taps_ref, f, grad_z(gp_ref[f], normed, scale, total, count))

    width = out_ref.shape[1]
    mean1, inverse1 = moments1_ref[0:1], moments1_ref[1:2]
    gain1 = gain1_ref[...]
    payload_ref[...] = jnp.zeros_like(payload_ref)
    for g in range(4):
        acc = jnp.zeros(out_ref.shape[1:], F32)
        for a in range(3):
            source = g + 1 - a
            if source < 0:
                rows = ends_ref.at[0]
            elif source > 3:
                rows = ends_ref.at[1]
            else:
                rows = taps_ref.at[source]
            part = None
            for b in range(3):
                t = 3 * a + b
                term = mm_nt(
                    rows[b * width : (b + 1) * width, :], w_ref[:, 256 * t : 256 * t + 256]
                )
                part = term if part is None else part + term
            acc = acc + keep[g, a] * part
        normed = (z1_ref[g + 1] - mean1) * inverse1
        pre = normed * gain1[0:1] + gain1[1:2]
        gate = jax.nn.sigmoid(pre)
        gp = acc * (gate * (1.0 + pre * (1.0 - gate)))
        out_ref[g] = gp
        both = jnp.concatenate([column_sum(gp * normed), column_sum(gp)], axis=0)
        payload_ref[...] += jnp.broadcast_to(both[None], payload_ref.shape)
        if g == 0:
            bottom_ref[...] = gp.astype(BF)
        if g == 3:
            top_ref[...] = gp.astype(BF)


def unite_back_kernel(
    counts,
    keep,
    inside,
    blend,
    gp_ref,
    z_ref,
    above_ref,
    below_ref,
    landed_ref,
    moments_ref,
    gain_ref,
    up_w_ref,
    low_w_ref,
    columns_ref,
    low_z_ref,
    moments0_ref,
    low_gain_ref,
    taps_ref,
    rows_ref,
    low_gp_ref,
    sums_ref,
    ends_ref,
    flat_ref,
):
    total = jnp.sum(landed_ref[...], axis=0)
    mean, inverse = moments_ref[0:1], moments_ref[1:2]
    scale = gain_ref[0:1] * inverse
    count = counts[1]
    for ref, at, f in ((above_ref, 0, 0), (below_ref, 1, 5)):
        normed = (z_ref[f] - mean) * inverse
        edge = grad_z(ref[...].astype(F32), normed, scale, total, count)
        edge = edge.astype(F32) * inside[f + 1]
        store_taps(ends_ref, at, edge)
        flat_ref[5 * at] = edge.astype(BF)

    @pl.loop(0, 4)
    def _(f):
        normed = (z_ref[f + 1] - mean) * inverse
        edge = grad_z(gp_ref[f], normed, scale, total, count)
        store_taps(taps_ref, f, edge)
        flat_ref[f + 1] = edge

    width = gp_ref.shape[1]
    mean_l, inverse_l = moments0_ref[2:3, 0:128], moments0_ref[3:4, 0:128]
    low_gain = low_gain_ref[...]
    first = lax.broadcasted_iota(jnp.int32, (width, 128), 1) < 64
    rows_ref[...] = jnp.zeros_like(rows_ref)
    sums = [jnp.zeros((1, 128), F32), jnp.zeros((1, 128), F32)]
    for g in range(4):
        acc = jnp.zeros(gp_ref.shape[1:], F32)
        low = jnp.zeros((width, 256), F32)
        for a in range(3):
            source = g + 1 - a
            if source < 0:
                rows = ends_ref.at[0]
            elif source > 3:
                rows = ends_ref.at[1]
            else:
                rows = taps_ref.at[source]
            part = None
            for b in range(3):
                t = 3 * a + b
                term = mm_nt(
                    rows[b * width : (b + 1) * width, :], up_w_ref[:, 256 * t : 256 * t + 256]
                )
                part = term if part is None else part + term
            acc = acc + keep[g, a] * part
            low = low + keep[g, a] * mm_nt(flat_ref[source + 1], low_w_ref[a])
        pair, last = low[:, 0:128], low[:, 128:256]
        low_in = (
            tap_rows(jnp.where(first, pair, 0.0), 1)
            + jnp.where(first, pltpu.roll(pair, 64, 1), 0.0)
            + tap_rows(last, -1)
        )
        grown = mm(columns_ref[...], acc.astype(BF))
        for k in range(3):
            rows_ref[k] += blend[g + 2, k] * grown
        normed = (low_z_ref[g] - mean_l) * inverse_l
        pre = normed * low_gain[0:1] + low_gain[1:2]
        gate = jax.nn.sigmoid(pre)
        gp = low_in * (gate * (1.0 + pre * (1.0 - gate)))
        low_gp_ref[g] = gp
        sums[0] = sums[0] + column_sum(gp * normed)
        sums[1] = sums[1] + column_sum(gp)
    both = jnp.concatenate(sums, axis=0)
    sums_ref[...] = jnp.concatenate([both, jnp.zeros_like(both)], axis=1)


def conv_weight_kernel(keep, h_ref, taps_ref, out_ref):
    width = taps_ref.shape[1] // 3
    channels = out_ref.shape[1]
    low = lax.broadcasted_iota(jnp.int32, (channels, 128), 1) < 64
    grads = []
    for t in range(9):
        a, b = t // 3, t % 3
        acc = jnp.zeros((channels, 256), F32)
        for f in range(4):
            acc = acc + keep[f + 1, a] * mm_tn(
                h_ref[f + a, :, 0:channels] if channels < h_ref.shape[2] else h_ref[f + a],
                taps_ref[f, b * width : (b + 1) * width, :],
            )
        grads.append(acc)
        if t % 2 == 1 or t == 8:
            other = grads[t - 1] if t % 2 == 1 else acc
            mate = acc if t % 2 == 1 else jnp.zeros_like(acc)
            at = 128 * (t // 2)
            for j in range(2):
                x, y = other[:, 128 * j : 128 * j + 128], mate[:, 128 * j : 128 * j + 128]
                out_ref[2 * j, :, at : at + 128] = jnp.where(low, x, pltpu.roll(y, 64, 1)).astype(BF)
                out_ref[2 * j + 1, :, at : at + 128] = jnp.where(
                    low, pltpu.roll(x, 64, 1), y
                ).astype(BF)


def proj_back_sums_kernel(own_ref, above_ref, below_ref, z_ref, moments_ref, gain_ref, low_ref, gp_ref, payload_ref):
    normed = (z_ref[...] - moments_ref[0:1]) * moments_ref[1:2]
    pre = normed * gain_ref[0:1] + gain_ref[1:2]
    gate = jax.nn.sigmoid(pre)
    grad = own_ref[...] + above_ref[...] + below_ref[...]
    gp = grad * (gate * (1.0 + pre * (1.0 - gate)))
    gp_ref[...] = gp
    payload = jnp.concatenate([column_sum(gp * normed), column_sum(gp), low_ref[...]], axis=0)
    payload_ref[...] = jnp.broadcast_to(payload[None], payload_ref.shape)


def proj_back_kernel(
    counts,
    gp_ref,
    z_ref,
    landed_sums_ref,
    moments_ref,
    gain_ref,
    landed_ref,
    main_ref,
    pool_ref,
    out_ref,
    main_grad_ref,
    pool_grad_ref,
    total_ref,
):
    total = jnp.sum(landed_sums_ref[...], axis=0)
    total_ref[...] = total
    mean, inverse = moments_ref[0:1], moments_ref[1:2]
    normed = (z_ref[...] - mean) * inverse
    grad = grad_z(gp_ref[...], normed, gain_ref[0:1] * inverse, total, counts[0])
    columns = grad.shape[0]
    summed = column_sum(grad.astype(F32))
    high = summed.astype(BF).astype(F32)
    first = lax.broadcasted_iota(jnp.int32, (16, 256), 0) == 0
    high_rows = jnp.where(first, high, 0.0).astype(BF)
    low_rows = jnp.where(first, summed - high, 0.0).astype(BF)
    top = lax.broadcasted_iota(jnp.int32, (16, 128), 0)
    for s in range(out_ref.shape[0]):
        out_ref[s, 0:columns] = mm_nt(grad, main_ref[s]).astype(BF)
        pool = mm_nt(high_rows, pool_ref[s]) + mm_nt(low_rows, pool_ref[s])
        pool_high = pool[0:1].astype(BF).astype(F32)
        pair = jnp.where(top == 0, pool_high, jnp.where(top == 1, pool[0:1] - pool_high, 0.0))
        out_ref[s, columns : columns + 16] = pair.astype(BF)
        main_grad_ref[s] = mm_tn(landed_ref[s, 0:columns], grad).astype(BF)
        extra = landed_ref[s, columns : columns + 16]
        outer = mm_tn(extra, high_rows) + mm_tn(extra, low_rows)
        pool_grad_ref[s] = outer[0:32].astype(BF)


def spatial_back_sums_kernel(pixels, member, back_ref, spatial_ref, landed_ref, gains_ref, gp_ref, payload_ref):
    total = jnp.sum(landed_ref[...], axis=0)
    gains = gains_ref[...]
    mean, inverse = norm_of(total, pixels)
    columns = spatial_ref.shape[1]
    rows = [jnp.zeros((1, 128), F32), jnp.zeros((1, 128), F32)]
    pools = []
    for r in range(spatial_ref.shape[0]):
        normed = (spatial_ref[r] - mean) * inverse
        pre = normed * gains[0:1] + gains[1:2]
        gate = jax.nn.sigmoid(pre)
        gp = back_ref[r, 0:columns].astype(F32) * (gate * (1.0 + pre * (1.0 - gate)))
        gp_ref[r] = gp
        rows[0] = rows[0] + column_sum(gp * normed)
        rows[1] = rows[1] + column_sum(gp)
        pools.append(column_sum(back_ref[r, columns : columns + 16].astype(F32)))
    first = slot_mask((1, 128), 0)
    packed = [jnp.zeros((1, 128), F32), jnp.zeros((1, 128), F32)]
    for m in range(8):
        part = sum(member[r, m] * pools[r] for r in range(len(pools)))
        packed[m // 4] = packed[m // 4] + lane_roll(jnp.where(first, part, 0.0), 32 * (m % 4))
    payload = jnp.concatenate(rows + packed, axis=0)
    payload_ref[...] = jnp.broadcast_to(payload[None], payload_ref.shape)


def spatial_back_kernel(
    pixels, counts, gp_ref, spatial_ref, landed_ref, landed_back_ref, gains_ref, out_ref, pool_ref, gains_out_ref
):
    total = jnp.sum(landed_ref[...], axis=0)
    back = jnp.sum(landed_back_ref[...], axis=0)
    gains = gains_ref[...]
    mean, inverse = norm_of(total, pixels)
    scale = gains[0:1] * inverse
    for r in range(spatial_ref.shape[0]):
        normed = (spatial_ref[r] - mean) * inverse
        out_ref[r] = grad_z(gp_ref[r], normed, scale, back, pixels)
    normed, inverse_p, pre = pool_norm(total, counts, gains)
    gate = jax.nn.sigmoid(pre)
    gp = jnp.concatenate(pool_rows_of(back, 2), axis=0) * (gate * (1.0 + pre * (1.0 - gate)))
    gain_grad = column_sum(gp * normed)
    shift_grad = column_sum(gp)
    grad = gains[2:3] * inverse_p * (gp - (shift_grad + normed * gain_grad) / 8.0)
    pool_ref[...] = jnp.concatenate([grad[m : m + 1] / counts[m] for m in range(8)], axis=0)
    gains_out_ref[...] = jnp.concatenate([back[0:2], gain_grad, shift_grad], axis=0)


def aspp_back_kernel(
    place,
    keep,
    wide_ref,
    above_ref,
    below_ref,
    pool_ref,
    w_ref,
    feats_ref,
    grad_ref,
    weight_ref,
    reach_ref,
    spread_ref,
):
    height = wide_ref.shape[0]
    columns = wide_ref.shape[1]
    reach_ref[0:REACH] = above_ref[...]
    reach_ref[REACH : REACH + height] = wide_ref[...]
    reach_ref[REACH + height :] = below_ref[...]
    shape = (columns, 128)
    masks = [slot_mask(shape, slot) for slot in range(4)]
    ids = lax.broadcasted_iota(jnp.int32, shape, 0)

    @pl.loop(0, height)
    def _(r):
        own = reach_ref[REACH + r].astype(F32)
        start = pl.multiple_of(r * columns, columns)
        for k, d in enumerate(DILATIONS):
            mixed = jnp.zeros(shape, F32)
            for a in range(3):
                source = own if a == 1 else reach_ref[REACH + r - (a - 1) * d].astype(F32)
                moved = lane_roll(source, 32 * (a - k - 1)) * keep[3 * k + a, r]
                mixed = jnp.where(masks[a], moved, mixed)
            left = jnp.where(ids < columns - d, pltpu.roll(mixed, columns - d, 0), 0.0)
            right = jnp.where(ids >= d, pltpu.roll(mixed, d, 0), 0.0)
            if k == 0:
                mixed = jnp.where(masks[3], lane_roll(own, 96), mixed)
            if k == 1:
                window = lane_roll(pool_ref[pl.ds(r, 1), :], 96)
                mixed = jnp.where(masks[3], window, mixed)
            for j, value in enumerate((left, mixed, right)):
                at = 128 * (3 * k + j)
                spread_ref[pl.ds(start, columns), at : at + 128] = value.astype(BF)

    n_y = feats_ref.shape[0] // 2
    block = grad_ref.shape[2]
    strip = 2 * block
    base = pl.multiple_of(place[0] * strip, strip)
    depth = grad_ref.shape[3]

    @pl.loop(0, 2 * n_y)
    def _(i):
        part = pl.multiple_of(base + (i // n_y) * block, block)
        deep = pl.multiple_of((i % n_y) * depth, depth)
        grad_ref[i // n_y, i % n_y] = mm_nt(
            spread_ref[pl.ds(part, block), :], w_ref[pl.ds(deep, depth), :]
        ).astype(BF)

    wide = feats_ref.shape[2]

    @pl.loop(0, n_y)
    def _(y):
        acc = jnp.zeros((wide, spread_ref.shape[1]), F32)
        for core in range(2):
            for x in range(spread_ref.shape[0] // strip):
                acc = acc + mm_tn(
                    feats_ref[core * n_y + y, x * block : (x + 1) * block, :],
                    spread_ref[x * strip + core * block : x * strip + (core + 1) * block, :],
                )
        weight_ref[pl.ds(pl.multiple_of(y * wide, wide), wide), :] = acc.astype(BF)


def on_device(
    features,
    low_level,
    labels,
    crop_rows,
    w_one,
    w_atrous,
    w_pool,
    w_proj,
    w_low,
    w_unite_up,
    w_unite_low,
    w_refine,
    w_classes,
    b_classes,
    gain_aspp,
    shift_aspp,
    gain_proj,
    shift_proj,
    gain_low,
    shift_low,
    gain_dec,
    shift_dec,
):
    n_y, n_z, n_x = lax.axis_size("y"), lax.axis_size("z"), lax.axis_size("x")
    core, yi, xi, zi = (lax.axis_index(a) for a in ("core", "y", "x", "z"))
    strip = lax.axis_index(STRIP)
    row = lax.axis_index(ALL)
    groups = lax.axis_size(ROWS)
    rows_in, columns, c_part = features.shape
    total_rows = rows_in * groups
    c_in = c_part * n_y
    fine_strip, c_low, fine_columns = low_level.shape
    fine_total = fine_strip * groups
    branch = w_proj.shape[1] * n_y
    o_part = w_one.shape[1]
    half = o_part // 2
    low_out = w_low.shape[1] * n_y
    classes = w_classes.shape[1]
    images = crop_rows.shape[0]
    pixels = float(total_rows * columns)
    fine_pixels = float(fine_total * fine_columns)
    image_ends = jnp.cumsum(crop_rows)
    fine_ends = 4 * image_ends
    counts = crop_rows.astype(F32) * float(columns)
    tall = 2 * rows_in
    rows8 = strip * tall + jnp.arange(tall, dtype=jnp.int32)

    counts_static = (pixels, fine_pixels)
    rows3 = row - 1 + jnp.arange(3, dtype=jnp.int32)
    fine8 = 4 * row - 2 + jnp.arange(8, dtype=jnp.int32)
    fine6, fine4 = fine8[1:7], fine8[2:6]
    inside = ((fine8 >= 0) & (fine8 < fine_total)).astype(F32)
    keep = jnp.stack([same_image(fine6, a - 1, fine_ends, fine_total) for a in range(3)], axis=1)
    keep_back = jnp.stack(
        [same_image(fine4 - (a - 1), a - 1, fine_ends, fine_total) for a in range(3)], axis=1
    )
    row_blend = blend_matrix(fine8, rows3, image_ends, total_rows)
    column_blend = blend_matrix(
        jnp.arange(fine_columns, dtype=jnp.int32),
        jnp.arange(columns, dtype=jnp.int32),
        jnp.zeros((1,), jnp.int32),
        columns,
    )
    columns_up = jnp.concatenate([shifted(column_blend, b, 0) for b in (-1, 0, 1)], axis=0)
    columns_up = jnp.concatenate([columns_up, columns_up], axis=1).astype(BF)
    columns_back = column_blend.T.astype(BF)
    up = jnp.stack([same_image(rows8, -d, image_ends, total_rows) for d in DILATIONS])
    down = jnp.stack([same_image(rows8, d, image_ends, total_rows) for d in DILATIONS])
    crops = jnp.arange(images, dtype=jnp.int32)
    member = (image_of(rows8, image_ends)[:, None] == crops[None, :]).astype(F32)

    feats = lax.all_gather(features.reshape(-1, c_part), GROUP, axis=0, tiled=False)

    atrous = w_atrous.transpose(0, 1, 3, 2, 4).reshape(w_one.shape[0], 27, o_part)
    own = jnp.concatenate([atrous, w_one[:, None], w_pool[:, None]], axis=1)
    paired = lax.all_to_all(own, "core", 2, 0, tiled=True)
    weights = lax.all_gather(paired.reshape(paired.shape[0], -1), STRIP, axis=0, tiled=True)

    vectors = [gain_dec, shift_dec, gain_proj, shift_proj, gain_low, shift_low]
    flat = jnp.concatenate([jnp.ravel(v) for v in vectors])
    flat = gathered(jnp.pad(flat, (0, -flat.shape[0] % 128)).reshape(-1, 128), "y").reshape(n_y, -1)
    whole, at = [], 0
    for v in vectors:
        piece = flat[:, at : at + v.size].reshape((n_y,) + v.shape)
        whole.append(jnp.moveaxis(piece, 0, -2).reshape(v.shape[:-1] + (-1,)))
        at += v.size
    gain_1, gain_2 = (jnp.stack([whole[0][i], whole[1][i]]) for i in range(2))
    gain_p = jnp.stack([whole[2], whole[3]])
    gain_l = jnp.pad(jnp.stack([whole[4], whole[5]]), ((0, 0), (0, 128 - low_out)))
    halves = jnp.stack([gain_aspp, shift_aspp])
    halves = lax.dynamic_slice_in_dim(halves, core * half, half, 2)
    gains_sp = jnp.concatenate(
        [
            halves[:, :4].reshape(2, -1),
            jnp.pad(halves[:, 4], ((0, 0), (0, 3 * half))),
        ]
    )

    def beside(block):
        parts = gathered(block.reshape(-1, 128), "y").reshape((n_y,) + block.shape)
        return jnp.moveaxis(parts, 0, -2).reshape(block.shape[:-1] + (-1,))

    k_row = w_refine.shape[0]
    shard = jnp.concatenate(
        [
            w_unite_up.reshape(k_row, 9, o_part),
            w_refine.reshape(k_row, 9, o_part),
            w_proj.reshape(k_row, -1, o_part),
            jnp.pad(w_low, ((0, 0), (0, o_part - w_low.shape[1])))[:, None],
        ],
        axis=1,
    )
    shard = jnp.pad(shard, ((0, 0), (0, -shard.shape[1] % 2), (0, 0)))
    dec = lax.all_gather(beside(shard).reshape(k_row, -1), ROWS, axis=0, tiled=True)
    up_w = dec[:, : 9 * branch]
    refine_w = dec[:, 9 * branch : 18 * branch]
    proj_rows = w_proj.shape[0] // k_row
    proj_w = dec[:, 18 * branch : (18 + proj_rows) * branch].reshape(-1, branch)
    shrink = dec[:, (18 + proj_rows) * branch : (19 + proj_rows) * branch]
    shrink = shrink.reshape(c_low, n_y, o_part)[:, :, : w_low.shape[1]].reshape(c_low, low_out)
    shrink = jnp.pad(shrink, ((0, 0), (0, 128 - low_out)))
    low_w9 = beside(w_unite_low.reshape(-1, o_part)).reshape(low_out, 3, 3, branch)
    low_w9 = low_w9.transpose(1, 2, 0, 3)
    low_w = jnp.pad(low_w9, ((0, 0), (0, 0), (0, 64 - low_out), (0, 0)))
    low_w = jnp.pad(low_w.reshape(3, 192, branch), ((0, 0), (0, 64), (0, 0)))
    classes_w = jnp.pad(gathered(w_classes, "y").reshape(branch, classes).T, ((0, 32 - classes), (0, 0)))
    class_bias = jnp.pad(b_classes[:, None], ((0, 32 - classes), (0, 127)))
    main_w = proj_w[: 4 * branch].reshape(4, n_y, 2, half, branch).transpose(2, 1, 0, 3, 4)
    main_w = main_w.reshape(2 * n_y, 4 * half, branch)
    pool_w = proj_w[4 * branch :].reshape(n_y, 2, half, branch).transpose(1, 0, 2, 3)
    pool_w = jnp.pad(pool_w.reshape(2 * n_y, half, branch), ((0, 0), (0, 3 * half), (0, 0)))

    low_own = lax.dynamic_slice_in_dim(low_level, yi * 4, 4, 0)
    labels_own = lax.dynamic_slice_in_dim(labels, yi * 4, 4, 0)
    low_z = dot("fcv,co->fvo", low_own, shrink)
    low_above = hop_open(low_z[2:].astype(BF), ALL, 1)
    low_below = hop_open(low_z[:2].astype(BF), ALL, -1)
    low_sums = jnp.stack([jnp.sum(low_z, axis=(0, 1)), jnp.sum(jnp.square(low_z), axis=(0, 1))])
    low_sums = jnp.pad(low_sums, ((0, 0), (0, branch - 128)))

    digits = features.reshape(rows_in, columns, c_part // (n_x * o_part), n_x, o_part)
    digits = jnp.moveaxis(digits, 3, 0).reshape(n_x, rows_in * columns, -1)
    by_x = lax.all_to_all(digits, "x", 0, 0, tiled=True)
    feats_x = lax.all_gather(by_x.reshape(-1, by_x.shape[2]), GROUP, axis=0, tiled=False)

    wide_c = 4 * half
    edge10, edge2 = ((10, columns, wide_c), BF), ((2, columns, wide_c), BF)
    part = ((tall, columns, wide_c), F32)
    padded_w, a0, a1, a2, p1, p2, p3, m1, m2, m3 = run_kernel(
        product_kernel,
        [],
        [feats, weights],
        [((c_in, 9 * wide_c), BF), part, part, part, edge10, edge10, edge2, edge10, edge10, edge2],
        [((tall * columns, 9 * wide_c), F32)],
    )
    edges = [
        hop_open(p1, STRIP, -1),
        hop_open(p2, STRIP, -2),
        hop_open(p3, STRIP, -3),
        hop_open(m1, STRIP, 1),
        hop_open(m2, STRIP, 2),
        hop_open(m3, STRIP, 3),
    ]
    n_strips = n_z * n_x
    spatial, payload = run_kernel(
        spatial_kernel,
        [up, down, member],
        [a0, a1, a2] + edges,
        [part, ((n_strips, 4, wide_c), F32)],
    )
    landed_sp = lax.all_to_all(payload, STRIP, 0, 0, tiled=True)
    (payload,) = run_kernel(
        functools.partial(act_kernel, pixels),
        [counts, member],
        [spatial, landed_sp, gains_sp],
        [((tall, columns + 16, wide_c), BF)],
    )

    landed = lax.all_to_all(payload, GROUP, 0, 0, tiled=True)
    n_first = 2 * n_x * n_y
    proj_z, payload = run_kernel(
        proj_kernel,
        [],
        [landed, main_w, pool_w, low_sums],
        [((columns, branch), F32), ((n_first, 4, branch), F32)],
    )

    def exchanged(block):
        block = lax.all_to_all(block, ("x", "core", "y"), 0, 0, tiled=True)
        block = jnp.broadcast_to(jnp.sum(block, axis=0)[None], (n_z,) + block.shape[1:])
        return lax.all_to_all(block, "z", 0, 0, tiled=True)

    proj_above = hop_open(proj_z, ALL, 1)
    proj_below = hop_open(proj_z, ALL, -1)
    landed_p = exchanged(payload)

    fine = (fine_columns, branch)
    sums2, sums4 = ((n_first, 2, branch), F32), ((n_first, 4, branch), F32)
    united_z, united_up, low_act, payload, moments_0 = run_kernel(
        functools.partial(unite_kernel, counts_static),
        [row_blend, keep, inside],
        [
            proj_z,
            proj_above,
            proj_below,
            landed_p,
            gain_p,
            low_z,
            low_above,
            low_below,
            gain_l,
            columns_up,
            up_w,
            low_w,
        ],
        [
            ((6,) + fine, F32),
            ((6,) + fine, BF),
            ((6, fine_columns, 128), BF),
            sums2,
            ((4, branch), F32),
        ],
        [
            ((8, 3 * fine_columns, branch), BF),
            ((8, fine_columns, 256), BF),
            ((3, columns, branch), F32),
            ((8, fine_columns, 128), F32),
        ],
    )
    landed_1 = exchanged(payload)
    hidden, refine_z, payload, moments_1 = run_kernel(
        functools.partial(refine_kernel, counts_static),
        [keep, inside],
        [united_z, landed_1, gain_1, refine_w],
        [((6,) + fine, BF), ((4,) + fine, F32), sums2, ((2, branch), F32)],
        [((6, 3 * fine_columns, branch), BF)],
    )
    landed_2 = exchanged(payload)
    edge = ((2,) + fine, BF)
    gp_2, payload, moments_2, top, bottom, classes_part = run_kernel(
        functools.partial(classes_kernel, images, classes, counts_static),
        [],
        [refine_z, landed_2, gain_2, labels_own, classes_w, class_bias],
        [((4,) + fine, F32), sums4, ((2, branch), F32), edge, edge, ((32, branch), F32)],
    )
    edge_above = hop_open(top, ALL, 1)
    edge_below = hop_open(bottom, ALL, -1)
    landed_g2 = exchanged(payload)
    edge = (fine, BF)
    gp_1, taps_2, payload, top, bottom = run_kernel(
        functools.partial(refine_back_kernel, counts_static),
        [keep_back, inside],
        [
            gp_2,
            refine_z,
            edge_above,
            edge_below,
            landed_g2,
            moments_2,
            gain_2,
            refine_w,
            united_z,
            moments_1,
            gain_1,
        ],
        [((4,) + fine, F32), ((4, 3 * fine_columns, branch), BF), sums2, edge, edge],
        [((2, 3 * fine_columns, branch), BF)],
    )
    edge_above = hop_open(top, ALL, 1)
    edge_below = hop_open(bottom, ALL, -1)
    landed_g1 = exchanged(payload)
    grad_lanes = 5 * 2 * o_part
    (refine_part,) = run_kernel(
        conv_weight_kernel, [keep], [hidden, taps_2], [((n_y, branch, grad_lanes), BF)]
    )
    taps_1, to_rows, gp_l, low_back = run_kernel(
        functools.partial(unite_back_kernel, counts_static),
        [keep_back, inside, row_blend],
        [
            gp_1,
            united_z,
            edge_above,
            edge_below,
            landed_g1,
            moments_1,
            gain_1,
            up_w,
            low_w,
            columns_back,
            low_z,
            moments_0,
            gain_l,
        ],
        [
            ((4, 3 * fine_columns, branch), BF),
            ((3, columns, branch), F32),
            ((4, fine_columns, 128), F32),
            ((2, branch), F32),
        ],
        [((2, 3 * fine_columns, branch), BF), ((6,) + fine, BF)],
    )
    (up_part,) = run_kernel(
        conv_weight_kernel, [keep], [united_up, taps_1], [((n_y, branch, grad_lanes), BF)]
    )
    (low_part,) = run_kernel(
        conv_weight_kernel, [keep], [low_act, taps_1], [((n_y, 128, grad_lanes), BF)]
    )

    to_above = hop_open(to_rows[0], ALL, -1)
    to_below = hop_open(to_rows[2], ALL, 1)
    gp_p, payload = run_kernel(
        proj_back_sums_kernel,
        [],
        [to_rows[1], to_above, to_below, proj_z, moments_0, gain_p, low_back],
        [((columns, branch), F32), sums4],
    )
    landed_gp = exchanged(payload)
    payload, main_part, pool_part, total_p = run_kernel(
        functools.partial(proj_back_kernel, counts_static),
        [],
        [gp_p, proj_z, landed_gp, moments_0, gain_p, landed, main_w, pool_w],
        [
            ((2 * n_y, columns + 16, wide_c), BF),
            ((2 * n_y, wide_c, branch), BF),
            ((2 * n_y, half, branch), BF),
            ((4, branch), F32),
        ],
    )
    back = lax.all_to_all(payload, GROUP, 0, 0, tiled=True)
    gp_sp, payload = run_kernel(
        functools.partial(spatial_back_sums_kernel, pixels),
        [member],
        [back, spatial, landed_sp, gains_sp],
        [part, ((n_strips, 4, wide_c), F32)],
    )
    landed_gsp = lax.all_to_all(payload, STRIP, 0, 0, tiled=True)
    grad_sp, pool_grad, gain_grads = run_kernel(
        functools.partial(spatial_back_kernel, pixels),
        [counts],
        [gp_sp, spatial, landed_sp, landed_gsp, gains_sp],
        [((tall, columns, wide_c), BF), ((8, wide_c), F32), ((4, wide_c), F32)],
    )

    group_rows = n_x * tall
    wide = gathered(grad_sp, "x").reshape(group_rows, columns, wide_c)
    reach_above = hop_open(wide[group_rows - REACH :], "z", 1)
    reach_below = hop_open(wide[:REACH], "z", -1)
    ids = zi * group_rows + jnp.arange(group_rows, dtype=jnp.int32)
    keep_group = jnp.stack(
        [
            same_image(ids - (a - 1) * d, (a - 1) * d, image_ends, total_rows)
            for d in DILATIONS
            for a in range(3)
        ]
    )
    member_group = (image_of(ids, image_ends)[:, None] == crops[None, :]).astype(F32)
    pool_window = jnp.dot(member_group, pool_grad, precision=PRECISE)
    grad_feats, aspp_part = run_kernel(
        aspp_back_kernel,
        [xi.astype(jnp.int32)[None], keep_group],
        [wide, reach_above, reach_below, pool_window, padded_w, feats_x],
        [
            ((2, n_y, rows_in * columns, c_part), BF),
            ((c_in // n_x, 9 * wide_c), BF),
        ],
        [
            ((group_rows + 2 * REACH, columns, wide_c), BF),
            ((group_rows * columns, 9 * wide_c), BF),
        ],
        limit=52,
    )

    mine = lax.dynamic_index_in_dim(grad_feats, core, 0, keepdims=False)
    theirs = hop(lax.dynamic_index_in_dim(grad_feats, 1 - core, 0, keepdims=False), "core", 1)
    paired = mine.astype(F32) + theirs.astype(F32)
    grad_features = scattered(paired, "y").reshape(features.shape)

    aspp_sum = lax.all_to_all(aspp_part.reshape(n_z, o_part, -1), "z", 0, 0, tiled=True)
    aspp_sum = jnp.sum(aspp_sum.astype(F32), axis=0).reshape(2, half, -1)
    mine = lax.dynamic_index_in_dim(aspp_sum, core, 0, keepdims=False)
    theirs = hop(lax.dynamic_index_in_dim(aspp_sum, 1 - core, 0, keepdims=False).astype(BF), "core", 1)
    theirs = theirs.astype(F32)
    pair = jnp.stack([jnp.where(core == 0, mine, theirs), jnp.where(core == 0, theirs, mine)], axis=1)
    pair = pair.reshape(half, 2, 3, 3, 4, half)
    grad_atrous = pair[:, :, :, :, :3].transpose(0, 2, 4, 3, 1, 5).reshape(w_atrous.shape)
    grad_one = pair[:, :, 0, 1, 3].reshape(w_one.shape)
    grad_pool = pair[:, :, 1, 1, 3].reshape(w_pool.shape)

    mean_l, inverse_l = moments_0[2, :128], moments_0[3, :128]
    normed_l = (low_z - mean_l) * inverse_l
    grad_low_z = (
        gain_l[0] * inverse_l * (gp_l - (total_p[3, :128] + normed_l * total_p[2, :128]) / fine_pixels)
    ).astype(BF)[:, :, :low_out]
    shrink_part = dot("fcv,fvo->co", low_own, grad_low_z)
    grad_low_all = gathered(grad_low_z.transpose(0, 2, 1), "y").reshape(fine_strip, low_out, fine_columns)
    shrink_own = lax.dynamic_slice_in_dim(shrink, yi * (c_low // n_y), c_low // n_y, 0)
    grad_low_level = dot("fov,co->fcv", grad_low_all, shrink_own[:, :low_out])

    def owned(part):
        return jnp.sum(lax.all_to_all(part.astype(BF), ROWS, 0, 0, tiled=True).astype(F32), axis=0)

    refine_sum = scattered(refine_part, "y")
    up_sum = scattered(up_part, "y")
    low_sum = scattered(low_part[:, :low_out], "y")[:, : 9 * o_part]
    class_sum = scattered(classes_part[:classes].T.reshape(n_y, -1, classes), "y")
    decoder_sum = owned(
        jnp.concatenate(
            [
                refine_sum.reshape(groups, -1),
                up_sum.reshape(groups, -1),
                low_sum.reshape(groups, -1),
                class_sum.reshape(groups, -1),
            ],
            axis=1,
        )
    )
    size_9 = k_row * grad_lanes

    def conv_grad(flat):
        return flat.reshape(k_row, grad_lanes)[:, : 9 * o_part].reshape(w_refine.shape)

    grad_refine = conv_grad(decoder_sum[:size_9])
    grad_unite_up = conv_grad(decoder_sum[size_9 : 2 * size_9])
    rest = decoder_sum[2 * size_9 :]
    size_low = low_out * 9 * o_part // groups
    rest = lax.all_to_all(
        jnp.broadcast_to(rest[None], (groups,) + rest.shape), ROWS, 0, 0, tiled=True
    )
    grad_unite_low = rest[:, :size_low].reshape(w_unite_low.shape)
    grad_classes = rest[:, size_low:].reshape(w_classes.shape)
    main_part = main_part.reshape(2, n_y, 4, half, branch).transpose(2, 1, 0, 3, 4)
    pool_part = pool_part.reshape(2, n_y, half, branch).transpose(1, 0, 2, 3)
    proj_part = jnp.concatenate([main_part.reshape(-1, branch), pool_part.reshape(-1, branch)])
    proj_sum = scattered(jnp.moveaxis(proj_part.reshape(-1, n_y, o_part), 1, 0), "y")
    shrink_sum = scattered(jnp.moveaxis(shrink_part.reshape(c_low, n_y, -1), 1, 0), "y")
    late_sum = owned(
        jnp.concatenate([proj_sum.reshape(groups, -1), shrink_sum.reshape(groups, -1)], axis=1)
    )
    size_p = w_proj.size
    grad_proj = late_sum[:size_p].reshape(w_proj.shape)
    grad_shrink = late_sum[size_p:].reshape(w_low.shape)

    total_2 = jnp.sum(landed_g2, axis=0)
    total_1 = jnp.sum(landed_g1, axis=0)
    grad_bias = total_2[2, :classes]
    loss_value = jnp.sum(total_2[3]) / images
    both = gathered(gain_grads, "core")
    both = both.reshape(2, 2, 2, 4, half)
    both = jnp.concatenate([both[:, 0], both[:, 1, :, :1]], axis=2)
    both = both.transpose(1, 2, 0, 3).reshape(2, 5, o_part)

    def own_channels(vector):
        size = vector.shape[-1] // n_y
        return lax.dynamic_slice_in_dim(vector, yi * size, size, vector.ndim - 1)

    return (
        loss_value,
        grad_features,
        grad_low_level,
        grad_one,
        grad_atrous,
        grad_pool,
        grad_proj,
        grad_shrink,
        grad_unite_up,
        grad_unite_low,
        grad_refine,
        grad_classes,
        grad_bias,
        both[0],
        both[1],
        own_channels(total_p[0]),
        own_channels(total_p[1]),
        own_channels(total_p[2, :low_out]),
        own_channels(total_p[3, :low_out]),
        own_channels(jnp.stack([total_1[0], total_2[0]])),
        own_channels(jnp.stack([total_1[1], total_2[1]])),
    )


def solution(mesh):
    torus = Mesh(mesh.devices.reshape(8, 4, 2, mesh.shape["ch"]), ALL)
    in_specs = (
        P(ROWS, None, "y"),
        P(ROWS, None, None),
        P(ROWS, None),
        P(),
        P(ROWS, "y"),
        P(ROWS, None, None, None, "y"),
        P(ROWS, "y"),
        P(ROWS, "y"),
        P(ROWS, "y"),
        P(ROWS, None, None, "y"),
        P(None, None, None, "y"),
        P(ROWS, None, None, "y"),
        P("y", None),
        P(),
        P(None, "y"),
        P(None, "y"),
        P("y"),
        P("y"),
        P("y"),
        P("y"),
        P(None, "y"),
        P(None, "y"),
    )
    out_specs = (
        P(),
        P(ROWS, None, "y"),
        P(ROWS, "y", None),
        P(ROWS, "y"),
        P(ROWS, None, None, None, "y"),
        P(ROWS, "y"),
        P(ROWS, "y"),
        P(ROWS, "y"),
        P(ROWS, None, None, "y"),
        P(None, None, None, "y"),
        P(ROWS, None, None, "y"),
        P("y", None),
        P(),
        P(None, "y"),
        P(None, "y"),
        P("y"),
        P("y"),
        P("y"),
        P("y"),
        P(None, "y"),
        P(None, "y"),
    )
    return jax.shard_map(
        on_device, mesh=torus, in_specs=in_specs, out_specs=out_specs, check_vma=False
    )
```

```python
import functools

import jax
import jax.numpy as jnp
import numpy as np
from jax import lax
from jax.experimental import pallas as pl
from jax.experimental.pallas import tpu as pltpu
from jax.sharding import Mesh
from jax.sharding import PartitionSpec as P

DILATIONS = (6, 12, 18)
REACH = 18
EPSILON = 1e-05
PRECISE = lax.Precision.HIGHEST
BF = jnp.bfloat16
F32 = jnp.float32

ROWS = ("z", "x", "core")
ALL = ("z", "x", "core", "y")
STRIP = ("z", "x")
GROUP = ("core", "y")


def hop(block, axes, distance):
    n = lax.axis_size(axes)
    return lax.ppermute(block, axes, [(i, (i + distance) % n) for i in range(n)])


def hop_open(block, axes, distance):
    n = lax.axis_size(axes)
    route = [(i, i + distance) for i in range(n) if 0 <= i + distance < n]
    return lax.ppermute(block, axes, route)


def summed_over(values, groups):
    for axes in groups:
        n = lax.axis_size(axes)
        copies = jnp.broadcast_to(values[None], (n,) + values.shape)
        values = jnp.sum(lax.all_to_all(copies, axes, 0, 0, tiled=True), axis=0)
    return values


def total_of(elements, groups):
    flat = jnp.concatenate([jnp.ravel(e) for e in elements])
    size = flat.shape[0]
    padded = jnp.pad(flat, (0, -size % 128)).reshape(-1, 128)
    out = summed_over(padded, groups).reshape(-1)
    results, at = [], 0
    for e in elements:
        results.append(out[at : at + e.size].reshape(e.shape))
        at += e.size
    return results


def total_all(elements):
    return total_of(elements, (("x", "core", "y"), ("z",)))


def scattered(pieces, axis):
    n = lax.axis_size(axis)
    me = lax.axis_index(axis)
    own = lax.dynamic_index_in_dim(pieces, me, 0, keepdims=False).astype(F32)
    low = pieces.astype(BF)
    for k in range(1, n):
        piece = lax.dynamic_index_in_dim(low, (me + k) % n, 0, keepdims=False)
        own = own + hop(piece, axis, k).astype(F32)
    return own


def gathered(block, axis):
    n = lax.axis_size(axis)
    me = lax.axis_index(axis)
    out = jnp.zeros((n,) + block.shape, block.dtype)
    out = lax.dynamic_update_index_in_dim(out, block, me, 0)
    for k in range(1, n):
        out = lax.dynamic_update_index_in_dim(out, hop(block, axis, k), (me - k) % n, 0)
    return out


def image_of(row_ids, image_ends):
    return sum((row_ids >= end).astype(jnp.int32) for end in image_ends)


def same_image(row_ids, offset, image_ends, extent):
    neighbour = row_ids + offset
    inside = (row_ids >= 0) & (row_ids < extent) & (neighbour >= 0) & (neighbour < extent)
    return (inside & (image_of(row_ids, image_ends) == image_of(neighbour, image_ends))).astype(F32)


def blend_matrix(fine_ids, coarse_ids, image_ends, extent):
    source = fine_ids // 4
    quarter = fine_ids % 4
    weight = jnp.where((quarter == 0) | (quarter == 3), 0.375, 0.125).astype(F32)
    upper = weight * (quarter < 2).astype(F32) * same_image(source, -1, image_ends, extent)
    lower = weight * (quarter >= 2).astype(F32) * same_image(source, 1, image_ends, extent)
    target = coarse_ids[None, :]
    centre = source[:, None]
    return (
        (target == centre).astype(F32) * (1.0 - upper - lower)[:, None]
        + (target == centre - 1).astype(F32) * upper[:, None]
        + (target == centre + 1).astype(F32) * lower[:, None]
    )


def shifted(values, step, axis):
    if step == 0:
        return values
    extent = values.shape[axis]
    pads = [(0, 0)] * values.ndim
    pads[axis] = (max(-step, 0), max(step, 0))
    padded = jnp.pad(values, pads)
    start = max(step, 0)
    return lax.slice_in_dim(padded, start, start + extent, axis=axis)


def silu_slope(pre):
    gate = jax.nn.sigmoid(pre)
    return gate * (1.0 + pre * (1.0 - gate))


def moments(sums, squares, count):
    average = sums / count
    return average, lax.rsqrt(squares / count - jnp.square(average) + EPSILON)


def split_two(values):
    high = values.astype(BF)
    return high, (values - high.astype(F32)).astype(BF)


def taps(values, sign):
    return jnp.concatenate([shifted(values, sign * b, 2) for b in (-1, 0, 1)], axis=1)


def dot(spec, a, b):
    return jnp.einsum(spec, a, b, preferred_element_type=F32)


def column_matrices(columns):
    blend = np.zeros((4 * columns, columns), np.float32)
    for v in range(4 * columns):
        source, quarter = divmod(v, 4)
        near = source - 1 if quarter < 2 else source + 1
        share = (0.375 if quarter in (0, 3) else 0.125) if 0 <= near < columns else 0.0
        blend[v, source] += 1.0 - share
        if share:
            blend[v, near] += share
    edge = np.zeros((1, columns), np.float32)
    moved = [np.concatenate([edge, blend[:-1]]), blend, np.concatenate([blend[1:], edge])]
    grown = np.concatenate(moved)
    return jnp.asarray(np.concatenate([grown, grown], axis=1), BF), jnp.asarray(blend.T, BF)


VMEM = pltpu.VMEM
SMEM = pltpu.SMEM


def mm(a, b):
    return lax.dot_general(a, b, (((1,), (0,)), ((), ())), preferred_element_type=F32)


def mm_nt(a, b):
    return lax.dot_general(a, b, (((1,), (1,)), ((), ())), preferred_element_type=F32)


def mm_tn(a, b):
    return lax.dot_general(a, b, (((0,), (0,)), ((), ())), preferred_element_type=F32)


LAYOUT = {}
for _name, _rows, _columns in (
    ("keep", 6, 3),
    ("keep_back", 4, 3),
    ("inside", 1, 8),
    ("blend", 8, 3),
    ("up", 3, 8),
    ("down", 3, 8),
    ("member", 8, 8),
    ("counts", 1, 8),
    ("bias", 1, 32),
    ("group", 9, 32),
):
    LAYOUT[_name] = (sum(r * c for _, r, c in LAYOUT.values()), _rows, _columns)


class Entries:
    def __init__(self, ref, name):
        self.ref = ref
        self.start, _, self.columns = LAYOUT[name]

    def __getitem__(self, index):
        if isinstance(index, tuple):
            return self.ref[self.start + index[0] * self.columns + index[1]]
        return self.ref[self.start + index]


def whole_block(shape):
    return pl.BlockSpec(shape, lambda i: (0,) * len(shape), pipeline_mode=pl.Buffered(1))


class Lanes:
    def __init__(self, array, width, index):
        self.array, self.shape, self.index = array, (array.shape[0], width), index

    def spec(self):
        return pl.BlockSpec(self.shape, lambda i: (0, self.index), pipeline_mode=pl.Buffered(1))


def run_kernel(body, scalars, arrays, outs, scratch=(), limit=56):
    specs = [a.spec() if isinstance(a, Lanes) else whole_block(a.shape) for a in arrays]
    arrays = [a.array if isinstance(a, Lanes) else a for a in arrays]
    return pl.pallas_call(
        body,
        grid=(1,),
        out_shape=[jax.ShapeDtypeStruct(shape, kind) for shape, kind in outs],
        in_specs=[pl.BlockSpec(memory_space=SMEM)] * len(scalars)
        + specs,
        out_specs=[whole_block(shape) for shape, _ in outs],
        scratch_shapes=[VMEM(shape, kind) for shape, kind in scratch],
        compiler_params=pltpu.CompilerParams(vmem_limit_bytes=limit * 2**20),
    )(*scalars, *arrays)


def tap_rows(values, step):
    if step == 0:
        return values
    extent = values.shape[0]
    ids = lax.broadcasted_iota(jnp.int32, values.shape, 0)
    moved = pltpu.roll(values, (-step) % extent, 0)
    return jnp.where((ids + step >= 0) & (ids + step < extent), moved, 0.0)


def column_sum(values):
    return jnp.sum(values, axis=0, keepdims=True)


def norm_of(total, count):
    mean = total[0:1] / count
    return mean, lax.rsqrt(total[1:2] / count - jnp.square(mean) + EPSILON)


def silu(pre):
    return pre * jax.nn.sigmoid(pre)


def slot_mask(shape, slot):
    lanes = lax.broadcasted_iota(jnp.int32, shape, len(shape) - 1)
    return (lanes >= 32 * slot) & (lanes < 32 * slot + 32)


def lane_roll(values, shift):
    shift = shift % 128
    return values if shift == 0 else pltpu.roll(values, shift, values.ndim - 1)


def product_kernel(
    place, mine_ref, theirs_ref, w_ref, pad_ref, a0_ref, a1_ref, a2_ref, p1, p2, p3, m1, m2, m3, acc
):
    n_y, rows, depth = mine_ref.shape
    block, n_x = 64, 4

    @pl.loop(0, w_ref.shape[0] // (block * n_x))
    def _(z):
        for hops in range(n_x):
            owner = lax.rem(place[0] - hops + n_x, n_x)
            source = pl.ds(pl.multiple_of((z * n_x + hops) * block, block), block)
            target = pl.ds(pl.multiple_of((z * n_x + owner) * block, block), block)
            for g in range(9):
                pad_ref[target, 128 * g : 128 * g + 96] = w_ref[source, 96 * g : 96 * g + 96]
                at = {1: 864, 4: 896}.get(g)
                if at is None:
                    pad_ref[target, 128 * g + 96 : 128 * g + 128] = jnp.zeros((block, 32), BF)
                else:
                    pad_ref[target, 128 * g + 96 : 128 * g + 128] = w_ref[source, at : at + 32]

    acc[...] = jnp.zeros_like(acc)

    @pl.loop(0, n_y)
    def _(i):
        owner = lax.rem(place[1] - i + n_y, n_y)
        deep = pl.ds(pl.multiple_of(owner * depth, depth), depth)
        own_rows = pl.ds(pl.multiple_of(place[2] * rows, rows), rows)
        other_rows = pl.ds(pl.multiple_of((1 - place[2]) * rows, rows), rows)
        acc[own_rows, :] += mm(mine_ref[i], pad_ref[deep, :])
        acc[other_rows, :] += mm(theirs_ref[i], pad_ref[deep, :])

    outs = (a0_ref, a1_ref, a2_ref)
    shape = a0_ref.shape
    columns = lax.broadcasted_iota(jnp.int32, shape, 1)
    for k, d in enumerate(DILATIONS):
        left, own, right = (
            acc[:, 128 * (3 * k + j) : 128 * (3 * k + j) + 128].reshape(shape) for j in range(3)
        )
        outs[k][...] = (
            own
            + jnp.where(columns >= d, pltpu.roll(left, d, 1), 0.0)
            + jnp.where(columns < shape[1] - d, pltpu.roll(right, shape[1] - d, 1), 0.0)
        )
    masks = [slot_mask(shape[1:], slot) for slot in range(4)]

    def pack(ref, pieces, lane):
        for block in range(ref.shape[0]):
            value = jnp.zeros(shape[1:], F32)
            for slot, (source, r) in enumerate(pieces[4 * block : 4 * block + 4]):
                value = jnp.where(masks[slot], lane_roll(source[r], 32 * (slot - lane)), value)
            ref[block] = value.astype(BF)

    pack(p1, [(a0_ref, r) for r in range(6)] + [(a1_ref, r) for r in range(4, 8)], 2)
    pack(p2, [(a1_ref, r) for r in range(4)] + [(a2_ref, r) for r in range(2, 8)], 2)
    pack(p3, [(a2_ref, r) for r in range(2)], 2)
    pack(m1, [(a0_ref, r) for r in range(2, 8)] + [(a1_ref, r) for r in range(4)], 0)
    pack(m2, [(a1_ref, r) for r in range(4, 8)] + [(a2_ref, r) for r in range(6)], 0)
    pack(m3, [(a2_ref, r) for r in range(6, 8)], 0)


def spatial_kernel(
    table, a0, a1, a2, p1, p2, p3, m1, m2, m3, out_ref, payload_ref
):
    up, down, member = (Entries(table, name) for name in ("up", "down", "member"))
    own = (a0, a1, a2)
    shape = out_ref.shape[1:]
    masks = [slot_mask(shape, slot) for slot in range(4)]

    def piece(ref, i, k):
        return lane_roll(ref[i // 4].astype(F32), 32 * (k + 1 - i % 4))

    def plus_of(k, r):
        if k == 0:
            return lane_roll(a0[6 + r], -32) if r < 2 else piece(p1, r - 2, k)
        if k == 1:
            return piece(p1, 6 + r, k) if r < 4 else piece(p2, r - 4, k)
        return piece(p2, 4 + r, k) if r < 6 else piece(p3, r - 6, k)

    def minus_of(k, r):
        if k == 0:
            return piece(m1, r, k) if r < 6 else lane_roll(a0[r - 6], 32)
        if k == 1:
            return piece(m2, r, k) if r < 4 else piece(m1, 2 + r, k)
        return piece(m3, r, k) if r < 2 else piece(m2, 2 + r, k)

    sums = jnp.zeros((1, 128), F32)
    squares = jnp.zeros((1, 128), F32)
    pools = []
    for r in range(out_ref.shape[0]):
        total = jnp.where(masks[0], lane_roll(a0[r], 32), 0.0)
        for k in range(3):
            term = (
                lane_roll(own[k][r], 32 * k)
                + up[k, r] * minus_of(k, r)
                + down[k, r] * plus_of(k, r)
            )
            total = jnp.where(masks[k + 1], term, total)
        out_ref[r] = total
        sums = sums + column_sum(total)
        squares = squares + column_sum(total * total)
        pools.append(lane_roll(column_sum(a1[r]), 32))
    first = slot_mask((1, 128), 0)
    packed = [jnp.zeros((1, 128), F32), jnp.zeros((1, 128), F32)]
    for m in range(8):
        part = sum(member[r, m] * pools[r] for r in range(len(pools)))
        packed[m // 4] = packed[m // 4] + lane_roll(jnp.where(first, part, 0.0), 32 * (m % 4))
    payload = jnp.concatenate([sums, squares] + packed, axis=0)
    payload_ref[...] = jnp.broadcast_to(payload[None], payload_ref.shape)


def pool_rows_of(total, slot_rows):
    first = slot_mask((1, 128), 0)
    rows = []
    for m in range(8):
        row = total[slot_rows + m // 4 : slot_rows + m // 4 + 1]
        rows.append(jnp.where(first, lane_roll(row, -32 * (m % 4)), 0.0))
    return rows


def pool_norm(total, counts, gains):
    rows = pool_rows_of(total, 2)
    z = jnp.concatenate([rows[m] / counts[m] for m in range(8)], axis=0)
    mean = jnp.mean(z, axis=0, keepdims=True)
    inverse = lax.rsqrt(jnp.mean(jnp.square(z - mean), axis=0, keepdims=True) + EPSILON)
    normed = (z - mean) * inverse
    return normed, inverse, normed * gains[2:3] + gains[3:4]


def act_kernel(pixels, table, spatial_ref, landed_ref, gains_ref, out_ref):
    counts, member = Entries(table, "counts"), Entries(table, "member")
    total = jnp.sum(landed_ref[...], axis=0)
    gains = gains_ref[...]
    mean, inverse = norm_of(total, pixels)
    _, _, pre = pool_norm(total, counts, gains)
    act = silu(pre)
    columns = spatial_ref.shape[1]
    first_row = lax.broadcasted_iota(jnp.int32, (16, 128), 0) == 0
    for r in range(spatial_ref.shape[0]):
        normed = (spatial_ref[r] - mean) * inverse
        out_ref[r, 0:columns] = silu(normed * gains[0:1] + gains[1:2]).astype(BF)
        row = sum(member[r, m] * act[m : m + 1] for m in range(8))
        row = jnp.where(slot_mask((1, 128), 0), row, 0.0)
        out_ref[r, columns : columns + 16] = jnp.where(first_row, row, 0.0).astype(BF)


def proj_kernel(landed_ref, main_ref, pool_ref, low_ref, out_ref, payload_ref):
    columns = out_ref.shape[0]
    acc = jnp.zeros(out_ref.shape, F32)
    extra = jnp.zeros((16, out_ref.shape[1]), F32)
    for s in range(landed_ref.shape[0]):
        acc = acc + mm(landed_ref[s, 0:columns], main_ref[s])
        extra = extra + mm(landed_ref[s, columns : columns + 16], pool_ref[s])
    z = acc + extra[0:1]
    out_ref[...] = z
    payload = jnp.concatenate([column_sum(z), column_sum(z * z), low_ref[...]], axis=0)
    payload_ref[...] = jnp.broadcast_to(payload[None], payload_ref.shape)


def sum_kernel(landed_ref, out_ref):
    total = jnp.sum(landed_ref[...], axis=0)
    out_ref[...] = jnp.broadcast_to(total[None], out_ref.shape)


def half_lanes(value, index):
    return lane_roll(value, -64 * index)[:, 0:64]


def pieces_kernel(landed_ref, refine_ref, unite_ref, proj_ref, shrink_ref, rest_ref):
    total = landed_ref[0].astype(F32)
    for i in range(1, landed_ref.shape[0]):
        total = total + landed_ref[i].astype(F32)
    for ref, start in ((refine_ref, 0), (unite_ref, 20)):
        for t in range(9):
            for c in range(4):
                row = start + 5 * c + t // 2
                ref[t, c : c + 1] = half_lanes(total[row : row + 1], t % 2)
    rest_ref[...] = total[40:45].astype(BF)
    for i in range(proj_ref.shape[0]):
        row = 45 + i // 2
        proj_ref[i : i + 1] = half_lanes(total[row : row + 1], i % 2)
    shrink_ref[...] = total[55:56]


def landed_kernel(place, landed_ref, mine_ref, theirs_ref, low_ref, classes_ref):
    block = landed_ref.shape[1] - 8
    total = landed_ref[0, 0:block].astype(F32)
    for z in range(1, landed_ref.shape[0]):
        total = total + landed_ref[z, 0:block].astype(F32)
    first, second = total[0 : block // 2], total[block // 2 :]
    zero = place[2] == 0
    mine_ref[...] = jnp.where(zero, first, second)
    theirs_ref[...] = jnp.where(zero, second, first).astype(BF)
    rows = low_ref.shape[1] // 8
    for t in range(9):
        at = 128 * (t // 2)
        for z in range(rows):
            part = landed_ref[z, block : block + 8, at : at + 128].astype(F32)
            low_ref[t, 8 * z : 8 * z + 8] = half_lanes(part, t % 2)
    tail = landed_ref[rows, block : block + 8, 0:640].astype(F32)
    for i in range(classes_ref.shape[0]):
        at = 128 * (i % 10 // 2)
        part = tail[i // 10 : i // 10 + 1, at : at + 128]
        classes_ref[i : i + 1] = half_lanes(part, i % 2)


def joined_kernel(place, mine_ref, theirs_ref, atrous_ref, one_ref, pool_ref):
    zero = place[2] == 0
    lanes = lax.broadcasted_iota(jnp.int32, (mine_ref.shape[0], 128), 1)
    for g in range(9):
        mine = mine_ref[:, 128 * g : 128 * g + 128]
        theirs = theirs_ref[:, 128 * g : 128 * g + 128].astype(F32)
        first, second = jnp.where(zero, mine, theirs), jnp.where(zero, theirs, mine)
        for a in range(4):
            pair = jnp.where(lanes < 32, lane_roll(first, -32 * a), lane_roll(second, 32 - 32 * a))
            if a < 3:
                atrous_ref[g // 3, a, g % 3] = pair[:, 0:64]
            elif g == 1:
                one_ref[...] = pair[:, 0:64]
            elif g == 4:
                pool_ref[...] = pair[:, 0:64]


def low_weight_kernel(raw_ref, out_ref):
    out_ref[...] = jnp.zeros_like(out_ref)
    rows = raw_ref.shape[2]
    first = lax.broadcasted_iota(jnp.int32, (rows, 128), 1) < 64
    for t in range(9):
        a, b = t // 3, t % 3
        for j in range(2):
            left = raw_ref[2 * j, t // 2].astype(F32)
            right = raw_ref[2 * j + 1, t // 2].astype(F32)
            if t % 2 == 0:
                right = pltpu.roll(right, 64, 1)
            else:
                left = pltpu.roll(left, 64, 1)
            value = jnp.where(first, left, right).astype(BF)
            out_ref[a, 64 * b : 64 * b + rows, 128 * j : 128 * j + 128] = value


def shared_weight_kernel(low_part, dec_ref, main_ref, pool_ref, shrink_ref, rows_ref):
    height = dec_ref.shape[0]
    n_s = main_ref.shape[0]
    for q in range(5):
        for j in range(2):
            at = 256 * q + 128 * j
            rows_ref[j, pl.ds(q, height, stride=5), :] = dec_ref[:, at : at + 128].astype(F32)
    for s in range(n_s):
        place = 64 * (s % (n_s // 2)) + 32 * (s // (n_s // 2))
        for branch in range(4):
            at = 256 * branch + place
            for j in range(2):
                main_ref[s, 32 * branch : 32 * branch + 32, 128 * j : 128 * j + 128] = rows_ref[
                    j, at : at + 32
                ].astype(BF)
        at = 1024 + place
        for j in range(2):
            pool_ref[s, 0:32, 128 * j : 128 * j + 128] = rows_ref[j, at : at + 32].astype(BF)
        pool_ref[s, 32:128] = jnp.zeros((96, 256), BF)
    lanes = lax.broadcasted_iota(jnp.int32, (height, 128), 1)
    value = jnp.zeros((height, 128), F32)
    for y in range(4):
        at = 256 * 5 + 128 * (y // 2)
        moved = lane_roll(dec_ref[:, at : at + 128].astype(F32), low_part * y - 64 * (y % 2))
        value = jnp.where((lanes >= low_part * y) & (lanes < low_part * (y + 1)), moved, value)
    shrink_ref[...] = value.astype(BF)


def unite_kernel(
    counts,
    table,
    own_ref,
    above_ref,
    below_ref,
    landed_ref,
    gain_ref,
    low_all_ref,
    low_gain_ref,
    columns_ref,
    up_w_ref,
    low_w_ref,
    z_ref,
    up_ref,
    act_ref,
    payload_ref,
    moments_ref,
    taps_ref,
    low_taps_ref,
    coarse_ref,
):
    blend, keep, inside = (Entries(table, name) for name in ("blend", "keep", "inside"))
    total = jnp.sum(landed_ref[...], axis=0)
    mean, inverse = norm_of(total, counts[0])
    mean_l, inverse_l = norm_of(total[2:4, 0:128], counts[1])
    moments_ref[0:1] = mean
    moments_ref[1:2] = inverse
    moments_ref[2:3] = total[2:3] / counts[1]
    moments_ref[3:4] = lax.rsqrt(
        total[3:4] / counts[1] - jnp.square(total[2:3] / counts[1]) + EPSILON
    )
    gain = gain_ref[...]
    low_gain = low_gain_ref[...]
    for k, ref in enumerate((above_ref, own_ref, below_ref)):
        pre = (ref[...] - mean) * inverse * gain[0:1] + gain[1:2]
        coarse_ref[k] = silu(pre).astype(BF).astype(F32)
    width = z_ref.shape[1]

    @pl.loop(0, 8)
    def _(f):
        row = (
            blend[f, 0] * coarse_ref[0] + blend[f, 1] * coarse_ref[1] + blend[f, 2] * coarse_ref[2]
        )
        high = row.astype(BF)
        rest = (row - high.astype(F32)).astype(BF)
        grown = mm(columns_ref[...], jnp.concatenate([high, rest], axis=0)) * inside[f]
        taps_ref[f] = grown.astype(BF)
        pre = (low_all_ref[f] - mean_l) * inverse_l * low_gain[0:1] + low_gain[1:2]
        act = silu(pre).astype(BF).astype(F32) * inside[f]
        pair = tap_rows(act, -1) + pltpu.roll(act, 64, 1)
        low_taps_ref[f] = jnp.concatenate([pair, tap_rows(act, 1)], axis=1).astype(BF)

        @pl.when((f >= 1) & (f <= 6))
        def _():
            up_ref[f - 1] = grown[width : 2 * width].astype(BF)
            act_ref[f - 1] = act.astype(BF)

    payload_ref[...] = jnp.zeros_like(payload_ref)

    @pl.loop(0, 6)
    def _(f):
        acc = jnp.zeros(z_ref.shape[1:], F32)
        for a in range(3):
            part = mm(low_taps_ref[f + a], low_w_ref[a])
            for b in range(3):
                t = 3 * a + b
                part = part + mm(
                    taps_ref[f + a, b * width : (b + 1) * width, :],
                    up_w_ref[:, 256 * t : 256 * t + 256],
                )
            acc = acc + keep[f, a] * part
        z_ref[f] = acc

        @pl.when((f >= 1) & (f <= 4))
        def _():
            both = jnp.concatenate([column_sum(acc), column_sum(acc * acc)], axis=0)
            payload_ref[...] += jnp.broadcast_to(both[None], payload_ref.shape)


def refine_kernel(
    counts,
    table,
    z_in_ref,
    landed_ref,
    gain_ref,
    w_ref,
    hidden_ref,
    z_ref,
    payload_ref,
    moments_ref,
    taps_ref,
):
    keep, inside = Entries(table, "keep"), Entries(table, "inside")
    total = jnp.sum(landed_ref[...], axis=0)
    mean, inverse = norm_of(total, counts[1])
    moments_ref[0:1] = mean
    moments_ref[1:2] = inverse
    gain = gain_ref[...]
    width = z_ref.shape[1]

    @pl.loop(0, 6)
    def _(f):
        pre = (z_in_ref[f] - mean) * inverse * gain[0:1] + gain[1:2]
        hidden = silu(pre).astype(BF).astype(F32) * inside[f + 1]
        hidden_ref[f] = hidden.astype(BF)
        for b in range(3):
            taps_ref[f, b * width : (b + 1) * width, :] = tap_rows(hidden, b - 1).astype(BF)

    payload_ref[...] = jnp.zeros_like(payload_ref)

    @pl.loop(0, 4)
    def _(f):
        acc = jnp.zeros(z_ref.shape[1:], F32)
        for a in range(3):
            part = None
            for b in range(3):
                t = 3 * a + b
                term = mm(
                    taps_ref[f + a, b * width : (b + 1) * width, :],
                    w_ref[:, 256 * t : 256 * t + 256],
                )
                part = term if part is None else part + term
            acc = acc + keep[f + 1, a] * part
        z_ref[f] = acc
        both = jnp.concatenate([column_sum(acc), column_sum(acc * acc)], axis=0)
        payload_ref[...] += jnp.broadcast_to(both[None], payload_ref.shape)


def classes_kernel(
    images,
    classes,
    counts,
    table,
    z_ref,
    landed_ref,
    gain_ref,
    labels_ref,
    w_ref,
    gp_ref,
    payload_ref,
    moments_ref,
    top_ref,
    bottom_ref,
    block_ref,
    part_ref,
):
    entries = Entries(table, "bias")
    total = jnp.sum(landed_ref[...], axis=0)
    mean, inverse = norm_of(total, counts[1])
    moments_ref[0:1] = mean
    moments_ref[1:2] = inverse
    gain = gain_ref[...]
    weight = w_ref[...]
    width = z_ref.shape[1]
    shape = (weight.shape[0], width)
    ids = lax.broadcasted_iota(jnp.int32, shape, 0)
    ones = jnp.ones((8, width), BF)
    bias = jnp.zeros(shape, F32)
    for i in range(classes):
        bias = jnp.where(ids == i, entries[i], bias)
    rows = [jnp.zeros((1, 256), F32) for _ in range(4)]
    part_ref[...] = jnp.zeros_like(part_ref)
    for f in range(4):
        normed = (z_ref[f] - mean) * inverse
        pre = normed * gain[0:1] + gain[1:2]
        gate = jax.nn.sigmoid(pre)
        refined = (pre * gate).astype(BF)
        logits = mm_nt(weight, refined) + bias
        valid = ids < classes
        logits = jnp.where(valid, logits, -1e30)
        highest = jnp.max(logits, axis=0, keepdims=True)
        exponent = jnp.exp(logits - highest)
        exp_total = jnp.sum(exponent, axis=0, keepdims=True)
        one_hot = ids == labels_ref[f : f + 1, :]
        picked = jnp.sum(jnp.where(one_hot, logits, 0.0), axis=0, keepdims=True)
        rows[3] = rows[3] + jnp.log(exp_total) + highest - picked
        share = exponent / exp_total - jnp.where(one_hot, 1.0, 0.0)
        grad = jnp.where(valid, share / images, 0.0).astype(BF)
        part_ref[...] += mm(grad, refined)
        counted = mm_nt(ones, grad)[0:1]
        rows[2] = rows[2] + jnp.concatenate(
            [counted, jnp.zeros((1, 256 - shape[0]), F32)], axis=1
        )
        gp = mm_tn(grad, weight) * (gate * (1.0 + pre * (1.0 - gate)))
        gp_ref[f] = gp
        rows[0] = rows[0] + column_sum(gp * normed)
        rows[1] = rows[1] + column_sum(gp)
        if f == 0:
            bottom_ref[0] = gp.astype(BF)
            bottom_ref[1] = normed.astype(BF)
        if f == 3:
            top_ref[0] = gp.astype(BF)
            top_ref[1] = normed.astype(BF)
    payload = jnp.concatenate(rows, axis=0)
    payload_ref[...] = jnp.broadcast_to(payload[None], payload_ref.shape)
    block_ref[...] = jnp.zeros_like(block_ref)
    first = lax.broadcasted_iota(jnp.int32, (1, 128), 1) < 64
    for i in range(0, classes, 2):
        for j in range(2):
            one, two = (part_ref[i + n : i + n + 1, 128 * j : 128 * j + 128] for n in range(2))
            at = 128 * (i % 10 // 2)
            for n, value in enumerate(
                (
                    jnp.where(first, one, pltpu.roll(two, 64, 1)),
                    jnp.where(first, pltpu.roll(one, 64, 1), two),
                )
            ):
                block_ref[2 * j + n, i // 10 : i // 10 + 1, at : at + 128] = value


def grad_z(gp, normed, scale, total, count):
    return (scale * (gp - (total[1:2] + normed * total[0:1]) / count)).astype(BF)


def store_taps(ref, f, values):
    width = values.shape[0]
    wide = values.astype(F32)
    for b in range(3):
        ref[f, b * width : (b + 1) * width, :] = tap_rows(wide, 1 - b).astype(BF)


def refine_back_kernel(
    counts,
    table,
    gp_ref,
    z_ref,
    above_ref,
    below_ref,
    landed_ref,
    moments_ref,
    gain_ref,
    w_ref,
    z1_ref,
    moments1_ref,
    gain1_ref,
    out_ref,
    taps_ref,
    payload_ref,
    top_ref,
    bottom_ref,
    total_ref,
    ends_ref,
):
    keep, inside = Entries(table, "keep_back"), Entries(table, "inside")
    total = jnp.sum(landed_ref[...], axis=0)
    total_ref[...] = total
    mean, inverse = moments_ref[0:1], moments_ref[1:2]
    scale = gain_ref[0:1] * inverse
    count = counts[1]
    for ref, at, f in ((above_ref, 0, 0), (below_ref, 1, 5)):
        edge = grad_z(ref[0].astype(F32), ref[1].astype(F32), scale, total, count)
        store_taps(ends_ref, at, edge.astype(F32) * inside[f + 1])

    @pl.loop(0, 4)
    def _(f):
        normed = (z_ref[f] - mean) * inverse
        store_taps(taps_ref, f, grad_z(gp_ref[f], normed, scale, total, count))

    width = out_ref.shape[1]
    mean1, inverse1 = moments1_ref[0:1], moments1_ref[1:2]
    gain1 = gain1_ref[...]
    payload_ref[...] = jnp.zeros_like(payload_ref)
    for g in range(4):
        acc = jnp.zeros(out_ref.shape[1:], F32)
        for a in range(3):
            source = g + 1 - a
            if source < 0:
                rows = ends_ref.at[0]
            elif source > 3:
                rows = ends_ref.at[1]
            else:
                rows = taps_ref.at[source]
            part = None
            for b in range(3):
                t = 3 * a + b
                term = mm_nt(
                    rows[b * width : (b + 1) * width, :], w_ref[:, 256 * t : 256 * t + 256]
                )
                part = term if part is None else part + term
            acc = acc + keep[g, a] * part
        normed = (z1_ref[g + 1] - mean1) * inverse1
        pre = normed * gain1[0:1] + gain1[1:2]
        gate = jax.nn.sigmoid(pre)
        gp = acc * (gate * (1.0 + pre * (1.0 - gate)))
        out_ref[g] = gp
        both = jnp.concatenate([column_sum(gp * normed), column_sum(gp)], axis=0)
        payload_ref[...] += jnp.broadcast_to(both[None], payload_ref.shape)
        if g == 0:
            bottom_ref[...] = gp.astype(BF)
        if g == 3:
            top_ref[...] = gp.astype(BF)


def unite_back_kernel(
    counts,
    table,
    gp_ref,
    z_ref,
    above_ref,
    below_ref,
    landed_ref,
    moments_ref,
    gain_ref,
    up_w_ref,
    low_w_ref,
    columns_ref,
    low_z_ref,
    moments0_ref,
    low_gain_ref,
    taps_ref,
    rows_ref,
    low_gp_ref,
    sums_ref,
    total_ref,
    ends_ref,
    flat_ref,
):
    keep, inside, blend = (Entries(table, name) for name in ("keep_back", "inside", "blend"))
    total = jnp.sum(landed_ref[...], axis=0)
    total_ref[...] = total
    mean, inverse = moments_ref[0:1], moments_ref[1:2]
    scale = gain_ref[0:1] * inverse
    count = counts[1]
    for ref, at, f in ((above_ref, 0, 0), (below_ref, 1, 5)):
        normed = (z_ref[f] - mean) * inverse
        edge = grad_z(ref[...].astype(F32), normed, scale, total, count)
        edge = edge.astype(F32) * inside[f + 1]
        store_taps(ends_ref, at, edge)
        flat_ref[5 * at] = edge.astype(BF)

    @pl.loop(0, 4)
    def _(f):
        normed = (z_ref[f + 1] - mean) * inverse
        edge = grad_z(gp_ref[f], normed, scale, total, count)
        store_taps(taps_ref, f, edge)
        flat_ref[f + 1] = edge

    width = gp_ref.shape[1]
    mean_l, inverse_l = moments0_ref[2:3, 0:128], moments0_ref[3:4, 0:128]
    low_gain = low_gain_ref[...]
    first = lax.broadcasted_iota(jnp.int32, (width, 128), 1) < 64
    rows_ref[...] = jnp.zeros_like(rows_ref)
    sums = [jnp.zeros((1, 128), F32), jnp.zeros((1, 128), F32)]
    for g in range(4):
        acc = jnp.zeros(gp_ref.shape[1:], F32)
        low = jnp.zeros((width, 256), F32)
        for a in range(3):
            source = g + 1 - a
            if source < 0:
                rows = ends_ref.at[0]
            elif source > 3:
                rows = ends_ref.at[1]
            else:
                rows = taps_ref.at[source]
            part = None
            for b in range(3):
                t = 3 * a + b
                term = mm_nt(
                    rows[b * width : (b + 1) * width, :], up_w_ref[:, 256 * t : 256 * t + 256]
                )
                part = term if part is None else part + term
            acc = acc + keep[g, a] * part
            low = low + keep[g, a] * mm_nt(flat_ref[source + 1], low_w_ref[a])
        pair, last = low[:, 0:128], low[:, 128:256]
        low_in = (
            tap_rows(jnp.where(first, pair, 0.0), 1)
            + jnp.where(first, pltpu.roll(pair, 64, 1), 0.0)
            + tap_rows(last, -1)
        )
        grown = mm(columns_ref[...], acc.astype(BF))
        for k in range(3):
            rows_ref[k] += blend[g + 2, k] * grown
        normed = (low_z_ref[g + 2] - mean_l) * inverse_l
        pre = normed * low_gain[0:1] + low_gain[1:2]
        gate = jax.nn.sigmoid(pre)
        gp = low_in * (gate * (1.0 + pre * (1.0 - gate)))
        low_gp_ref[g] = gp
        sums[0] = sums[0] + column_sum(gp * normed)
        sums[1] = sums[1] + column_sum(gp)
    both = jnp.concatenate(sums, axis=0)
    sums_ref[...] = jnp.concatenate([both, jnp.zeros_like(both)], axis=1)


def tap_gradients(keep, h_ref, taps_ref, store):
    width = taps_ref.shape[1] // 3
    channels = h_ref.shape[2]
    first = lax.broadcasted_iota(jnp.int32, (channels, 128), 1) < 64
    other = None
    for t in range(9):
        a, b = t // 3, t % 3
        acc = jnp.zeros((channels, 256), F32)
        for f in range(4):
            acc = acc + keep[f + 1, a] * mm_tn(
                h_ref[f + a], taps_ref[f, b * width : (b + 1) * width, :]
            )
        if t % 2 == 0 and t < 8:
            other = acc
            continue
        x, y = (other, acc) if t % 2 == 1 else (acc, jnp.zeros_like(acc))
        for j in range(2):
            left, right = x[:, 128 * j : 128 * j + 128], y[:, 128 * j : 128 * j + 128]
            store(2 * j, 128 * (t // 2), jnp.where(first, left, pltpu.roll(right, 64, 1)))
            store(2 * j + 1, 128 * (t // 2), jnp.where(first, pltpu.roll(left, 64, 1), right))


def store_rows(out_ref, rows_ref):
    height = out_ref.shape[1]

    def store(y, at, value):
        rows_ref[...] = value
        for i in range(4):
            out_ref[y, :, 640 * i + at : 640 * i + at + 128] = rows_ref[
                pl.ds(i, height, stride=4), :
            ].astype(BF)

    return store


def refine_weight_kernel(table, h_ref, taps_ref, out_ref, rows_ref):
    tap_gradients(Entries(table, "keep"), h_ref, taps_ref, store_rows(out_ref, rows_ref))


def unite_weight_kernel(table, h_ref, act_ref, taps_ref, classes_ref, out_ref, rows_ref):
    keep = Entries(table, "keep")
    tap_gradients(keep, h_ref, taps_ref, store_rows(out_ref, rows_ref))

    def store_low(y, at, value):
        out_ref[y, 0:48, 2560 + at : 2560 + at + 128] = value[0:48].astype(BF)

    tap_gradients(keep, act_ref, taps_ref, store_low)
    out_ref[:, 48:64, 2560:3200] = classes_ref[...].astype(BF)


def low_back_kernel(count, gp_ref, z_ref, total_ref, moments_ref, gain_ref, low_ref, out_ref, part_ref):
    mean, inverse = moments_ref[2:3, 0:128], moments_ref[3:4, 0:128]
    total = total_ref[2:4, 0:128]
    scale = gain_ref[0:1] * inverse
    used = out_ref.shape[1]
    part = jnp.zeros(part_ref.shape, F32)
    for f in range(out_ref.shape[0]):
        normed = (z_ref[f + 2] - mean) * inverse
        grad = grad_z(gp_ref[f], normed, scale, total, count).astype(F32)
        turned = jnp.transpose(grad)[0:used].astype(BF)
        out_ref[f] = turned
        part = part + mm_nt(turned, low_ref[f + 2])
    part_ref[...] = part


def proj_back_sums_kernel(own_ref, above_ref, below_ref, z_ref, moments_ref, gain_ref, low_ref, gp_ref, payload_ref):
    normed = (z_ref[...] - moments_ref[0:1]) * moments_ref[1:2]
    pre = normed * gain_ref[0:1] + gain_ref[1:2]
    gate = jax.nn.sigmoid(pre)
    grad = own_ref[...] + above_ref[...] + below_ref[...]
    gp = grad * (gate * (1.0 + pre * (1.0 - gate)))
    gp_ref[...] = gp
    payload = jnp.concatenate([column_sum(gp * normed), column_sum(gp), low_ref[...]], axis=0)
    payload_ref[...] = jnp.broadcast_to(payload[None], payload_ref.shape)


def proj_back_kernel(
    counts,
    gp_ref,
    z_ref,
    landed_sums_ref,
    moments_ref,
    gain_ref,
    landed_ref,
    main_ref,
    pool_ref,
    out_ref,
    weight_ref,
    total_ref,
    rows_ref,
):
    total = jnp.sum(landed_sums_ref[...], axis=0)
    total_ref[...] = total
    mean, inverse = moments_ref[0:1], moments_ref[1:2]
    normed = (z_ref[...] - mean) * inverse
    grad = grad_z(gp_ref[...], normed, gain_ref[0:1] * inverse, total, counts[0])
    columns = grad.shape[0]
    summed = column_sum(grad.astype(F32))
    high = summed.astype(BF).astype(F32)
    first = lax.broadcasted_iota(jnp.int32, (16, 256), 0) == 0
    high_rows = jnp.where(first, high, 0.0).astype(BF)
    low_rows = jnp.where(first, summed - high, 0.0).astype(BF)
    top = lax.broadcasted_iota(jnp.int32, (16, 128), 0)
    n_s = out_ref.shape[0]
    for s in range(n_s):
        out_ref[s, 0:columns] = mm_nt(grad, main_ref[s]).astype(BF)
        pool = mm_nt(high_rows, pool_ref[s]) + mm_nt(low_rows, pool_ref[s])
        pool_high = pool[0:1].astype(BF).astype(F32)
        pair = jnp.where(top == 0, pool_high, jnp.where(top == 1, pool[0:1] - pool_high, 0.0))
        out_ref[s, columns : columns + 16] = pair.astype(BF)
        place = 64 * (s % (n_s // 2)) + 32 * (s // (n_s // 2))
        main = mm_tn(landed_ref[s, 0:columns], grad)
        for branch in range(4):
            at = 256 * branch + place
            for j in range(2):
                rows_ref[j, at : at + 32] = main[
                    32 * branch : 32 * branch + 32, 128 * j : 128 * j + 128
                ]
        extra = landed_ref[s, columns : columns + 16]
        outer = mm_tn(extra, high_rows) + mm_tn(extra, low_rows)
        for j in range(2):
            rows_ref[j, 1024 + place : 1024 + place + 32] = outer[0:32, 128 * j : 128 * j + 128]
    half = rows_ref.shape[1] // 2
    left = lax.broadcasted_iota(jnp.int32, (half, 128), 1) < 64
    for j in range(2):
        even = rows_ref[j, pl.ds(0, half, stride=2), :]
        odd = rows_ref[j, pl.ds(1, half, stride=2), :]
        weight_ref[2 * j] = jnp.where(left, even, pltpu.roll(odd, 64, 1)).astype(BF)
        weight_ref[2 * j + 1] = jnp.where(left, pltpu.roll(even, 64, 1), odd).astype(BF)


def spatial_back_sums_kernel(
    pixels, table, back_ref, spatial_ref, landed_ref, gains_ref, gp_ref, payload_ref
):
    member = Entries(table, "member")
    total = jnp.sum(landed_ref[...], axis=0)
    gains = gains_ref[...]
    mean, inverse = norm_of(total, pixels)
    columns = spatial_ref.shape[1]
    rows = [jnp.zeros((1, 128), F32), jnp.zeros((1, 128), F32)]
    pools = []
    for r in range(spatial_ref.shape[0]):
        normed = (spatial_ref[r] - mean) * inverse
        pre = normed * gains[0:1] + gains[1:2]
        gate = jax.nn.sigmoid(pre)
        gp = back_ref[r, 0:columns].astype(F32) * (gate * (1.0 + pre * (1.0 - gate)))
        gp_ref[r] = gp
        rows[0] = rows[0] + column_sum(gp * normed)
        rows[1] = rows[1] + column_sum(gp)
        pools.append(column_sum(back_ref[r, columns : columns + 16].astype(F32)))
    first = slot_mask((1, 128), 0)
    packed = [jnp.zeros((1, 128), F32), jnp.zeros((1, 128), F32)]
    for m in range(8):
        part = sum(member[r, m] * pools[r] for r in range(len(pools)))
        packed[m // 4] = packed[m // 4] + lane_roll(jnp.where(first, part, 0.0), 32 * (m % 4))
    payload = jnp.concatenate(rows + packed, axis=0)
    payload_ref[...] = jnp.broadcast_to(payload[None], payload_ref.shape)


def spatial_back_kernel(
    pixels,
    table,
    gp_ref,
    spatial_ref,
    landed_ref,
    landed_back_ref,
    gains_ref,
    out_ref,
    pool_ref,
    gains_out_ref,
):
    counts = Entries(table, "counts")
    total = jnp.sum(landed_ref[...], axis=0)
    back = jnp.sum(landed_back_ref[...], axis=0)
    gains = gains_ref[...]
    mean, inverse = norm_of(total, pixels)
    scale = gains[0:1] * inverse
    for r in range(spatial_ref.shape[0]):
        normed = (spatial_ref[r] - mean) * inverse
        out_ref[r] = grad_z(gp_ref[r], normed, scale, back, pixels)
    normed, inverse_p, pre = pool_norm(total, counts, gains)
    gate = jax.nn.sigmoid(pre)
    gp = jnp.concatenate(pool_rows_of(back, 2), axis=0) * (gate * (1.0 + pre * (1.0 - gate)))
    gain_grad = column_sum(gp * normed)
    shift_grad = column_sum(gp)
    grad = gains[2:3] * inverse_p * (gp - (shift_grad + normed * gain_grad) / 8.0)
    pool_ref[...] = jnp.concatenate([grad[m : m + 1] / counts[m] for m in range(8)], axis=0)
    gains_out_ref[...] = jnp.concatenate([back[0:2], gain_grad, shift_grad], axis=0)


def spread_kernel(
    place,
    table,
    wide_ref,
    above_ref,
    below_ref,
    pool_ref,
    feats_ref,
    rest_ref,
    weight_ref,
    own_ref,
    spread_ref,
    reach_ref,
):
    keep = Entries(table, "group")
    height = wide_ref.shape[0]
    columns = wide_ref.shape[1]
    reach_ref[0:REACH] = above_ref[...]
    reach_ref[REACH : REACH + height] = wide_ref[...]
    reach_ref[REACH + height :] = below_ref[...]
    shape = (columns, 128)
    masks = [slot_mask(shape, slot) for slot in range(4)]
    ids = lax.broadcasted_iota(jnp.int32, shape, 0)

    @pl.loop(0, height)
    def _(r):
        own = reach_ref[REACH + r].astype(F32)
        start = pl.multiple_of(r * columns, columns)
        for k, d in enumerate(DILATIONS):
            mixed = jnp.zeros(shape, F32)
            for a in range(3):
                source = own if a == 1 else reach_ref[REACH + r - (a - 1) * d].astype(F32)
                moved = lane_roll(source, 32 * (a - k - 1)) * keep[3 * k + a, r]
                mixed = jnp.where(masks[a], moved, mixed)
            left = jnp.where(ids < columns - d, pltpu.roll(mixed, columns - d, 0), 0.0)
            right = jnp.where(ids >= d, pltpu.roll(mixed, d, 0), 0.0)
            if k == 0:
                mixed = jnp.where(masks[3], lane_roll(own, 96), mixed)
            if k == 1:
                window = lane_roll(pool_ref[pl.ds(r, 1), :], 96)
                mixed = jnp.where(masks[3], window, mixed)
            for j, value in enumerate((left, mixed, right)):
                at = 128 * (3 * k + j)
                spread_ref[pl.ds(start, columns), at : at + 128] = value.astype(BF)

    n_y = feats_ref.shape[0] // 2
    block = feats_ref.shape[1] * 8 // height
    strip = 2 * block
    wide = feats_ref.shape[2]

    @pl.loop(0, n_y)
    def _(y):
        acc = jnp.zeros((wide, spread_ref.shape[1]), F32)
        for core in range(2):
            for x in range(spread_ref.shape[0] // strip):
                acc = acc + mm_tn(
                    feats_ref[core * n_y + y, x * block : (x + 1) * block, :],
                    spread_ref[x * strip + core * block : x * strip + (core + 1) * block, :],
                )
        half = wide // 2
        for i in range(2):
            weight_ref[2 * y + i, 0:half, :] = acc[half * i : half * (i + 1)].astype(BF)

    rows, lanes = rest_ref.shape
    for z in range(weight_ref.shape[0]):
        weight_ref[z, 64 : 64 + rows, 0:lanes] = rest_ref[...]
        weight_ref[z, 64 : 64 + rows, lanes:] = jnp.zeros((rows, weight_ref.shape[2] - lanes), BF)

    own_ref[...] = spread_ref[pl.ds(pl.multiple_of(place[0] * strip, strip), strip), :]


def feature_kernel(spread_ref, w_ref, grad_ref):
    n_y, block, depth = grad_ref.shape[1:]

    @pl.loop(0, 2 * n_y)
    def _(i):
        part = pl.multiple_of((i // n_y) * block, block)
        deep = pl.multiple_of((i % n_y) * depth, depth)
        grad_ref[i // n_y, i % n_y] = mm_nt(
            spread_ref[pl.ds(part, block), :], w_ref[pl.ds(deep, depth), :]
        ).astype(BF)


def on_device(
    features,
    low_level,
    labels,
    crop_rows,
    w_one,
    w_atrous,
    w_pool,
    w_proj,
    w_low,
    w_unite_up,
    w_unite_low,
    w_refine,
    w_classes,
    b_classes,
    gain_aspp,
    shift_aspp,
    gain_proj,
    shift_proj,
    gain_low,
    shift_low,
    gain_dec,
    shift_dec,
):
    n_y, n_z, n_x = lax.axis_size("y"), lax.axis_size("z"), lax.axis_size("x")
    core, yi, xi, zi = (lax.axis_index(a) for a in ("core", "y", "x", "z"))
    strip = lax.axis_index(STRIP)
    row = lax.axis_index(ALL)
    groups = lax.axis_size(ROWS)
    rows_in, columns, c_part = features.shape
    total_rows = rows_in * groups
    c_in = c_part * n_y
    fine_strip, c_low, fine_columns = low_level.shape
    fine_total = fine_strip * groups
    branch = w_proj.shape[1] * n_y
    o_part = w_one.shape[1]
    half = o_part // 2
    low_out = w_low.shape[1] * n_y
    classes = w_classes.shape[1]
    images = crop_rows.shape[0]
    pixels = float(total_rows * columns)
    fine_pixels = float(fine_total * fine_columns)
    tall = 2 * rows_in
    counts_static = (pixels, fine_pixels)

    atrous = w_atrous.transpose(0, 1, 3, 2, 4).reshape(w_one.shape[0], 27, o_part)
    own = jnp.concatenate([atrous, w_one[:, None], w_pool[:, None]], axis=1)
    paired = lax.all_to_all(own, "core", 2, 0, tiled=True)
    paired = paired.reshape(paired.shape[0], -1)
    first = jnp.concatenate([paired] + [hop(paired, "x", k) for k in range(1, n_x)])
    inputs = (
        features,
        low_level,
        w_proj,
        w_low,
        w_unite_up,
        w_unite_low,
        w_refine,
        w_classes,
        gain_proj,
        shift_proj,
        gain_low,
        shift_low,
        gain_dec,
        shift_dec,
    )
    first, inputs = lax.optimization_barrier((first, inputs))
    (
        features,
        low_level,
        w_proj,
        w_low,
        w_unite_up,
        w_unite_low,
        w_refine,
        w_classes,
        gain_proj,
        shift_proj,
        gain_low,
        shift_low,
        gain_dec,
        shift_dec,
    ) = inputs
    first = lax.all_gather(first, "z", axis=0, tiled=True)

    flat_feats = features.reshape(-1, c_part)
    feats = jnp.stack([flat_feats] + [hop(flat_feats, "y", k) for k in range(1, n_y)])
    feats_other = hop(feats, "core", 1)

    k_row = w_refine.shape[0]
    shard = jnp.concatenate(
        [
            w_unite_up.reshape(k_row, 9, o_part),
            w_refine.reshape(k_row, 9, o_part),
            w_proj.reshape(k_row, -1, o_part),
            jnp.pad(w_low, ((0, 0), (0, o_part - w_low.shape[1])))[:, None],
        ],
        axis=1,
    )
    low_raw = jnp.pad(w_unite_low.reshape(low_out, 9, o_part), ((0, 0), (0, 1), (0, 0)))
    low_raw = low_raw.reshape(low_out, 5, 2 * o_part).transpose(1, 0, 2)
    class_raw = jnp.pad(w_classes.T, ((0, 32 - classes), (0, 0)))
    sizes = [shard.size, low_raw.size, class_raw.size]
    sent = jnp.concatenate([shard.reshape(-1, 128), low_raw.reshape(-1, 128), class_raw.reshape(-1, 128)])
    sent = gathered(sent, "y").reshape(n_y, -1)
    shard = sent[:, : sizes[0]].reshape(n_y, k_row, 24, o_part)
    shard = shard.transpose(1, 2, 0, 3).reshape(k_row, -1)
    low_raw = sent[:, sizes[0] : sizes[0] + sizes[1]].reshape((n_y,) + low_raw.shape)
    classes_w = sent[:, sizes[0] + sizes[1] :].reshape(n_y, 32, o_part)
    classes_w = classes_w.transpose(1, 0, 2).reshape(32, branch)
    shard = gathered(gathered(shard, "core"), "x").reshape(-1, shard.shape[1])
    strips = [(r * n_y, (r + 1) * n_y) for r in range(groups - 1)]
    route = strips + [(target + n_y - 1, source + n_y - 1) for source, target in strips]
    edge = jnp.where(yi == 0, low_level[-2:], low_level[:2])
    edge = lax.ppermute(edge, ALL, route)
    low_rows = jnp.concatenate([edge, low_level, edge], axis=0)
    low_rows = lax.dynamic_slice_in_dim(low_rows, yi * 4, 8, 0)
    labels_own = lax.dynamic_slice_in_dim(labels, yi * 4, 4, 0)

    place = jnp.stack([xi, yi, core]).astype(jnp.int32)
    wide_c = 4 * half
    edge10, edge2 = ((3, columns, wide_c), BF), ((1, columns, wide_c), BF)
    part = ((tall, columns, wide_c), F32)
    later = (gain_low, shift_low, gain_dec, shift_dec, gain_proj, shift_proj)
    later += (crop_rows, b_classes, gain_aspp, shift_aspp)
    later, shard = lax.optimization_barrier((later, shard))
    gain_low, shift_low, gain_dec, shift_dec, gain_proj, shift_proj = later[:6]
    crop_rows, b_classes, gain_aspp, shift_aspp = later[6:]
    image_ends, reached = [], jnp.int32(0)
    for m in range(images):
        reached = reached + crop_rows[m]
        image_ends.append(reached)
    fine_ends = [4 * end for end in image_ends]
    counts = crop_rows.astype(F32) * float(columns)
    rows8 = strip * tall + jnp.arange(tall, dtype=jnp.int32)

    rows3 = row - 1 + jnp.arange(3, dtype=jnp.int32)
    fine8 = 4 * row - 2 + jnp.arange(8, dtype=jnp.int32)
    fine6, fine4 = fine8[1:7], fine8[2:6]
    inside = ((fine8 >= 0) & (fine8 < fine_total)).astype(F32)
    keep = jnp.stack([same_image(fine6, a - 1, fine_ends, fine_total) for a in range(3)], axis=1)
    keep_back = jnp.stack(
        [same_image(fine4 - (a - 1), a - 1, fine_ends, fine_total) for a in range(3)], axis=1
    )
    row_blend = blend_matrix(fine8, rows3, image_ends, total_rows)
    columns_up, columns_back = column_matrices(columns)
    up = jnp.stack([same_image(rows8, -d, image_ends, total_rows) for d in DILATIONS])
    down = jnp.stack([same_image(rows8, d, image_ends, total_rows) for d in DILATIONS])
    crops = jnp.arange(images, dtype=jnp.int32)
    member = (image_of(rows8, image_ends)[:, None] == crops[None, :]).astype(F32)

    ids = zi * (n_x * tall) + jnp.arange(n_x * tall, dtype=jnp.int32)
    keep_group = jnp.stack(
        [
            same_image(ids - (a - 1) * d, (a - 1) * d, image_ends, total_rows)
            for d in DILATIONS
            for a in range(3)
        ]
    )
    entries = [
        keep,
        keep_back,
        inside,
        row_blend,
        up,
        down,
        member,
        counts,
        jnp.pad(b_classes, (0, 32 - classes)),
        keep_group,
    ]
    table = jnp.concatenate([jnp.ravel(e) for e in entries])
    halves = jnp.stack([gain_aspp, shift_aspp])
    halves = lax.dynamic_slice_in_dim(halves, core * half, half, 2)
    gains_sp = jnp.concatenate(
        [
            halves[:, :4].reshape(2, -1),
            jnp.pad(halves[:, 4], ((0, 0), (0, 3 * half))),
        ]
    )
    lows = jnp.pad(jnp.stack([gain_low, shift_low]), ((0, 0), (0, o_part - gain_low.shape[0])))
    vectors = jnp.concatenate(
        [
            jnp.stack([gain_dec, shift_dec], axis=1).reshape(4, -1),
            jnp.stack([gain_proj, shift_proj]),
            lows,
        ]
    )
    vectors = gathered(vectors.reshape(4, 128), "y").reshape(n_y, 8, o_part).transpose(1, 0, 2)
    lows = vectors[6:, :, : gain_low.shape[0]].reshape(2, low_out)
    vectors = vectors[:6].reshape(6, branch)
    gain_1, gain_2, gain_p = vectors[0:2], vectors[2:4], vectors[4:6]
    gain_l = jnp.pad(lows, ((0, 0), (0, 128 - low_out)))
    (low_w,) = run_kernel(low_weight_kernel, [], [low_raw], [((3, 256, branch), BF)])
    moved = (feats, feats_other, low_rows, shard, low_w, classes_w, table, gains_sp)
    moved += (gain_1, gain_2, gain_p, gain_l)
    first, moved = lax.optimization_barrier((first, moved))
    feats, feats_other, low_rows, shard, low_w, classes_w, table, gains_sp = moved[:8]
    gain_1, gain_2, gain_p, gain_l = moved[8:]
    dec = lax.all_gather(shard, "z", axis=0, tiled=True)
    padded_w, a0, a1, a2, p1, p2, p3, m1, m2, m3 = run_kernel(
        product_kernel,
        [place],
        [feats, feats_other, first],
        [((c_in, 9 * wide_c), BF), part, part, part, edge10, edge10, edge2, edge10, edge10, edge2],
        [((tall * columns, 9 * wide_c), F32)],
    )
    features, _ = lax.optimization_barrier((features, p1))
    digits = features.reshape(rows_in, columns, c_part // (n_x * o_part), n_x, o_part)
    digits = jnp.moveaxis(digits, 3, 0).reshape(n_x, rows_in * columns, -1)
    by_x = lax.all_to_all(digits, "x", 0, 0, tiled=True).reshape(-1, digits.shape[2])
    edges = [
        hop_open(p1, STRIP, -1),
        hop_open(p2, STRIP, -2),
        hop_open(p3, STRIP, -3),
        hop_open(m1, STRIP, 1),
        hop_open(m2, STRIP, 2),
        hop_open(m3, STRIP, 3),
    ]
    by_x, edges = lax.optimization_barrier((by_x, edges))
    n_strips = n_z * n_x
    spatial, payload = run_kernel(
        spatial_kernel,
        [table],
        [a0, a1, a2] + edges,
        [part, ((n_strips, 4, wide_c), F32)],
    )
    landed_sp = lax.all_to_all(payload, STRIP, 0, 0, tiled=True)
    pieces_w = ((2 * n_y, 4 * half, branch), BF)
    main_w, pool_w, shrink = run_kernel(
        functools.partial(shared_weight_kernel, w_low.shape[1]),
        [],
        [Lanes(dec, 6 * branch, 3)],
        [pieces_w, pieces_w, ((c_low, 128), BF)],
        [((2, w_proj.shape[0] * groups, 128), F32)],
    )
    low_z = dot("fcv,co->fvo", low_rows, shrink)
    low_sums = jnp.stack(
        [jnp.sum(low_z[2:6], axis=(0, 1)), jnp.sum(jnp.square(low_z[2:6]), axis=(0, 1))]
    )
    low_sums = jnp.pad(low_sums, ((0, 0), (0, branch - 128)))
    (payload,) = run_kernel(
        functools.partial(act_kernel, pixels),
        [table],
        [spatial, landed_sp, gains_sp],
        [((tall, columns + 16, wide_c), BF)],
    )

    landed = lax.all_to_all(payload, GROUP, 0, 0, tiled=True)
    n_first = 2 * n_x * n_y
    proj_z, payload = run_kernel(
        proj_kernel,
        [],
        [landed, main_w, pool_w, low_sums],
        [((columns, branch), F32), ((n_first, 4, branch), F32)],
    )

    def exchanged(block):
        block = lax.all_to_all(block, ("x", "core", "y"), 0, 0, tiled=True)
        (block,) = run_kernel(sum_kernel, [], [block], [((n_z,) + block.shape[1:], F32)])
        return lax.all_to_all(block, "z", 0, 0, tiled=True)

    proj_above = hop_open(proj_z, ALL, 1)
    proj_below = hop_open(proj_z, ALL, -1)
    landed_p = exchanged(payload)

    feats_x = lax.all_gather(by_x, GROUP, axis=0, tiled=False)

    fine = (fine_columns, branch)
    sums2, sums4 = ((n_first, 2, branch), F32), ((n_first, 4, branch), F32)
    united_z, united_up, low_act, payload, moments_0 = run_kernel(
        functools.partial(unite_kernel, counts_static),
        [table],
        [
            proj_z,
            proj_above,
            proj_below,
            landed_p,
            gain_p,
            low_z,
            gain_l,
            columns_up,
            Lanes(dec, 9 * branch, 0),
            low_w,
        ],
        [
            ((6,) + fine, F32),
            ((6,) + fine, BF),
            ((6, fine_columns, 128), BF),
            sums2,
            ((4, branch), F32),
        ],
        [
            ((8, 3 * fine_columns, branch), BF),
            ((8, fine_columns, 256), BF),
            ((3, columns, branch), F32),
        ],
    )
    landed_1 = exchanged(payload)
    hidden, refine_z, payload, moments_1 = run_kernel(
        functools.partial(refine_kernel, counts_static),
        [table],
        [united_z, landed_1, gain_1, Lanes(dec, 9 * branch, 1)],
        [((6,) + fine, BF), ((4,) + fine, F32), sums2, ((2, branch), F32)],
        [((6, 3 * fine_columns, branch), BF)],
    )
    landed_2 = exchanged(payload)
    edge = ((2,) + fine, BF)
    gp_2, payload, moments_2, top, bottom, class_block = run_kernel(
        functools.partial(classes_kernel, images, classes, counts_static),
        [table],
        [refine_z, landed_2, gain_2, labels_own, classes_w],
        [
            ((4,) + fine, F32),
            sums4,
            ((2, branch), F32),
            edge,
            edge,
            ((n_y, 16, 10 * o_part), F32),
        ],
        [((32, branch), F32)],
    )
    edge_above = hop_open(top, ALL, 1)
    edge_below = hop_open(bottom, ALL, -1)
    landed_g2 = exchanged(payload)
    edge = (fine, BF)
    gp_1, taps_2, payload, top, bottom, total_2 = run_kernel(
        functools.partial(refine_back_kernel, counts_static),
        [table],
        [
            gp_2,
            refine_z,
            edge_above,
            edge_below,
            landed_g2,
            moments_2,
            gain_2,
            Lanes(dec, 9 * branch, 1),
            united_z,
            moments_1,
            gain_1,
        ],
        [
            ((4,) + fine, F32),
            ((4, 3 * fine_columns, branch), BF),
            sums2,
            edge,
            edge,
            ((4, branch), F32),
        ],
        [((2, 3 * fine_columns, branch), BF)],
    )
    edge_above = hop_open(top, ALL, 1)
    edge_below = hop_open(bottom, ALL, -1)
    landed_g1 = exchanged(payload)
    grad_lanes = 5 * 2 * o_part
    (refine_part,) = run_kernel(
        refine_weight_kernel,
        [table],
        [hidden, taps_2],
        [((n_y, groups, k_row * grad_lanes), BF)],
        [((branch, 128), F32)],
    )
    taps_1, to_rows, gp_l, low_back, total_1 = run_kernel(
        functools.partial(unite_back_kernel, counts_static),
        [table],
        [
            gp_1,
            united_z,
            edge_above,
            edge_below,
            landed_g1,
            moments_1,
            gain_1,
            Lanes(dec, 9 * branch, 0),
            low_w,
            columns_back,
            low_z,
            moments_0,
            gain_l,
        ],
        [
            ((4, 3 * fine_columns, branch), BF),
            ((3, columns, branch), F32),
            ((4, fine_columns, 128), F32),
            ((2, branch), F32),
            ((2, branch), F32),
        ],
        [((2, 3 * fine_columns, branch), BF), ((6,) + fine, BF)],
    )
    to_above = hop_open(to_rows[0], ALL, -1)
    to_below = hop_open(to_rows[2], ALL, 1)
    gp_p, payload = run_kernel(
        proj_back_sums_kernel,
        [],
        [to_rows[1], to_above, to_below, proj_z, moments_0, gain_p, low_back],
        [((columns, branch), F32), sums4],
    )
    taps_late, payload = lax.optimization_barrier((taps_1, payload))
    (unite_part,) = run_kernel(
        unite_weight_kernel,
        [table],
        [united_up, low_act, taps_late, class_block],
        [((n_y, groups, (k_row + 1) * grad_lanes), BF)],
        [((branch, 128), F32)],
    )
    landed_gp = exchanged(payload)
    payload, proj_part, total_p = run_kernel(
        functools.partial(proj_back_kernel, counts_static),
        [],
        [gp_p, proj_z, landed_gp, moments_0, gain_p, landed, main_w, pool_w],
        [
            ((2 * n_y, columns + 16, wide_c), BF),
            ((n_y, w_proj.shape[0] * groups // 2, 2 * o_part), BF),
            ((4, branch), F32),
        ],
        [((2, w_proj.shape[0] * groups, 128), F32)],
    )
    back = lax.all_to_all(payload, GROUP, 0, 0, tiled=True)
    gp_sp, payload = run_kernel(
        functools.partial(spatial_back_sums_kernel, pixels),
        [table],
        [back, spatial, landed_sp, gains_sp],
        [part, ((n_strips, 4, wide_c), F32)],
    )
    gp_l, proj_part, payload = lax.optimization_barrier((gp_l, proj_part, payload))
    landed_gsp = lax.all_to_all(payload, STRIP, 0, 0, tiled=True)
    grad_sp, pool_grad, gain_grads = run_kernel(
        functools.partial(spatial_back_kernel, pixels),
        [table],
        [gp_sp, spatial, landed_sp, landed_gsp, gains_sp],
        [((tall, columns, wide_c), BF), ((8, wide_c), F32), ((4, wide_c), F32)],
    )

    group_rows = n_x * tall
    grad_low_z, shrink_part = run_kernel(
        functools.partial(low_back_kernel, fine_pixels),
        [],
        [gp_l, low_z, total_p, moments_0, gain_l, low_rows],
        [((4, low_out, fine_columns), BF), ((low_out, c_low), F32)],
    )
    grad_low_all = gathered(grad_low_z, "y").reshape(fine_strip, low_out, fine_columns)
    shrink_own = lax.dynamic_slice_in_dim(shrink, yi * (c_low // n_y), c_low // n_y, 0)
    grad_low_level = dot("fov,co->fcv", grad_low_all, shrink_own[:, :low_out])

    late = jnp.concatenate(
        [proj_part, shrink_part.reshape(n_y, -1, 2 * o_part).astype(BF)], axis=1
    )
    late = scattered(late, "y").astype(BF)
    n_proj = proj_part.shape[1]
    shrink_sum = late[n_proj:].reshape(-1, groups, w_low.shape[0]).transpose(1, 0, 2)
    pieces = [
        scattered(refine_part, "y").astype(BF),
        scattered(unite_part, "y").astype(BF),
        late[:n_proj].reshape(groups, -1),
        shrink_sum.reshape(groups, -1),
    ]
    filled = sum(piece.shape[1] for piece in pieces)
    pieces = jnp.concatenate(pieces + [jnp.zeros((groups, -filled % 1024), BF)], axis=1)
    pieces = pieces.reshape(groups, -1, 128)
    pieces, grad_sp = lax.optimization_barrier((pieces, grad_sp))
    wide = gathered(grad_sp, "x").reshape(group_rows, columns, wide_c)
    reach_above = hop_open(wide[group_rows - REACH :], "z", 1)
    reach_below = hop_open(wide[:REACH], "z", -1)
    pieces = lax.all_to_all(pieces, ROWS, 0, 0, tiled=True)
    taps9 = (9, k_row, o_part)
    grad_refine, grad_unite_up, grad_proj, shrink_sum, rest = run_kernel(
        pieces_kernel,
        [],
        [pieces],
        [(taps9, F32), (taps9, F32), (w_proj.shape, F32), ((1, 128), F32), ((5, 128), BF)],
    )
    grad_refine, grad_unite_up = (
        g.reshape(3, 3, k_row, o_part).transpose(2, 0, 1, 3) for g in (grad_refine, grad_unite_up)
    )
    grad_shrink = shrink_sum[0, : w_low.size].reshape(-1, w_low.shape[0]).T
    rest = gathered(gathered(rest, "core"), "x").reshape(2 * n_x, grad_lanes)
    member_group = (image_of(ids, image_ends)[:, None] == crops[None, :]).astype(F32)
    pool_window = jnp.dot(member_group, pool_grad, precision=PRECISE)
    own_lanes = (tall * columns, 9 * wide_c)
    aspp_part, spread = run_kernel(
        spread_kernel,
        [place, table],
        [wide, reach_above, reach_below, pool_window, feats_x, rest],
        [((n_z, o_part + 2 * n_x, 9 * wide_c), BF), (own_lanes, BF)],
        [
            ((group_rows * columns, 9 * wide_c), BF),
            ((group_rows + 2 * REACH, columns, wide_c), BF),
        ],
    )
    (grad_feats,) = run_kernel(
        feature_kernel,
        [],
        [spread, padded_w],
        [((2, n_y, rows_in * columns, c_part), BF)],
    )

    aspp_sum = lax.all_to_all(aspp_part, "z", 0, 0, tiled=True)
    half_rows = (half, 9 * wide_c)
    mine_w, theirs_w, grad_unite_low, grad_classes = run_kernel(
        landed_kernel,
        [place],
        [aspp_sum],
        [(half_rows, F32), (half_rows, BF), ((9, low_out, o_part), F32), ((classes, o_part), F32)],
    )
    grad_unite_low = grad_unite_low.reshape(3, 3, low_out, o_part).transpose(2, 0, 1, 3)
    grad_classes = grad_classes.T
    theirs_w = hop(theirs_w, "core", 1)
    grad_atrous, grad_one, grad_pool = run_kernel(
        joined_kernel,
        [place],
        [mine_w, theirs_w],
        [((3, 3, 3, half, o_part), F32), ((half, o_part), F32), ((half, o_part), F32)],
    )
    grad_atrous = grad_atrous.transpose(3, 0, 1, 2, 4)

    mine = lax.dynamic_index_in_dim(grad_feats, core, 0, keepdims=False)
    theirs = hop(lax.dynamic_index_in_dim(grad_feats, 1 - core, 0, keepdims=False), "core", 1)
    paired = mine.astype(F32) + theirs.astype(F32)
    grad_features = scattered(paired, "y").reshape(features.shape)

    grad_bias = total_2[2, :classes]
    loss_value = jnp.sum(total_2[3]) / images
    both = gathered(gain_grads, "core")
    both = both.reshape(2, 2, 2, 4, half)
    both = jnp.concatenate([both[:, 0], both[:, 1, :, :1]], axis=2)
    both = both.transpose(1, 2, 0, 3).reshape(2, 5, o_part)

    def own_channels(vector):
        size = vector.shape[-1] // n_y
        return lax.dynamic_slice_in_dim(vector, yi * size, size, vector.ndim - 1)

    return (
        loss_value,
        grad_features,
        grad_low_level,
        grad_one,
        grad_atrous,
        grad_pool,
        grad_proj,
        grad_shrink,
        grad_unite_up,
        grad_unite_low,
        grad_refine,
        grad_classes,
        grad_bias,
        both[0],
        both[1],
        own_channels(total_p[0]),
        own_channels(total_p[1]),
        own_channels(total_p[2, :low_out]),
        own_channels(total_p[3, :low_out]),
        own_channels(jnp.stack([total_1[0], total_2[0]])),
        own_channels(jnp.stack([total_1[1], total_2[1]])),
    )


def solution(mesh):
    torus = Mesh(mesh.devices.reshape(8, 4, 2, mesh.shape["ch"]), ALL)
    in_specs = (
        P(ROWS, None, "y"),
        P(ROWS, None, None),
        P(ROWS, None),
        P(),
        P(ROWS, "y"),
        P(ROWS, None, None, None, "y"),
        P(ROWS, "y"),
        P(ROWS, "y"),
        P(ROWS, "y"),
        P(ROWS, None, None, "y"),
        P(None, None, None, "y"),
        P(ROWS, None, None, "y"),
        P("y", None),
        P(),
        P(None, "y"),
        P(None, "y"),
        P("y"),
        P("y"),
        P("y"),
        P("y"),
        P(None, "y"),
        P(None, "y"),
    )
    out_specs = (
        P(),
        P(ROWS, None, "y"),
        P(ROWS, "y", None),
        P(ROWS, "y"),
        P(ROWS, None, None, None, "y"),
        P(ROWS, "y"),
        P(ROWS, "y"),
        P(ROWS, "y"),
        P(ROWS, None, None, "y"),
        P(None, None, None, "y"),
        P(ROWS, None, None, "y"),
        P("y", None),
        P(),
        P(None, "y"),
        P(None, "y"),
        P("y"),
        P("y"),
        P("y"),
        P("y"),
        P(None, "y"),
        P(None, "y"),
    )
    return jax.shard_map(
        on_device, mesh=torus, in_specs=in_specs, out_specs=out_specs, check_vma=False
    )
```

```python
import functools

import jax
import jax.numpy as jnp
import numpy as np
from jax import lax
from jax.experimental import pallas as pl
from jax.experimental.pallas import tpu as pltpu
from jax.sharding import Mesh
from jax.sharding import PartitionSpec as P

DILATIONS = (6, 12, 18)
REACH = 18
EPSILON = 1e-05
BF = jnp.bfloat16
F32 = jnp.float32

ROWS = ("z", "x", "core")
ALL = ("z", "x", "core", "y")
STRIP = ("z", "x")
GROUP = ("core", "y")


def hop(block, axes, distance):
    n = lax.axis_size(axes)
    return lax.ppermute(block, axes, [(i, (i + distance) % n) for i in range(n)])


def hop_open(block, axes, distance):
    n = lax.axis_size(axes)
    route = [(i, i + distance) for i in range(n) if 0 <= i + distance < n]
    return lax.ppermute(block, axes, route)


def scattered(pieces, axis):
    n = lax.axis_size(axis)
    me = lax.axis_index(axis)
    own = lax.dynamic_index_in_dim(pieces, me, 0, keepdims=False).astype(F32)
    low = pieces.astype(BF)
    for k in range(1, n):
        piece = lax.dynamic_index_in_dim(low, (me + k) % n, 0, keepdims=False)
        own = own + hop(piece, axis, k).astype(F32)
    return own


def gathered(block, axis):
    n = lax.axis_size(axis)
    me = lax.axis_index(axis)
    out = jnp.zeros((n,) + block.shape, block.dtype)
    out = lax.dynamic_update_index_in_dim(out, block, me, 0)
    for k in range(1, n):
        out = lax.dynamic_update_index_in_dim(out, hop(block, axis, k), (me - k) % n, 0)
    return out


def shifted(values, step, axis):
    if step == 0:
        return values
    extent = values.shape[axis]
    pads = [(0, 0)] * values.ndim
    pads[axis] = (max(-step, 0), max(step, 0))
    padded = jnp.pad(values, pads)
    start = max(step, 0)
    return lax.slice_in_dim(padded, start, start + extent, axis=axis)


def taps(values, sign):
    return jnp.concatenate([shifted(values, sign * b, 2) for b in (-1, 0, 1)], axis=1)


def dot(spec, a, b):
    return jnp.einsum(spec, a, b, preferred_element_type=F32)


def column_matrices(columns):
    blend = np.zeros((4 * columns, columns), np.float32)
    for v in range(4 * columns):
        source, quarter = divmod(v, 4)
        near = source - 1 if quarter < 2 else source + 1
        share = (0.375 if quarter in (0, 3) else 0.125) if 0 <= near < columns else 0.0
        blend[v, source] += 1.0 - share
        if share:
            blend[v, near] += share
    edge = np.zeros((1, columns), np.float32)
    moved = [np.concatenate([edge, blend[:-1]]), blend, np.concatenate([blend[1:], edge])]
    grown = np.concatenate(moved)
    return jnp.asarray(np.concatenate([grown, grown], axis=1), BF), jnp.asarray(blend.T, BF)


VMEM = pltpu.VMEM
SMEM = pltpu.SMEM


def mm(a, b):
    return lax.dot_general(a, b, (((1,), (0,)), ((), ())), preferred_element_type=F32)


def mm_nt(a, b):
    return lax.dot_general(a, b, (((1,), (1,)), ((), ())), preferred_element_type=F32)


def mm_tn(a, b):
    return lax.dot_general(a, b, (((0,), (0,)), ((), ())), preferred_element_type=F32)


SPARE = (0, 2, 3)
LAYOUT = {}
for _name, _rows, _columns in (
    ("keep", 6, 3),
    ("keep_back", 4, 3),
    ("inside", 1, 8),
    ("blend", 8, 3),
    ("up", 3, 8),
    ("down", 3, 8),
    ("group", 9, 32),
    ("member", 8, 8),
    ("crowd", 32, 8),
    ("counts", 1, 8),
    ("bias", 1, 32),
):
    LAYOUT[_name] = (sum(r * c for _, r, c in LAYOUT.values()), _rows, _columns)


def pair_entries(tall, reach_rows):
    rows = []

    def add(fine, by, at, offset, base=0.0, slope=1.0, crop=-1):
        rows.append((fine, by == "row", by == "strip", by == "group", at, offset, base, slope, crop))

    for f in range(6):
        for a in range(3):
            add(1, "row", f - 1, a - 1)
    for f in range(4):
        for a in range(3):
            add(1, "row", f - (a - 1), a - 1)
    for f in range(8):
        add(1, "row", f - 2, 0)
    for f in range(8):
        source, quarter = divmod(f - 2, 4)
        step = -1 if quarter < 2 else 1
        share = 0.375 if quarter in (0, 3) else 0.125
        for k in range(3):
            target = k - 1
            if target == source:
                add(0, "row", source, step, 1.0, -share)
            elif target == source + step:
                add(0, "row", source, step, 0.0, share)
            else:
                add(0, "row", source, step, 0.0, 0.0)
    for sign in (-1, 1):
        for d in DILATIONS:
            for r in range(tall):
                add(0, "strip", r, sign * d)
    for d in DILATIONS:
        for a in range(3):
            for r in range(reach_rows):
                add(0, "group", r - (a - 1) * d, (a - 1) * d)
    for r in range(tall):
        for m in range(8):
            add(0, "strip", r, 0, crop=m)
    for r in range(reach_rows):
        for m in range(8):
            add(0, "group", r, 0, crop=m)
    return np.array(rows, np.float32).T


class Entries:
    def __init__(self, ref, name):
        self.ref = ref
        self.start, _, self.columns = LAYOUT[name]

    def __getitem__(self, index):
        if isinstance(index, tuple):
            return self.ref[self.start + index[0] * self.columns + index[1]]
        return self.ref[self.start + index]


def whole_block(shape):
    return pl.BlockSpec(shape, lambda i: (0,) * len(shape), pipeline_mode=pl.Buffered(1))


class Lanes:
    def __init__(self, array, width, index):
        self.array, self.shape, self.index = array, (array.shape[0], width), index

    def spec(self):
        return pl.BlockSpec(self.shape, lambda i: (0, self.index), pipeline_mode=pl.Buffered(1))


def run_kernel(body, scalars, arrays, outs, scratch=(), limit=56):
    specs = [a.spec() if isinstance(a, Lanes) else whole_block(a.shape) for a in arrays]
    arrays = [a.array if isinstance(a, Lanes) else a for a in arrays]
    return pl.pallas_call(
        body,
        grid=(1,),
        out_shape=[jax.ShapeDtypeStruct(shape, kind) for shape, kind in outs],
        in_specs=[pl.BlockSpec(memory_space=SMEM)] * len(scalars)
        + specs,
        out_specs=[whole_block(shape) for shape, _ in outs],
        scratch_shapes=[VMEM(shape, kind) for shape, kind in scratch],
        compiler_params=pltpu.CompilerParams(vmem_limit_bytes=limit * 2**20),
    )(*scalars, *arrays)


def tap_rows(values, step):
    if step == 0:
        return values
    extent = values.shape[0]
    ids = lax.broadcasted_iota(jnp.int32, values.shape, 0)
    moved = pltpu.roll(values, (-step) % extent, 0)
    return jnp.where((ids + step >= 0) & (ids + step < extent), moved, 0.0)


def column_sum(values):
    return jnp.sum(values, axis=0, keepdims=True)


def norm_of(total, count):
    mean = total[0:1] / count
    return mean, lax.rsqrt(total[1:2] / count - jnp.square(mean) + EPSILON)


def silu(pre):
    return pre * jax.nn.sigmoid(pre)


def slot_mask(shape, slot):
    lanes = lax.broadcasted_iota(jnp.int32, shape, len(shape) - 1)
    return (lanes >= 32 * slot) & (lanes < 32 * slot + 32)


def lane_roll(values, shift):
    shift = shift % 128
    return values if shift == 0 else pltpu.roll(values, shift, values.ndim - 1)


def product_kernel(
    place, mine_ref, theirs_ref, w_ref, pad_ref, a0_ref, a1_ref, a2_ref, p1, p2, p3, m1, m2, m3, acc
):
    n_y, rows, depth = mine_ref.shape
    block, n_x = 64, 4

    @pl.loop(0, w_ref.shape[0] // (block * n_x))
    def _(z):
        for hops in range(n_x):
            owner = lax.rem(place[0] - hops + n_x, n_x)
            source = pl.ds(pl.multiple_of((z * n_x + hops) * block, block), block)
            target = pl.ds(pl.multiple_of((z * n_x + owner) * block, block), block)
            for g in range(9):
                pad_ref[target, 128 * g : 128 * g + 96] = w_ref[source, 96 * g : 96 * g + 96]
                at = {1: 864, 4: 896}.get(g)
                if at is None:
                    pad_ref[target, 128 * g + 96 : 128 * g + 128] = jnp.zeros((block, 32), BF)
                else:
                    pad_ref[target, 128 * g + 96 : 128 * g + 128] = w_ref[source, at : at + 32]

    acc[...] = jnp.zeros_like(acc)

    @pl.loop(0, n_y)
    def _(i):
        owner = lax.rem(place[1] - i + n_y, n_y)
        deep = pl.ds(pl.multiple_of(owner * depth, depth), depth)
        own_rows = pl.ds(pl.multiple_of(place[2] * rows, rows), rows)
        other_rows = pl.ds(pl.multiple_of((1 - place[2]) * rows, rows), rows)
        acc[own_rows, :] += mm(mine_ref[i], pad_ref[deep, :])
        acc[other_rows, :] += mm(theirs_ref[i], pad_ref[deep, :])

    outs = (a0_ref, a1_ref, a2_ref)
    shape = a0_ref.shape
    columns = lax.broadcasted_iota(jnp.int32, shape, 1)
    for k, d in enumerate(DILATIONS):
        left, own, right = (
            acc[:, 128 * (3 * k + j) : 128 * (3 * k + j) + 128].reshape(shape) for j in range(3)
        )
        outs[k][...] = (
            own
            + jnp.where(columns >= d, pltpu.roll(left, d, 1), 0.0)
            + jnp.where(columns < shape[1] - d, pltpu.roll(right, shape[1] - d, 1), 0.0)
        )
    masks = [slot_mask(shape[1:], slot) for slot in range(4)]

    def pack(ref, pieces, lane):
        for block in range(ref.shape[0]):
            value = jnp.zeros(shape[1:], F32)
            for slot, (source, r) in enumerate(pieces[4 * block : 4 * block + 4]):
                value = jnp.where(masks[slot], lane_roll(source[r], 32 * (slot - lane)), value)
            ref[block] = value.astype(BF)

    pack(p1, [(a0_ref, r) for r in range(6)] + [(a1_ref, r) for r in range(4, 8)], 2)
    pack(p2, [(a1_ref, r) for r in range(4)] + [(a2_ref, r) for r in range(2, 8)], 2)
    pack(p3, [(a2_ref, r) for r in range(2)], 2)
    pack(m1, [(a0_ref, r) for r in range(2, 8)] + [(a1_ref, r) for r in range(4)], 0)
    pack(m2, [(a1_ref, r) for r in range(4, 8)] + [(a2_ref, r) for r in range(6)], 0)
    pack(m3, [(a2_ref, r) for r in range(6, 8)], 0)


def spatial_kernel(
    table, a0, a1, a2, p1, p2, p3, m1, m2, m3, out_ref, payload_ref
):
    up, down, member = (Entries(table, name) for name in ("up", "down", "member"))
    own = (a0, a1, a2)
    shape = out_ref.shape[1:]
    masks = [slot_mask(shape, slot) for slot in range(4)]

    def piece(ref, i, k):
        return lane_roll(ref[i // 4].astype(F32), 32 * (k + 1 - i % 4))

    def plus_of(k, r):
        if k == 0:
            return lane_roll(a0[6 + r], -32) if r < 2 else piece(p1, r - 2, k)
        if k == 1:
            return piece(p1, 6 + r, k) if r < 4 else piece(p2, r - 4, k)
        return piece(p2, 4 + r, k) if r < 6 else piece(p3, r - 6, k)

    def minus_of(k, r):
        if k == 0:
            return piece(m1, r, k) if r < 6 else lane_roll(a0[r - 6], 32)
        if k == 1:
            return piece(m2, r, k) if r < 4 else piece(m1, 2 + r, k)
        return piece(m3, r, k) if r < 2 else piece(m2, 2 + r, k)

    sums = jnp.zeros((1, 128), F32)
    squares = jnp.zeros((1, 128), F32)
    pools = []
    for r in range(out_ref.shape[0]):
        total = jnp.where(masks[0], lane_roll(a0[r], 32), 0.0)
        for k in range(3):
            term = (
                lane_roll(own[k][r], 32 * k)
                + up[k, r] * minus_of(k, r)
                + down[k, r] * plus_of(k, r)
            )
            total = jnp.where(masks[k + 1], term, total)
        out_ref[r] = total
        sums = sums + column_sum(total)
        squares = squares + column_sum(total * total)
        pools.append(lane_roll(column_sum(a1[r]), 32))
    first = slot_mask((1, 128), 0)
    packed = [jnp.zeros((1, 128), F32), jnp.zeros((1, 128), F32)]
    for m in range(8):
        part = sum(member[r, m] * pools[r] for r in range(len(pools)))
        packed[m // 4] = packed[m // 4] + lane_roll(jnp.where(first, part, 0.0), 32 * (m % 4))
    payload = jnp.concatenate([sums, squares] + packed, axis=0)
    payload_ref[...] = jnp.broadcast_to(payload[None], payload_ref.shape)


def pool_rows_of(total, slot_rows):
    first = slot_mask((1, 128), 0)
    rows = []
    for m in range(8):
        row = total[slot_rows + m // 4 : slot_rows + m // 4 + 1]
        rows.append(jnp.where(first, lane_roll(row, -32 * (m % 4)), 0.0))
    return rows


def pool_norm(total, counts, gains):
    rows = pool_rows_of(total, 2)
    z = jnp.concatenate([rows[m] / counts[m] for m in range(8)], axis=0)
    mean = jnp.mean(z, axis=0, keepdims=True)
    inverse = lax.rsqrt(jnp.mean(jnp.square(z - mean), axis=0, keepdims=True) + EPSILON)
    normed = (z - mean) * inverse
    return normed, inverse, normed * gains[2:3] + gains[3:4]


def act_kernel(pixels, table, spatial_ref, landed_ref, gains_ref, out_ref):
    counts, member = Entries(table, "counts"), Entries(table, "member")
    total = jnp.sum(landed_ref[...], axis=0)
    gains = gains_ref[...]
    mean, inverse = norm_of(total, pixels)
    _, _, pre = pool_norm(total, counts, gains)
    act = silu(pre)
    columns = spatial_ref.shape[1]
    first_row = lax.broadcasted_iota(jnp.int32, (16, 128), 0) == 0
    for r in range(spatial_ref.shape[0]):
        normed = (spatial_ref[r] - mean) * inverse
        out_ref[r, 0:columns] = silu(normed * gains[0:1] + gains[1:2]).astype(BF)
        row = sum(member[r, m] * act[m : m + 1] for m in range(8))
        row = jnp.where(slot_mask((1, 128), 0), row, 0.0)
        out_ref[r, columns : columns + 16] = jnp.where(first_row, row, 0.0).astype(BF)


def proj_kernel(landed_ref, main_ref, pool_ref, low_ref, out_ref, payload_ref):
    columns = out_ref.shape[0]
    acc = jnp.zeros(out_ref.shape, F32)
    extra = jnp.zeros((16, out_ref.shape[1]), F32)
    for s in range(landed_ref.shape[0]):
        acc = acc + mm(landed_ref[s, 0:columns], main_ref[s])
        extra = extra + mm(landed_ref[s, columns : columns + 16], pool_ref[s])
    z = acc + extra[0:1]
    out_ref[...] = z
    payload = jnp.concatenate([column_sum(z), column_sum(z * z), low_ref[...]], axis=0)
    payload_ref[...] = jnp.broadcast_to(payload[None], payload_ref.shape)


def sum_kernel(landed_ref, out_ref):
    total = jnp.sum(landed_ref[...], axis=0)
    out_ref[...] = jnp.broadcast_to(total[None], out_ref.shape)


def half_lanes(value, index):
    return lane_roll(value, -64 * index)[:, 0:64]


def pieces_kernel(landed_ref, refine_ref, unite_ref, proj_ref, shrink_ref, rest_ref):
    total = landed_ref[0].astype(F32)
    for i in range(1, landed_ref.shape[0]):
        total = total + landed_ref[i].astype(F32)
    for ref, start in ((refine_ref, 0), (unite_ref, 20)):
        for t in range(9):
            for c in range(4):
                row = start + 5 * c + t // 2
                ref[t, c : c + 1] = half_lanes(total[row : row + 1], t % 2)
    rest_ref[...] = total[40:45].astype(BF)
    for i in range(proj_ref.shape[0]):
        row = 45 + i // 2
        proj_ref[i : i + 1] = half_lanes(total[row : row + 1], i % 2)
    shrink_ref[...] = total[55:56]


def landed_kernel(place, landed_ref, mine_ref, theirs_ref, low_ref, classes_ref):
    block = landed_ref.shape[1] - 8
    total = landed_ref[0, 0:block].astype(F32)
    for z in range(1, landed_ref.shape[0]):
        total = total + landed_ref[z, 0:block].astype(F32)
    first, second = total[0 : block // 2], total[block // 2 :]
    zero = place[2] == 0
    mine_ref[...] = jnp.where(zero, first, second)
    theirs_ref[...] = jnp.where(zero, second, first).astype(BF)
    rows = low_ref.shape[1] // 8
    for t in range(9):
        at = 128 * (t // 2)
        for z in range(rows):
            part = landed_ref[z, block : block + 8, at : at + 128].astype(F32)
            low_ref[t, 8 * z : 8 * z + 8] = half_lanes(part, t % 2)
    tail = landed_ref[rows, block : block + 8, 0:640].astype(F32)
    for i in range(classes_ref.shape[0]):
        at = 128 * (i % 10 // 2)
        part = tail[i // 10 : i // 10 + 1, at : at + 128]
        classes_ref[i : i + 1] = half_lanes(part, i % 2)


def joined_kernel(place, mine_ref, theirs_ref, atrous_ref, one_ref, pool_ref):
    zero = place[2] == 0
    lanes = lax.broadcasted_iota(jnp.int32, (mine_ref.shape[0], 128), 1)
    for g in range(8):
        mine = mine_ref[:, 128 * g : 128 * g + 128]
        theirs = theirs_ref[:, 128 * g : 128 * g + 128].astype(F32)
        first, second = jnp.where(zero, mine, theirs), jnp.where(zero, theirs, mine)
        for a in range(4):
            pair = jnp.where(lanes < 32, lane_roll(first, -32 * a), lane_roll(second, 32 - 32 * a))
            if a < 3:
                atrous_ref[g // 3, a, g % 3] = pair[:, 0:64]
            elif g in SPARE:
                atrous_ref[2, SPARE.index(g), 2] = pair[:, 0:64]
            elif g == 1:
                one_ref[...] = pair[:, 0:64]
            elif g == 4:
                pool_ref[...] = pair[:, 0:64]


def low_weight_kernel(raw_ref, out_ref):
    out_ref[...] = jnp.zeros_like(out_ref)
    rows = raw_ref.shape[2]
    first = lax.broadcasted_iota(jnp.int32, (rows, 128), 1) < 64
    for t in range(9):
        a, b = t // 3, t % 3
        for j in range(2):
            left = raw_ref[2 * j, t // 2].astype(F32)
            right = raw_ref[2 * j + 1, t // 2].astype(F32)
            if t % 2 == 0:
                right = pltpu.roll(right, 64, 1)
            else:
                left = pltpu.roll(left, 64, 1)
            value = jnp.where(first, left, right).astype(BF)
            out_ref[a, 64 * b : 64 * b + rows, 128 * j : 128 * j + 128] = value


def shared_weight_kernel(low_part, dec_ref, main_ref, pool_ref, shrink_ref, rows_ref):
    height = dec_ref.shape[0]
    n_s = main_ref.shape[0]
    for q in range(5):
        for j in range(2):
            at = 256 * q + 128 * j
            rows_ref[j, pl.ds(q, height, stride=5), :] = dec_ref[:, at : at + 128].astype(F32)
    for s in range(n_s):
        place = 64 * (s % (n_s // 2)) + 32 * (s // (n_s // 2))
        for branch in range(4):
            at = 256 * branch + place
            for j in range(2):
                main_ref[s, 32 * branch : 32 * branch + 32, 128 * j : 128 * j + 128] = rows_ref[
                    j, at : at + 32
                ].astype(BF)
        at = 1024 + place
        for j in range(2):
            pool_ref[s, 0:32, 128 * j : 128 * j + 128] = rows_ref[j, at : at + 32].astype(BF)
        pool_ref[s, 32:128] = jnp.zeros((96, 256), BF)
    lanes = lax.broadcasted_iota(jnp.int32, (height, 128), 1)
    value = jnp.zeros((height, 128), F32)
    for y in range(4):
        at = 256 * 5 + 128 * (y // 2)
        moved = lane_roll(dec_ref[:, at : at + 128].astype(F32), low_part * y - 64 * (y % 2))
        value = jnp.where((lanes >= low_part * y) & (lanes < low_part * (y + 1)), moved, value)
    shrink_ref[...] = value.astype(BF)


def unite_kernel(
    counts,
    table,
    own_ref,
    above_ref,
    below_ref,
    landed_ref,
    gain_ref,
    low_all_ref,
    low_gain_ref,
    columns_ref,
    up_w_ref,
    low_w_ref,
    z_ref,
    up_ref,
    act_ref,
    payload_ref,
    moments_ref,
    taps_ref,
    low_taps_ref,
    coarse_ref,
):
    blend, keep, inside = (Entries(table, name) for name in ("blend", "keep", "inside"))
    total = jnp.sum(landed_ref[...], axis=0)
    mean, inverse = norm_of(total, counts[0])
    mean_l, inverse_l = norm_of(total[2:4, 0:128], counts[1])
    moments_ref[0:1] = mean
    moments_ref[1:2] = inverse
    moments_ref[2:3] = total[2:3] / counts[1]
    moments_ref[3:4] = lax.rsqrt(
        total[3:4] / counts[1] - jnp.square(total[2:3] / counts[1]) + EPSILON
    )
    gain = gain_ref[...]
    low_gain = low_gain_ref[...]
    for k, ref in enumerate((above_ref, own_ref, below_ref)):
        pre = (ref[...] - mean) * inverse * gain[0:1] + gain[1:2]
        coarse_ref[k] = silu(pre).astype(BF).astype(F32)
    width = z_ref.shape[1]

    @pl.loop(0, 8)
    def _(f):
        row = (
            blend[f, 0] * coarse_ref[0] + blend[f, 1] * coarse_ref[1] + blend[f, 2] * coarse_ref[2]
        )
        high = row.astype(BF)
        rest = (row - high.astype(F32)).astype(BF)
        grown = mm(columns_ref[...], jnp.concatenate([high, rest], axis=0)) * inside[f]
        taps_ref[f] = grown.astype(BF)
        pre = (low_all_ref[f] - mean_l) * inverse_l * low_gain[0:1] + low_gain[1:2]
        act = silu(pre).astype(BF).astype(F32) * inside[f]
        pair = tap_rows(act, -1) + pltpu.roll(act, 64, 1)
        low_taps_ref[f] = jnp.concatenate([pair, tap_rows(act, 1)], axis=1).astype(BF)

        @pl.when((f >= 1) & (f <= 6))
        def _():
            up_ref[f - 1] = grown[width : 2 * width].astype(BF)
            act_ref[f - 1] = act.astype(BF)

    payload_ref[...] = jnp.zeros_like(payload_ref)

    @pl.loop(0, 6)
    def _(f):
        acc = jnp.zeros(z_ref.shape[1:], F32)
        for a in range(3):
            part = mm(low_taps_ref[f + a], low_w_ref[a])
            for b in range(3):
                t = 3 * a + b
                part = part + mm(
                    taps_ref[f + a, b * width : (b + 1) * width, :],
                    up_w_ref[:, 256 * t : 256 * t + 256],
                )
            acc = acc + keep[f, a] * part
        z_ref[f] = acc

        @pl.when((f >= 1) & (f <= 4))
        def _():
            both = jnp.concatenate([column_sum(acc), column_sum(acc * acc)], axis=0)
            payload_ref[...] += jnp.broadcast_to(both[None], payload_ref.shape)


def refine_kernel(
    counts,
    table,
    z_in_ref,
    landed_ref,
    gain_ref,
    w_ref,
    hidden_ref,
    z_ref,
    payload_ref,
    moments_ref,
    taps_ref,
):
    keep, inside = Entries(table, "keep"), Entries(table, "inside")
    total = jnp.sum(landed_ref[...], axis=0)
    mean, inverse = norm_of(total, counts[1])
    moments_ref[0:1] = mean
    moments_ref[1:2] = inverse
    gain = gain_ref[...]
    width = z_ref.shape[1]

    @pl.loop(0, 6)
    def _(f):
        pre = (z_in_ref[f] - mean) * inverse * gain[0:1] + gain[1:2]
        hidden = silu(pre).astype(BF).astype(F32) * inside[f + 1]
        hidden_ref[f] = hidden.astype(BF)
        for b in range(3):
            taps_ref[f, b * width : (b + 1) * width, :] = tap_rows(hidden, b - 1).astype(BF)

    payload_ref[...] = jnp.zeros_like(payload_ref)

    @pl.loop(0, 4)
    def _(f):
        acc = jnp.zeros(z_ref.shape[1:], F32)
        for a in range(3):
            part = None
            for b in range(3):
                t = 3 * a + b
                term = mm(
                    taps_ref[f + a, b * width : (b + 1) * width, :],
                    w_ref[:, 256 * t : 256 * t + 256],
                )
                part = term if part is None else part + term
            acc = acc + keep[f + 1, a] * part
        z_ref[f] = acc
        both = jnp.concatenate([column_sum(acc), column_sum(acc * acc)], axis=0)
        payload_ref[...] += jnp.broadcast_to(both[None], payload_ref.shape)


def classes_kernel(
    images,
    classes,
    counts,
    table,
    z_ref,
    landed_ref,
    gain_ref,
    labels_ref,
    w_ref,
    gp_ref,
    payload_ref,
    moments_ref,
    top_ref,
    bottom_ref,
    block_ref,
    part_ref,
):
    entries = Entries(table, "bias")
    total = jnp.sum(landed_ref[...], axis=0)
    mean, inverse = norm_of(total, counts[1])
    moments_ref[0:1] = mean
    moments_ref[1:2] = inverse
    gain = gain_ref[...]
    weight = w_ref[...]
    width = z_ref.shape[1]
    shape = (weight.shape[0], width)
    ids = lax.broadcasted_iota(jnp.int32, shape, 0)
    ones = jnp.ones((8, width), BF)
    bias = jnp.zeros(shape, F32)
    for i in range(classes):
        bias = jnp.where(ids == i, entries[i], bias)
    rows = [jnp.zeros((1, 256), F32) for _ in range(4)]
    part_ref[...] = jnp.zeros_like(part_ref)
    for f in range(4):
        normed = (z_ref[f] - mean) * inverse
        pre = normed * gain[0:1] + gain[1:2]
        gate = jax.nn.sigmoid(pre)
        refined = (pre * gate).astype(BF)
        logits = mm_nt(weight, refined) + bias
        valid = ids < classes
        logits = jnp.where(valid, logits, -1e30)
        highest = jnp.max(logits, axis=0, keepdims=True)
        exponent = jnp.exp(logits - highest)
        exp_total = jnp.sum(exponent, axis=0, keepdims=True)
        one_hot = ids == labels_ref[f : f + 1, :]
        picked = jnp.sum(jnp.where(one_hot, logits, 0.0), axis=0, keepdims=True)
        rows[3] = rows[3] + jnp.log(exp_total) + highest - picked
        share = exponent / exp_total - jnp.where(one_hot, 1.0, 0.0)
        grad = jnp.where(valid, share / images, 0.0).astype(BF)
        part_ref[...] += mm(grad, refined)
        counted = mm_nt(ones, grad)[0:1]
        rows[2] = rows[2] + jnp.concatenate(
            [counted, jnp.zeros((1, 256 - shape[0]), F32)], axis=1
        )
        gp = mm_tn(grad, weight) * (gate * (1.0 + pre * (1.0 - gate)))
        gp_ref[f] = gp
        rows[0] = rows[0] + column_sum(gp * normed)
        rows[1] = rows[1] + column_sum(gp)
        if f == 0:
            bottom_ref[0] = gp.astype(BF)
            bottom_ref[1] = normed.astype(BF)
        if f == 3:
            top_ref[0] = gp.astype(BF)
            top_ref[1] = normed.astype(BF)
    payload = jnp.concatenate(rows, axis=0)
    payload_ref[...] = jnp.broadcast_to(payload[None], payload_ref.shape)
    block_ref[...] = jnp.zeros_like(block_ref)
    first = lax.broadcasted_iota(jnp.int32, (1, 128), 1) < 64
    for i in range(0, classes, 2):
        for j in range(2):
            one, two = (part_ref[i + n : i + n + 1, 128 * j : 128 * j + 128] for n in range(2))
            at = 128 * (i % 10 // 2)
            for n, value in enumerate(
                (
                    jnp.where(first, one, pltpu.roll(two, 64, 1)),
                    jnp.where(first, pltpu.roll(one, 64, 1), two),
                )
            ):
                block_ref[2 * j + n, i // 10 : i // 10 + 1, at : at + 128] = value


def grad_z(gp, normed, scale, total, count):
    return (scale * (gp - (total[1:2] + normed * total[0:1]) / count)).astype(BF)


def store_taps(ref, f, values):
    width = values.shape[0]
    wide = values.astype(F32)
    for b in range(3):
        ref[f, b * width : (b + 1) * width, :] = tap_rows(wide, 1 - b).astype(BF)


def refine_back_kernel(
    counts,
    table,
    gp_ref,
    z_ref,
    above_ref,
    below_ref,
    landed_ref,
    moments_ref,
    gain_ref,
    w_ref,
    z1_ref,
    moments1_ref,
    gain1_ref,
    out_ref,
    taps_ref,
    payload_ref,
    top_ref,
    bottom_ref,
    total_ref,
    ends_ref,
):
    keep, inside = Entries(table, "keep_back"), Entries(table, "inside")
    total = jnp.sum(landed_ref[...], axis=0)
    total_ref[...] = total
    mean, inverse = moments_ref[0:1], moments_ref[1:2]
    scale = gain_ref[0:1] * inverse
    count = counts[1]
    for ref, at, f in ((above_ref, 0, 0), (below_ref, 1, 5)):
        edge = grad_z(ref[0].astype(F32), ref[1].astype(F32), scale, total, count)
        store_taps(ends_ref, at, edge.astype(F32) * inside[f + 1])

    @pl.loop(0, 4)
    def _(f):
        normed = (z_ref[f] - mean) * inverse
        store_taps(taps_ref, f, grad_z(gp_ref[f], normed, scale, total, count))

    width = out_ref.shape[1]
    mean1, inverse1 = moments1_ref[0:1], moments1_ref[1:2]
    gain1 = gain1_ref[...]
    payload_ref[...] = jnp.zeros_like(payload_ref)
    for g in range(4):
        acc = jnp.zeros(out_ref.shape[1:], F32)
        for a in range(3):
            source = g + 1 - a
            if source < 0:
                rows = ends_ref.at[0]
            elif source > 3:
                rows = ends_ref.at[1]
            else:
                rows = taps_ref.at[source]
            part = None
            for b in range(3):
                t = 3 * a + b
                term = mm_nt(
                    rows[b * width : (b + 1) * width, :], w_ref[:, 256 * t : 256 * t + 256]
                )
                part = term if part is None else part + term
            acc = acc + keep[g, a] * part
        normed = (z1_ref[g + 1] - mean1) * inverse1
        pre = normed * gain1[0:1] + gain1[1:2]
        gate = jax.nn.sigmoid(pre)
        gp = acc * (gate * (1.0 + pre * (1.0 - gate)))
        out_ref[g] = gp
        both = jnp.concatenate([column_sum(gp * normed), column_sum(gp)], axis=0)
        payload_ref[...] += jnp.broadcast_to(both[None], payload_ref.shape)
        if g == 0:
            bottom_ref[...] = gp.astype(BF)
        if g == 3:
            top_ref[...] = gp.astype(BF)


def unite_back_kernel(
    counts,
    table,
    gp_ref,
    z_ref,
    above_ref,
    below_ref,
    landed_ref,
    moments_ref,
    gain_ref,
    up_w_ref,
    low_w_ref,
    columns_ref,
    low_z_ref,
    moments0_ref,
    low_gain_ref,
    taps_ref,
    rows_ref,
    low_gp_ref,
    sums_ref,
    total_ref,
    ends_ref,
    flat_ref,
):
    keep, inside, blend = (Entries(table, name) for name in ("keep_back", "inside", "blend"))
    total = jnp.sum(landed_ref[...], axis=0)
    total_ref[...] = total
    mean, inverse = moments_ref[0:1], moments_ref[1:2]
    scale = gain_ref[0:1] * inverse
    count = counts[1]
    for ref, at, f in ((above_ref, 0, 0), (below_ref, 1, 5)):
        normed = (z_ref[f] - mean) * inverse
        edge = grad_z(ref[...].astype(F32), normed, scale, total, count)
        edge = edge.astype(F32) * inside[f + 1]
        store_taps(ends_ref, at, edge)
        flat_ref[5 * at] = edge.astype(BF)

    @pl.loop(0, 4)
    def _(f):
        normed = (z_ref[f + 1] - mean) * inverse
        edge = grad_z(gp_ref[f], normed, scale, total, count)
        store_taps(taps_ref, f, edge)
        flat_ref[f + 1] = edge

    width = gp_ref.shape[1]
    mean_l, inverse_l = moments0_ref[2:3, 0:128], moments0_ref[3:4, 0:128]
    low_gain = low_gain_ref[...]
    first = lax.broadcasted_iota(jnp.int32, (width, 128), 1) < 64
    rows_ref[...] = jnp.zeros_like(rows_ref)
    sums = [jnp.zeros((1, 128), F32), jnp.zeros((1, 128), F32)]
    for g in range(4):
        acc = jnp.zeros(gp_ref.shape[1:], F32)
        low = jnp.zeros((width, 256), F32)
        for a in range(3):
            source = g + 1 - a
            if source < 0:
                rows = ends_ref.at[0]
            elif source > 3:
                rows = ends_ref.at[1]
            else:
                rows = taps_ref.at[source]
            part = None
            for b in range(3):
                t = 3 * a + b
                term = mm_nt(
                    rows[b * width : (b + 1) * width, :], up_w_ref[:, 256 * t : 256 * t + 256]
                )
                part = term if part is None else part + term
            acc = acc + keep[g, a] * part
            low = low + keep[g, a] * mm_nt(flat_ref[source + 1], low_w_ref[a])
        pair, last = low[:, 0:128], low[:, 128:256]
        low_in = (
            tap_rows(jnp.where(first, pair, 0.0), 1)
            + jnp.where(first, pltpu.roll(pair, 64, 1), 0.0)
            + tap_rows(last, -1)
        )
        grown = mm(columns_ref[...], acc.astype(BF))
        for k in range(3):
            rows_ref[k] += blend[g + 2, k] * grown
        normed = (low_z_ref[g + 2] - mean_l) * inverse_l
        pre = normed * low_gain[0:1] + low_gain[1:2]
        gate = jax.nn.sigmoid(pre)
        gp = low_in * (gate * (1.0 + pre * (1.0 - gate)))
        low_gp_ref[g] = gp
        sums[0] = sums[0] + column_sum(gp * normed)
        sums[1] = sums[1] + column_sum(gp)
    both = jnp.concatenate(sums, axis=0)
    sums_ref[...] = jnp.concatenate([both, jnp.zeros_like(both)], axis=1)


def tap_gradients(keep, h_ref, taps_ref, store):
    width = taps_ref.shape[1] // 3
    channels = h_ref.shape[2]
    first = lax.broadcasted_iota(jnp.int32, (channels, 128), 1) < 64
    other = None
    for t in range(9):
        a, b = t // 3, t % 3
        acc = jnp.zeros((channels, 256), F32)
        for f in range(4):
            acc = acc + keep[f + 1, a] * mm_tn(
                h_ref[f + a], taps_ref[f, b * width : (b + 1) * width, :]
            )
        if t % 2 == 0 and t < 8:
            other = acc
            continue
        x, y = (other, acc) if t % 2 == 1 else (acc, jnp.zeros_like(acc))
        for j in range(2):
            left, right = x[:, 128 * j : 128 * j + 128], y[:, 128 * j : 128 * j + 128]
            store(2 * j, 128 * (t // 2), jnp.where(first, left, pltpu.roll(right, 64, 1)))
            store(2 * j + 1, 128 * (t // 2), jnp.where(first, pltpu.roll(left, 64, 1), right))


def store_rows(out_ref, rows_ref):
    height = out_ref.shape[1]

    def store(y, at, value):
        rows_ref[...] = value
        for i in range(4):
            out_ref[y, :, 640 * i + at : 640 * i + at + 128] = rows_ref[
                pl.ds(i, height, stride=4), :
            ].astype(BF)

    return store


def refine_weight_kernel(table, h_ref, taps_ref, out_ref, rows_ref):
    tap_gradients(Entries(table, "keep"), h_ref, taps_ref, store_rows(out_ref, rows_ref))


def unite_weight_kernel(table, h_ref, act_ref, taps_ref, classes_ref, out_ref, rows_ref):
    keep = Entries(table, "keep")
    tap_gradients(keep, h_ref, taps_ref, store_rows(out_ref, rows_ref))

    def store_low(y, at, value):
        out_ref[y, 0:48, 2560 + at : 2560 + at + 128] = value[0:48].astype(BF)

    tap_gradients(keep, act_ref, taps_ref, store_low)
    out_ref[:, 48:64, 2560:3200] = classes_ref[...].astype(BF)


def low_back_kernel(count, gp_ref, z_ref, total_ref, moments_ref, gain_ref, low_ref, out_ref, part_ref):
    mean, inverse = moments_ref[2:3, 0:128], moments_ref[3:4, 0:128]
    total = total_ref[2:4, 0:128]
    scale = gain_ref[0:1] * inverse
    used = out_ref.shape[1]
    part = jnp.zeros(part_ref.shape, F32)
    for f in range(out_ref.shape[0]):
        normed = (z_ref[f + 2] - mean) * inverse
        grad = grad_z(gp_ref[f], normed, scale, total, count).astype(F32)
        turned = jnp.transpose(grad)[0:used].astype(BF)
        out_ref[f] = turned
        part = part + mm_nt(turned, low_ref[f + 2])
    part_ref[...] = part


def proj_back_sums_kernel(own_ref, above_ref, below_ref, z_ref, moments_ref, gain_ref, low_ref, gp_ref, payload_ref):
    normed = (z_ref[...] - moments_ref[0:1]) * moments_ref[1:2]
    pre = normed * gain_ref[0:1] + gain_ref[1:2]
    gate = jax.nn.sigmoid(pre)
    grad = own_ref[...] + above_ref[...] + below_ref[...]
    gp = grad * (gate * (1.0 + pre * (1.0 - gate)))
    gp_ref[...] = gp
    payload = jnp.concatenate([column_sum(gp * normed), column_sum(gp), low_ref[...]], axis=0)
    payload_ref[...] = jnp.broadcast_to(payload[None], payload_ref.shape)


def proj_back_kernel(
    counts,
    gp_ref,
    z_ref,
    landed_sums_ref,
    moments_ref,
    gain_ref,
    landed_ref,
    main_ref,
    pool_ref,
    out_ref,
    weight_ref,
    total_ref,
    rows_ref,
):
    total = jnp.sum(landed_sums_ref[...], axis=0)
    total_ref[...] = total
    mean, inverse = moments_ref[0:1], moments_ref[1:2]
    normed = (z_ref[...] - mean) * inverse
    grad = grad_z(gp_ref[...], normed, gain_ref[0:1] * inverse, total, counts[0])
    columns = grad.shape[0]
    summed = column_sum(grad.astype(F32))
    high = summed.astype(BF).astype(F32)
    first = lax.broadcasted_iota(jnp.int32, (16, 256), 0) == 0
    high_rows = jnp.where(first, high, 0.0).astype(BF)
    low_rows = jnp.where(first, summed - high, 0.0).astype(BF)
    top = lax.broadcasted_iota(jnp.int32, (16, 128), 0)
    n_s = out_ref.shape[0]
    for s in range(n_s):
        out_ref[s, 0:columns] = mm_nt(grad, main_ref[s]).astype(BF)
        pool = mm_nt(high_rows, pool_ref[s]) + mm_nt(low_rows, pool_ref[s])
        pool_high = pool[0:1].astype(BF).astype(F32)
        pair = jnp.where(top == 0, pool_high, jnp.where(top == 1, pool[0:1] - pool_high, 0.0))
        out_ref[s, columns : columns + 16] = pair.astype(BF)
        place = 64 * (s % (n_s // 2)) + 32 * (s // (n_s // 2))
        main = mm_tn(landed_ref[s, 0:columns], grad)
        for branch in range(4):
            at = 256 * branch + place
            for j in range(2):
                rows_ref[j, at : at + 32] = main[
                    32 * branch : 32 * branch + 32, 128 * j : 128 * j + 128
                ]
        extra = landed_ref[s, columns : columns + 16]
        outer = mm_tn(extra, high_rows) + mm_tn(extra, low_rows)
        for j in range(2):
            rows_ref[j, 1024 + place : 1024 + place + 32] = outer[0:32, 128 * j : 128 * j + 128]
    half = rows_ref.shape[1] // 2
    left = lax.broadcasted_iota(jnp.int32, (half, 128), 1) < 64
    for j in range(2):
        even = rows_ref[j, pl.ds(0, half, stride=2), :]
        odd = rows_ref[j, pl.ds(1, half, stride=2), :]
        weight_ref[2 * j] = jnp.where(left, even, pltpu.roll(odd, 64, 1)).astype(BF)
        weight_ref[2 * j + 1] = jnp.where(left, pltpu.roll(even, 64, 1), odd).astype(BF)


def spatial_back_sums_kernel(
    pixels, table, back_ref, spatial_ref, landed_ref, gains_ref, gp_ref, payload_ref
):
    member = Entries(table, "member")
    total = jnp.sum(landed_ref[...], axis=0)
    gains = gains_ref[...]
    mean, inverse = norm_of(total, pixels)
    columns = spatial_ref.shape[1]
    rows = [jnp.zeros((1, 128), F32), jnp.zeros((1, 128), F32)]
    pools = []
    for r in range(spatial_ref.shape[0]):
        normed = (spatial_ref[r] - mean) * inverse
        pre = normed * gains[0:1] + gains[1:2]
        gate = jax.nn.sigmoid(pre)
        gp = back_ref[r, 0:columns].astype(F32) * (gate * (1.0 + pre * (1.0 - gate)))
        gp_ref[r] = gp
        rows[0] = rows[0] + column_sum(gp * normed)
        rows[1] = rows[1] + column_sum(gp)
        pools.append(column_sum(back_ref[r, columns : columns + 16].astype(F32)))
    first = slot_mask((1, 128), 0)
    packed = [jnp.zeros((1, 128), F32), jnp.zeros((1, 128), F32)]
    for m in range(8):
        part = sum(member[r, m] * pools[r] for r in range(len(pools)))
        packed[m // 4] = packed[m // 4] + lane_roll(jnp.where(first, part, 0.0), 32 * (m % 4))
    payload = jnp.concatenate(rows + packed, axis=0)
    payload_ref[...] = jnp.broadcast_to(payload[None], payload_ref.shape)


def spatial_back_kernel(
    pixels,
    table,
    gp_ref,
    spatial_ref,
    landed_ref,
    landed_back_ref,
    gains_ref,
    out_ref,
    pool_ref,
    gains_out_ref,
):
    counts = Entries(table, "counts")
    total = jnp.sum(landed_ref[...], axis=0)
    back = jnp.sum(landed_back_ref[...], axis=0)
    gains = gains_ref[...]
    mean, inverse = norm_of(total, pixels)
    scale = gains[0:1] * inverse
    for r in range(spatial_ref.shape[0]):
        normed = (spatial_ref[r] - mean) * inverse
        out_ref[r] = grad_z(gp_ref[r], normed, scale, back, pixels)
    normed, inverse_p, pre = pool_norm(total, counts, gains)
    gate = jax.nn.sigmoid(pre)
    gp = jnp.concatenate(pool_rows_of(back, 2), axis=0) * (gate * (1.0 + pre * (1.0 - gate)))
    gain_grad = column_sum(gp * normed)
    shift_grad = column_sum(gp)
    grad = gains[2:3] * inverse_p * (gp - (shift_grad + normed * gain_grad) / 8.0)
    pool_ref[...] = jnp.concatenate([grad[m : m + 1] / counts[m] for m in range(8)], axis=0)
    gains_out_ref[...] = jnp.concatenate([back[0:2], gain_grad, shift_grad], axis=0)


def spread_kernel(
    place,
    table,
    wide_ref,
    above_ref,
    below_ref,
    pool_ref,
    feats_ref,
    rest_ref,
    weight_ref,
    own_ref,
    spread_ref,
    reach_ref,
):
    keep, crowd = Entries(table, "group"), Entries(table, "crowd")
    height = wide_ref.shape[0]
    columns = wide_ref.shape[1]
    reach_ref[0:REACH] = above_ref[...]
    reach_ref[REACH : REACH + height] = wide_ref[...]
    reach_ref[REACH + height :] = below_ref[...]
    shape = (columns, 128)
    masks = [slot_mask(shape, slot) for slot in range(4)]
    ids = lax.broadcasted_iota(jnp.int32, shape, 0)

    @pl.loop(0, height)
    def _(r):
        own = reach_ref[REACH + r].astype(F32)
        start = pl.multiple_of(r * columns, columns)
        for k, d in enumerate(DILATIONS):
            mixed = jnp.zeros(shape, F32)
            for a in range(3):
                source = own if a == 1 else reach_ref[REACH + r - (a - 1) * d].astype(F32)
                moved = lane_roll(source, 32 * (a - k - 1)) * keep[3 * k + a, r]
                mixed = jnp.where(masks[a], moved, mixed)
            left = jnp.where(ids < columns - d, pltpu.roll(mixed, columns - d, 0), 0.0)
            right = jnp.where(ids >= d, pltpu.roll(mixed, d, 0), 0.0)
            if k == 0:
                mixed = jnp.where(masks[3], lane_roll(own, 96), mixed)
            if k == 1:
                window = sum(crowd[r, m] * pool_ref[m : m + 1] for m in range(8))
                window = lane_roll(window, 96)
                mixed = jnp.where(masks[3], window, mixed)
            for j, value in enumerate((left, mixed, right)):
                at = 128 * (3 * k + j)
                spread_ref[pl.ds(start, columns), at : at + 128] = value.astype(BF)

    n_y = feats_ref.shape[0] // 2
    block = feats_ref.shape[1] * 8 // height
    strip = 2 * block
    wide = feats_ref.shape[2]

    @pl.loop(0, n_y)
    def _(y):
        acc = jnp.zeros((wide, spread_ref.shape[1]), F32)
        for core in range(2):
            for x in range(spread_ref.shape[0] // strip):
                turn = lax.rem(place[0] - x + 4, 4)
                acc = acc + mm_tn(
                    feats_ref[core * n_y + y, pl.ds(pl.multiple_of(turn * block, block), block), :],
                    spread_ref[x * strip + core * block : x * strip + (core + 1) * block, :],
                )
        half = wide // 2
        last = acc[:, 1024:1152]
        fourth = slot_mask((wide, 128), 3)
        for g in range(8):
            piece = acc[:, 128 * g : 128 * g + 128]
            if g in SPARE:
                piece = jnp.where(fourth, lane_roll(last, 32 * (3 - SPARE.index(g))), piece)
            for i in range(2):
                weight_ref[2 * y + i, 0:half, 128 * g : 128 * g + 128] = piece[
                    half * i : half * (i + 1)
                ].astype(BF)

    rows, lanes = rest_ref.shape
    for z in range(weight_ref.shape[0]):
        weight_ref[z, 64 : 64 + rows, 0:lanes] = rest_ref[...]
        weight_ref[z, 64 : 64 + rows, lanes:] = jnp.zeros((rows, weight_ref.shape[2] - lanes), BF)

    own_ref[...] = spread_ref[pl.ds(pl.multiple_of(place[0] * strip, strip), strip), :]


def feature_kernel(place, spread_ref, w_ref, mine_ref, theirs_ref):
    n_y, block, depth = mine_ref.shape
    own = pl.multiple_of(place[2] * block, block)
    other = pl.multiple_of((1 - place[2]) * block, block)

    @pl.loop(0, n_y)
    def _(y):
        weight = w_ref[pl.ds(pl.multiple_of(y * depth, depth), depth), :]
        theirs_ref[y] = mm_nt(spread_ref[pl.ds(other, block), :], weight).astype(BF)
        mine_ref[y] = mm_nt(spread_ref[pl.ds(own, block), :], weight).astype(BF)


def feature_sum_kernel(place, mine_ref, theirs_ref, own_ref, sent_ref):
    n_y = mine_ref.shape[0]

    def total(y):
        return mine_ref[y].astype(F32) + theirs_ref[y].astype(F32)

    own_ref[...] = total(place[1])
    for step in range(1, n_y):
        sent_ref[step - 1] = total(lax.rem(place[1] + step, n_y)).astype(BF)


def on_device(
    features,
    low_level,
    labels,
    crop_rows,
    w_one,
    w_atrous,
    w_pool,
    w_proj,
    w_low,
    w_unite_up,
    w_unite_low,
    w_refine,
    w_classes,
    b_classes,
    gain_aspp,
    shift_aspp,
    gain_proj,
    shift_proj,
    gain_low,
    shift_low,
    gain_dec,
    shift_dec,
):
    n_y, n_z, n_x = lax.axis_size("y"), lax.axis_size("z"), lax.axis_size("x")
    core, yi, xi, zi = (lax.axis_index(a) for a in ("core", "y", "x", "z"))
    strip = lax.axis_index(STRIP)
    row = lax.axis_index(ALL)
    groups = lax.axis_size(ROWS)
    rows_in, columns, c_part = features.shape
    total_rows = rows_in * groups
    c_in = c_part * n_y
    fine_strip, c_low, fine_columns = low_level.shape
    fine_total = fine_strip * groups
    branch = w_proj.shape[1] * n_y
    o_part = w_one.shape[1]
    half = o_part // 2
    low_out = w_low.shape[1] * n_y
    classes = w_classes.shape[1]
    images = crop_rows.shape[0]
    pixels = float(total_rows * columns)
    fine_pixels = float(fine_total * fine_columns)
    tall = 2 * rows_in
    counts_static = (pixels, fine_pixels)

    atrous = w_atrous.transpose(0, 1, 3, 2, 4).reshape(w_one.shape[0], 27, o_part)
    own = jnp.concatenate([atrous, w_one[:, None], w_pool[:, None]], axis=1)
    paired = lax.all_to_all(own, "core", 2, 0, tiled=True)
    paired = paired.reshape(paired.shape[0], -1)
    first = jnp.concatenate([paired] + [hop(paired, "x", k) for k in range(1, n_x)])
    inputs = (
        features,
        low_level,
        w_proj,
        w_low,
        w_unite_up,
        w_unite_low,
        w_refine,
        w_classes,
        gain_proj,
        shift_proj,
        gain_low,
        shift_low,
        gain_dec,
        shift_dec,
    )
    first, inputs = lax.optimization_barrier((first, inputs))
    (
        features,
        low_level,
        w_proj,
        w_low,
        w_unite_up,
        w_unite_low,
        w_refine,
        w_classes,
        gain_proj,
        shift_proj,
        gain_low,
        shift_low,
        gain_dec,
        shift_dec,
    ) = inputs
    first = lax.all_gather(first, "z", axis=0, tiled=True)

    flat_feats = features.reshape(-1, c_part)
    feats = jnp.stack([flat_feats] + [hop(flat_feats, "y", k) for k in range(1, n_y)])
    feats_other = hop(feats, "core", 1)

    k_row = w_refine.shape[0]
    shard = jnp.concatenate(
        [
            w_unite_up.reshape(k_row, 9, o_part),
            w_refine.reshape(k_row, 9, o_part),
            w_proj.reshape(k_row, -1, o_part),
            jnp.pad(w_low, ((0, 0), (0, o_part - w_low.shape[1])))[:, None],
        ],
        axis=1,
    )
    low_raw = jnp.pad(w_unite_low.reshape(low_out, 9, o_part), ((0, 0), (0, 1), (0, 0)))
    low_raw = low_raw.reshape(low_out, 5, 2 * o_part).transpose(1, 0, 2)
    class_raw = jnp.pad(w_classes.T, ((0, 32 - classes), (0, 0)))
    lows = jnp.pad(jnp.stack([gain_low, shift_low]), ((0, 0), (0, o_part - gain_low.shape[0])))
    vectors = jnp.concatenate(
        [
            jnp.stack([gain_dec, shift_dec], axis=1).reshape(4, -1),
            jnp.stack([gain_proj, shift_proj]),
            lows,
        ]
    ).reshape(4, 128)
    parts = []
    for _ in range(3):
        part = lax.reduce_precision(vectors, 8, 7)
        parts.append(part.astype(BF))
        vectors = vectors - part
    sizes = [shard.size, low_raw.size, class_raw.size]
    sent = [shard, low_raw, class_raw, jnp.concatenate(parts)]
    sent = jnp.concatenate([block.reshape(-1, 128) for block in sent])
    sent = gathered(sent, "y").reshape(n_y, -1)
    shard = sent[:, : sizes[0]].reshape(n_y, k_row, 24, o_part)
    shard = shard.transpose(1, 2, 0, 3).reshape(k_row, -1)
    low_raw = sent[:, sizes[0] : sizes[0] + sizes[1]].reshape((n_y,) + low_raw.shape)
    triple = sent[:, sum(sizes) :].reshape(n_y, 3, 4, 128)
    classes_w = sent[:, sizes[0] + sizes[1] : sum(sizes)].reshape(n_y, 32, o_part)
    classes_w = classes_w.transpose(1, 0, 2).reshape(32, branch)
    shard = gathered(gathered(shard, "core"), "x").reshape(-1, shard.shape[1])
    strips = [(r * n_y, (r + 1) * n_y) for r in range(groups - 1)]
    route = strips + [(target + n_y - 1, source + n_y - 1) for source, target in strips]
    edge = jnp.where(yi == 0, low_level[-2:], low_level[:2])
    edge = lax.ppermute(edge, ALL, route)
    low_rows = jnp.concatenate([edge, low_level, edge], axis=0)
    low_rows = lax.dynamic_slice_in_dim(low_rows, yi * 4, 8, 0)
    labels_own = lax.dynamic_slice_in_dim(labels, yi * 4, 4, 0)

    place = jnp.stack([xi, yi, core]).astype(jnp.int32)
    wide_c = 4 * half
    edge10, edge2 = ((3, columns, wide_c), BF), ((1, columns, wide_c), BF)
    part = ((tall, columns, wide_c), F32)
    later = (triple, crop_rows, b_classes, gain_aspp, shift_aspp)
    later, shard = lax.optimization_barrier((later, shard))
    triple, crop_rows, b_classes, gain_aspp, shift_aspp = later
    ends, reached = [], jnp.int32(0)
    for m in range(images):
        reached = reached + crop_rows[m]
        ends.append(reached)
    fine, by_row, by_strip, by_group, at, offset, base, slope, crop = pair_entries(tall, n_x * tall)
    fine, by_row, by_strip, by_group, at, offset, crop = (
        v.astype(np.int32) for v in (fine, by_row, by_strip, by_group, at, offset, crop)
    )
    scale = 1 + 3 * fine
    first_id = by_row * (scale * row) + by_strip * (tall * strip) + by_group * (n_x * tall * zi) + at
    second_id = first_id + offset
    extent = scale * total_rows

    def image(ids):
        return sum((ids >= scale * end).astype(jnp.int32) for end in ends)

    first_image = image(first_id)
    valid = (first_id >= 0) & (first_id < extent) & (second_id >= 0) & (second_id < extent)
    same = (valid & (first_image == image(second_id))).astype(F32)
    pairs = jnp.where(crop >= 0, (first_image == crop).astype(F32), base + slope * same)
    counts = crop_rows.astype(F32) * float(columns)
    table = jnp.concatenate([pairs, counts, jnp.pad(b_classes, (0, 32 - classes))])
    columns_up, columns_back = column_matrices(columns)
    halves = jnp.stack([gain_aspp, shift_aspp])
    halves = lax.dynamic_slice_in_dim(halves, core * half, half, 2)
    gains_sp = jnp.concatenate(
        [
            halves[:, :4].reshape(2, -1),
            jnp.pad(halves[:, 4], ((0, 0), (0, 3 * half))),
        ]
    )
    vectors = jnp.sum(triple.astype(F32), axis=1).reshape(n_y, 8, o_part).transpose(1, 0, 2)
    lows = vectors[6:, :, : gain_low.shape[0]].reshape(2, low_out)
    vectors = vectors[:6].reshape(6, branch)
    gain_1, gain_2, gain_p = vectors[0:2], vectors[2:4], vectors[4:6]
    gain_l = jnp.pad(lows, ((0, 0), (0, 128 - low_out)))
    (low_w,) = run_kernel(low_weight_kernel, [], [low_raw], [((3, 256, branch), BF)])
    moved = (feats, feats_other, low_rows, shard, low_w, classes_w, table, gains_sp)
    moved += (gain_1, gain_2, gain_p, gain_l)
    first, moved = lax.optimization_barrier((first, moved))
    feats, feats_other, low_rows, shard, low_w, classes_w, table, gains_sp = moved[:8]
    gain_1, gain_2, gain_p, gain_l = moved[8:]
    dec = lax.all_gather(shard, "z", axis=0, tiled=True)
    padded_w, a0, a1, a2, p1, p2, p3, m1, m2, m3 = run_kernel(
        product_kernel,
        [place],
        [feats, feats_other, first],
        [((c_in, 9 * wide_c), BF), part, part, part, edge10, edge10, edge2, edge10, edge10, edge2],
        [((tall * columns, 9 * wide_c), F32)],
    )
    edges = [
        hop_open(p1, STRIP, -1),
        hop_open(p2, STRIP, -2),
        hop_open(p3, STRIP, -3),
        hop_open(m1, STRIP, 1),
        hop_open(m2, STRIP, 2),
        hop_open(m3, STRIP, 3),
    ]
    n_strips = n_z * n_x
    spatial, payload = run_kernel(
        spatial_kernel,
        [table],
        [a0, a1, a2] + edges,
        [part, ((n_strips, 4, wide_c), F32)],
    )
    landed_sp = lax.all_to_all(payload, STRIP, 0, 0, tiled=True)
    pieces_w = ((2 * n_y, 4 * half, branch), BF)
    main_w, pool_w, shrink = run_kernel(
        functools.partial(shared_weight_kernel, w_low.shape[1]),
        [],
        [Lanes(dec, 6 * branch, 3)],
        [pieces_w, pieces_w, ((c_low, 128), BF)],
        [((2, w_proj.shape[0] * groups, 128), F32)],
    )
    low_z = dot("fcv,co->fvo", low_rows, shrink)
    low_sums = jnp.stack(
        [jnp.sum(low_z[2:6], axis=(0, 1)), jnp.sum(jnp.square(low_z[2:6]), axis=(0, 1))]
    )
    low_sums = jnp.pad(low_sums, ((0, 0), (0, branch - 128)))
    (payload,) = run_kernel(
        functools.partial(act_kernel, pixels),
        [table],
        [spatial, landed_sp, gains_sp],
        [((tall, columns + 16, wide_c), BF)],
    )

    landed = lax.all_to_all(payload, GROUP, 0, 0, tiled=True)
    n_first = 2 * n_x * n_y
    proj_z, payload = run_kernel(
        proj_kernel,
        [],
        [landed, main_w, pool_w, low_sums],
        [((columns, branch), F32), ((n_first, 4, branch), F32)],
    )

    def exchanged(block):
        block = lax.all_to_all(block, ("x", "core", "y"), 0, 0, tiled=True)
        (block,) = run_kernel(sum_kernel, [], [block], [((n_z,) + block.shape[1:], F32)])
        return lax.all_to_all(block, "z", 0, 0, tiled=True)

    proj_above = hop_open(proj_z, ALL, 1)
    proj_below = hop_open(proj_z, ALL, -1)
    landed_p = exchanged(payload)


    fine = (fine_columns, branch)
    sums2, sums4 = ((n_first, 2, branch), F32), ((n_first, 4, branch), F32)
    united_z, united_up, low_act, payload, moments_0 = run_kernel(
        functools.partial(unite_kernel, counts_static),
        [table],
        [
            proj_z,
            proj_above,
            proj_below,
            landed_p,
            gain_p,
            low_z,
            gain_l,
            columns_up,
            Lanes(dec, 9 * branch, 0),
            low_w,
        ],
        [
            ((6,) + fine, F32),
            ((6,) + fine, BF),
            ((6, fine_columns, 128), BF),
            sums2,
            ((4, branch), F32),
        ],
        [
            ((8, 3 * fine_columns, branch), BF),
            ((8, fine_columns, 256), BF),
            ((3, columns, branch), F32),
        ],
    )
    features, _ = lax.optimization_barrier((features, united_z))
    digits = features.reshape(rows_in, columns, c_part // (n_x * o_part), n_x, o_part)
    digits = jnp.moveaxis(digits, 3, 0).reshape(n_x, rows_in * columns, -1)
    by_x = [lax.dynamic_index_in_dim(digits, xi, 0, keepdims=False)]
    for k in range(1, n_x):
        piece = lax.dynamic_index_in_dim(digits, (xi + k) % n_x, 0, keepdims=False)
        by_x.append(hop(piece, "x", k))
    by_x = jnp.concatenate(by_x)
    landed_1 = exchanged(payload)
    hidden, refine_z, payload, moments_1 = run_kernel(
        functools.partial(refine_kernel, counts_static),
        [table],
        [united_z, landed_1, gain_1, Lanes(dec, 9 * branch, 1)],
        [((6,) + fine, BF), ((4,) + fine, F32), sums2, ((2, branch), F32)],
        [((6, 3 * fine_columns, branch), BF)],
    )
    landed_2 = exchanged(payload)
    by_x, landed_2 = lax.optimization_barrier((by_x, landed_2))
    feats_x = lax.all_gather(by_x, GROUP, axis=0, tiled=False)
    edge = ((2,) + fine, BF)
    gp_2, payload, moments_2, top, bottom, class_block = run_kernel(
        functools.partial(classes_kernel, images, classes, counts_static),
        [table],
        [refine_z, landed_2, gain_2, labels_own, classes_w],
        [
            ((4,) + fine, F32),
            sums4,
            ((2, branch), F32),
            edge,
            edge,
            ((n_y, 16, 10 * o_part), F32),
        ],
        [((32, branch), F32)],
    )
    edge_above = hop_open(top, ALL, 1)
    edge_below = hop_open(bottom, ALL, -1)
    landed_g2 = exchanged(payload)
    edge = (fine, BF)
    gp_1, taps_2, payload, top, bottom, total_2 = run_kernel(
        functools.partial(refine_back_kernel, counts_static),
        [table],
        [
            gp_2,
            refine_z,
            edge_above,
            edge_below,
            landed_g2,
            moments_2,
            gain_2,
            Lanes(dec, 9 * branch, 1),
            united_z,
            moments_1,
            gain_1,
        ],
        [
            ((4,) + fine, F32),
            ((4, 3 * fine_columns, branch), BF),
            sums2,
            edge,
            edge,
            ((4, branch), F32),
        ],
        [((2, 3 * fine_columns, branch), BF)],
    )
    edge_above = hop_open(top, ALL, 1)
    edge_below = hop_open(bottom, ALL, -1)
    landed_g1 = exchanged(payload)
    grad_lanes = 5 * 2 * o_part
    (refine_part,) = run_kernel(
        refine_weight_kernel,
        [table],
        [hidden, taps_2],
        [((n_y, groups, k_row * grad_lanes), BF)],
        [((branch, 128), F32)],
    )
    taps_1, to_rows, gp_l, low_back, total_1 = run_kernel(
        functools.partial(unite_back_kernel, counts_static),
        [table],
        [
            gp_1,
            united_z,
            edge_above,
            edge_below,
            landed_g1,
            moments_1,
            gain_1,
            Lanes(dec, 9 * branch, 0),
            low_w,
            columns_back,
            low_z,
            moments_0,
            gain_l,
        ],
        [
            ((4, 3 * fine_columns, branch), BF),
            ((3, columns, branch), F32),
            ((4, fine_columns, 128), F32),
            ((2, branch), F32),
            ((2, branch), F32),
        ],
        [((2, 3 * fine_columns, branch), BF), ((6,) + fine, BF)],
    )
    to_above = hop_open(to_rows[0], ALL, -1)
    to_below = hop_open(to_rows[2], ALL, 1)
    gp_p, payload = run_kernel(
        proj_back_sums_kernel,
        [],
        [to_rows[1], to_above, to_below, proj_z, moments_0, gain_p, low_back],
        [((columns, branch), F32), sums4],
    )
    taps_late, payload = lax.optimization_barrier((taps_1, payload))
    (unite_part,) = run_kernel(
        unite_weight_kernel,
        [table],
        [united_up, low_act, taps_late, class_block],
        [((n_y, groups, (k_row + 1) * grad_lanes), BF)],
        [((branch, 128), F32)],
    )
    landed_gp = exchanged(payload)
    payload, proj_part, total_p = run_kernel(
        functools.partial(proj_back_kernel, counts_static),
        [],
        [gp_p, proj_z, landed_gp, moments_0, gain_p, landed, main_w, pool_w],
        [
            ((2 * n_y, columns + 16, wide_c), BF),
            ((n_y, w_proj.shape[0] * groups // 2, 2 * o_part), BF),
            ((4, branch), F32),
        ],
        [((2, w_proj.shape[0] * groups, 128), F32)],
    )
    back = lax.all_to_all(payload, GROUP, 0, 0, tiled=True)
    gp_sp, payload = run_kernel(
        functools.partial(spatial_back_sums_kernel, pixels),
        [table],
        [back, spatial, landed_sp, gains_sp],
        [part, ((n_strips, 4, wide_c), F32)],
    )
    grad_low_z, shrink_part = run_kernel(
        functools.partial(low_back_kernel, fine_pixels),
        [],
        [gp_l, low_z, total_p, moments_0, gain_l, low_rows],
        [((4, low_out, fine_columns), BF), ((low_out, c_low), F32)],
    )
    shrink_part, grad_low_z, proj_part, payload = lax.optimization_barrier(
        (shrink_part, grad_low_z, proj_part, payload)
    )
    landed_gsp = lax.all_to_all(payload, STRIP, 0, 0, tiled=True)
    grad_sp, pool_grad, gain_grads = run_kernel(
        functools.partial(spatial_back_kernel, pixels),
        [table],
        [gp_sp, spatial, landed_sp, landed_gsp, gains_sp],
        [((tall, columns, wide_c), BF), ((8, wide_c), F32), ((4, wide_c), F32)],
    )

    group_rows = n_x * tall
    grad_low_all = gathered(grad_low_z, "y").reshape(fine_strip, low_out, fine_columns)
    shrink_own = lax.dynamic_slice_in_dim(shrink, yi * (c_low // n_y), c_low // n_y, 0)
    grad_low_level = dot("fov,co->fcv", grad_low_all, shrink_own[:, :low_out])

    late = jnp.concatenate(
        [proj_part, shrink_part.reshape(n_y, -1, 2 * o_part).astype(BF)], axis=1
    )
    late = scattered(late, "y").astype(BF)
    n_proj = proj_part.shape[1]
    shrink_sum = late[n_proj:].reshape(-1, groups, w_low.shape[0]).transpose(1, 0, 2)
    pieces = [
        scattered(refine_part, "y").astype(BF),
        scattered(unite_part, "y").astype(BF),
        late[:n_proj].reshape(groups, -1),
        shrink_sum.reshape(groups, -1),
    ]
    filled = sum(piece.shape[1] for piece in pieces)
    pieces = jnp.concatenate(pieces + [jnp.zeros((groups, -filled % 1024), BF)], axis=1)
    pieces = pieces.reshape(groups, -1, 128)
    pieces = pieces.reshape(n_z * n_x, 2, -1, 128)
    mine = lax.dynamic_index_in_dim(pieces, core, 1, keepdims=False).astype(F32)
    theirs = hop(lax.dynamic_index_in_dim(pieces, 1 - core, 1, keepdims=False), "core", 1)
    pieces = (mine + theirs.astype(F32)).astype(BF)
    hops = [hop(grad_sp, "x", k) for k in range(1, n_x)]
    pieces, hops[0] = lax.optimization_barrier((pieces, hops[0]))
    wide = jnp.zeros((n_x,) + grad_sp.shape, BF)
    for k, block in enumerate([grad_sp] + hops):
        wide = lax.dynamic_update_index_in_dim(wide, block, (xi - k) % n_x, 0)
    wide = wide.reshape(group_rows, columns, wide_c)
    reach_above = hop_open(wide[group_rows - REACH :], "z", 1)
    reach_below = hop_open(wide[:REACH], "z", -1)
    pieces = lax.all_to_all(pieces, STRIP, 0, 0, tiled=True)
    taps9 = (9, k_row, o_part)
    grad_refine, grad_unite_up, grad_proj, shrink_sum, rest = run_kernel(
        pieces_kernel,
        [],
        [pieces],
        [(taps9, F32), (taps9, F32), (w_proj.shape, F32), ((1, 128), F32), ((5, 128), BF)],
    )
    grad_refine, grad_unite_up = (
        g.reshape(3, 3, k_row, o_part).transpose(2, 0, 1, 3) for g in (grad_refine, grad_unite_up)
    )
    grad_shrink = shrink_sum[0, : w_low.size].reshape(-1, w_low.shape[0]).T
    rest = gathered(gathered(rest, "core"), "x").reshape(2 * n_x, grad_lanes)
    own_lanes = (tall * columns, 9 * wide_c)
    aspp_part, spread = run_kernel(
        spread_kernel,
        [place, table],
        [wide, reach_above, reach_below, pool_grad, feats_x, rest],
        [((n_z, o_part + 2 * n_x, 8 * wide_c), BF), (own_lanes, BF)],
        [
            ((group_rows * columns, 9 * wide_c), BF),
            ((group_rows + 2 * REACH, columns, wide_c), BF),
        ],
    )
    halves = ((n_y, rows_in * columns, c_part), BF)
    mine, theirs = run_kernel(feature_kernel, [place], [spread, padded_w], [halves, halves])

    aspp_sum = lax.all_to_all(aspp_part, "z", 0, 0, tiled=True)
    half_rows = (half, 8 * wide_c)
    mine_w, theirs_w, grad_unite_low, grad_classes = run_kernel(
        landed_kernel,
        [place],
        [aspp_sum],
        [(half_rows, F32), (half_rows, BF), ((9, low_out, o_part), F32), ((classes, o_part), F32)],
    )
    grad_unite_low = grad_unite_low.reshape(3, 3, low_out, o_part).transpose(2, 0, 1, 3)
    grad_classes = grad_classes.T
    theirs_w = hop(theirs_w, "core", 1)
    grad_atrous, grad_one, grad_pool = run_kernel(
        joined_kernel,
        [place],
        [mine_w, theirs_w],
        [((3, 3, 3, half, o_part), F32), ((half, o_part), F32), ((half, o_part), F32)],
    )
    grad_atrous = grad_atrous.transpose(3, 0, 1, 2, 4)

    theirs = hop(theirs, "core", 1)
    flat_part = (rows_in * columns, c_part)
    grad_features, sent = run_kernel(
        feature_sum_kernel,
        [place],
        [mine, theirs],
        [(flat_part, F32), ((n_y - 1,) + flat_part, BF)],
    )
    for k in range(1, n_y):
        grad_features = grad_features + hop(sent[k - 1], "y", k).astype(F32)
    grad_features = grad_features.reshape(features.shape)

    grad_bias = total_2[2, :classes]
    loss_value = jnp.sum(total_2[3]) / images
    both = gathered(gain_grads, "core")
    both = both.reshape(2, 2, 2, 4, half)
    both = jnp.concatenate([both[:, 0], both[:, 1, :, :1]], axis=2)
    both = both.transpose(1, 2, 0, 3).reshape(2, 5, o_part)

    def own_channels(vector):
        size = vector.shape[-1] // n_y
        return lax.dynamic_slice_in_dim(vector, yi * size, size, vector.ndim - 1)

    return (
        loss_value,
        grad_features,
        grad_low_level,
        grad_one,
        grad_atrous,
        grad_pool,
        grad_proj,
        grad_shrink,
        grad_unite_up,
        grad_unite_low,
        grad_refine,
        grad_classes,
        grad_bias,
        both[0],
        both[1],
        own_channels(total_p[0]),
        own_channels(total_p[1]),
        own_channels(total_p[2, :low_out]),
        own_channels(total_p[3, :low_out]),
        own_channels(jnp.stack([total_1[0], total_2[0]])),
        own_channels(jnp.stack([total_1[1], total_2[1]])),
    )


def solution(mesh):
    torus = Mesh(mesh.devices.reshape(8, 4, 2, mesh.shape["ch"]), ALL)
    in_specs = (
        P(ROWS, None, "y"),
        P(ROWS, None, None),
        P(ROWS, None),
        P(),
        P(ROWS, "y"),
        P(ROWS, None, None, None, "y"),
        P(ROWS, "y"),
        P(ROWS, "y"),
        P(ROWS, "y"),
        P(ROWS, None, None, "y"),
        P(None, None, None, "y"),
        P(ROWS, None, None, "y"),
        P("y", None),
        P(),
        P(None, "y"),
        P(None, "y"),
        P("y"),
        P("y"),
        P("y"),
        P("y"),
        P(None, "y"),
        P(None, "y"),
    )
    out_specs = (
        P(),
        P(ROWS, None, "y"),
        P(ROWS, "y", None),
        P(ROWS, "y"),
        P(ROWS, None, None, None, "y"),
        P(ROWS, "y"),
        P(ROWS, "y"),
        P(ROWS, "y"),
        P(ROWS, None, None, "y"),
        P(None, None, None, "y"),
        P(ROWS, None, None, "y"),
        P("y", None),
        P(),
        P(None, "y"),
        P(None, "y"),
        P("y"),
        P("y"),
        P("y"),
        P("y"),
        P(None, "y"),
        P(None, "y"),
    )
    return jax.shard_map(
        on_device, mesh=torus, in_specs=in_specs, out_specs=out_specs, check_vma=False
    )
```

```python
import functools

import jax
import jax.numpy as jnp
import numpy as np
from jax import lax
from jax.experimental import pallas as pl
from jax.experimental.pallas import tpu as pltpu
from jax.sharding import Mesh
from jax.sharding import PartitionSpec as P

DILATIONS = (6, 12, 18)
REACH = 18
EPSILON = 1e-05
BF = jnp.bfloat16
F32 = jnp.float32

ROWS = ("z", "x", "core")
ALL = ("z", "x", "core", "y")
STRIP = ("z", "x")
GROUP = ("core", "y")


def hop(block, axes, distance):
    n = lax.axis_size(axes)
    return lax.ppermute(block, axes, [(i, (i + distance) % n) for i in range(n)])


def hop_open(block, axes, distance):
    n = lax.axis_size(axes)
    route = [(i, i + distance) for i in range(n) if 0 <= i + distance < n]
    return lax.ppermute(block, axes, route)


def scattered(pieces, axis):
    n = lax.axis_size(axis)
    me = lax.axis_index(axis)
    own = lax.dynamic_index_in_dim(pieces, me, 0, keepdims=False).astype(F32)
    low = pieces.astype(BF)
    for k in range(1, n):
        piece = lax.dynamic_index_in_dim(low, (me + k) % n, 0, keepdims=False)
        own = own + hop(piece, axis, k).astype(F32)
    return own


def gathered(block, axis):
    n = lax.axis_size(axis)
    me = lax.axis_index(axis)
    out = jnp.zeros((n,) + block.shape, block.dtype)
    out = lax.dynamic_update_index_in_dim(out, block, me, 0)
    for k in range(1, n):
        out = lax.dynamic_update_index_in_dim(out, hop(block, axis, k), (me - k) % n, 0)
    return out


def shifted(values, step, axis):
    if step == 0:
        return values
    extent = values.shape[axis]
    pads = [(0, 0)] * values.ndim
    pads[axis] = (max(-step, 0), max(step, 0))
    padded = jnp.pad(values, pads)
    start = max(step, 0)
    return lax.slice_in_dim(padded, start, start + extent, axis=axis)


def taps(values, sign):
    return jnp.concatenate([shifted(values, sign * b, 2) for b in (-1, 0, 1)], axis=1)


def dot(spec, a, b):
    return jnp.einsum(spec, a, b, preferred_element_type=F32)


def column_matrices(columns):
    blend = np.zeros((4 * columns, columns), np.float32)
    for v in range(4 * columns):
        source, quarter = divmod(v, 4)
        near = source - 1 if quarter < 2 else source + 1
        share = (0.375 if quarter in (0, 3) else 0.125) if 0 <= near < columns else 0.0
        blend[v, source] += 1.0 - share
        if share:
            blend[v, near] += share
    edge = np.zeros((1, columns), np.float32)
    moved = [np.concatenate([edge, blend[:-1]]), blend, np.concatenate([blend[1:], edge])]
    grown = np.concatenate(moved)
    return jnp.asarray(np.concatenate([grown, grown], axis=1), BF), jnp.asarray(blend.T, BF)


VMEM = pltpu.VMEM
SMEM = pltpu.SMEM


def mm(a, b):
    return lax.dot_general(a, b, (((1,), (0,)), ((), ())), preferred_element_type=F32)


def mm_nt(a, b):
    return lax.dot_general(a, b, (((1,), (1,)), ((), ())), preferred_element_type=F32)


def mm_tn(a, b):
    return lax.dot_general(a, b, (((0,), (0,)), ((), ())), preferred_element_type=F32)


SPARE = (0, 2, 3)
LAYOUT = {}
for _name, _rows, _columns in (
    ("keep", 6, 3),
    ("keep_back", 4, 3),
    ("inside", 1, 8),
    ("blend", 8, 3),
    ("up", 3, 8),
    ("down", 3, 8),
    ("group", 9, 32),
    ("member", 8, 8),
    ("crowd", 32, 8),
    ("counts", 1, 8),
    ("bias", 1, 32),
):
    LAYOUT[_name] = (sum(r * c for _, r, c in LAYOUT.values()), _rows, _columns)


def pair_entries(tall, reach_rows):
    rows = []

    def add(fine, by, at, offset, base=0.0, slope=1.0, crop=-1):
        rows.append((fine, by == "row", by == "strip", by == "group", at, offset, base, slope, crop))

    for f in range(6):
        for a in range(3):
            add(1, "row", f - 1, a - 1)
    for f in range(4):
        for a in range(3):
            add(1, "row", f - (a - 1), a - 1)
    for f in range(8):
        add(1, "row", f - 2, 0)
    for f in range(8):
        source, quarter = divmod(f - 2, 4)
        step = -1 if quarter < 2 else 1
        share = 0.375 if quarter in (0, 3) else 0.125
        for k in range(3):
            target = k - 1
            if target == source:
                add(0, "row", source, step, 1.0, -share)
            elif target == source + step:
                add(0, "row", source, step, 0.0, share)
            else:
                add(0, "row", source, step, 0.0, 0.0)
    for sign in (-1, 1):
        for d in DILATIONS:
            for r in range(tall):
                add(0, "strip", r, sign * d)
    for d in DILATIONS:
        for a in range(3):
            for r in range(reach_rows):
                add(0, "group", r - (a - 1) * d, (a - 1) * d)
    for r in range(tall):
        for m in range(8):
            add(0, "strip", r, 0, crop=m)
    for r in range(reach_rows):
        for m in range(8):
            add(0, "group", r, 0, crop=m)
    return np.array(rows, np.float32).T


class Entries:
    def __init__(self, ref, name):
        self.ref = ref
        self.start, _, self.columns = LAYOUT[name]

    def __getitem__(self, index):
        if isinstance(index, tuple):
            return self.ref[self.start + index[0] * self.columns + index[1]]
        return self.ref[self.start + index]


def whole_block(shape):
    return pl.BlockSpec(shape, lambda i: (0,) * len(shape), pipeline_mode=pl.Buffered(1))


class Lanes:
    def __init__(self, array, width, index):
        self.array, self.shape, self.index = array, (array.shape[0], width), index

    def spec(self):
        return pl.BlockSpec(self.shape, lambda i: (0, self.index), pipeline_mode=pl.Buffered(1))


def run_kernel(body, scalars, arrays, outs, scratch=(), limit=56):
    specs = [a.spec() if isinstance(a, Lanes) else whole_block(a.shape) for a in arrays]
    arrays = [a.array if isinstance(a, Lanes) else a for a in arrays]
    return pl.pallas_call(
        body,
        grid=(1,),
        out_shape=[jax.ShapeDtypeStruct(shape, kind) for shape, kind in outs],
        in_specs=[pl.BlockSpec(memory_space=SMEM)] * len(scalars)
        + specs,
        out_specs=[whole_block(shape) for shape, _ in outs],
        scratch_shapes=[VMEM(shape, kind) for shape, kind in scratch],
        compiler_params=pltpu.CompilerParams(vmem_limit_bytes=limit * 2**20),
    )(*scalars, *arrays)


def tap_rows(values, step):
    if step == 0:
        return values
    extent = values.shape[0]
    ids = lax.broadcasted_iota(jnp.int32, values.shape, 0)
    moved = pltpu.roll(values, (-step) % extent, 0)
    return jnp.where((ids + step >= 0) & (ids + step < extent), moved, 0.0)


def column_sum(values):
    return jnp.sum(values, axis=0, keepdims=True)


def norm_of(total, count):
    mean = total[0:1] / count
    return mean, lax.rsqrt(total[1:2] / count - jnp.square(mean) + EPSILON)


def silu(pre):
    return pre * jax.nn.sigmoid(pre)


def slot_mask(shape, slot):
    lanes = lax.broadcasted_iota(jnp.int32, shape, len(shape) - 1)
    return (lanes >= 32 * slot) & (lanes < 32 * slot + 32)


def lane_roll(values, shift):
    shift = shift % 128
    return values if shift == 0 else pltpu.roll(values, shift, values.ndim - 1)


def product_kernel(
    place, mine_ref, theirs_ref, w_ref, pad_ref, a0_ref, a1_ref, a2_ref, p1, p2, p3, m1, m2, m3, acc
):
    n_y, rows, depth = mine_ref.shape
    block, n_x = 64, 4

    @pl.loop(0, w_ref.shape[0] // (block * n_x))
    def _(z):
        for hops in range(n_x):
            owner = lax.rem(place[0] - hops + n_x, n_x)
            source = pl.ds(pl.multiple_of((z * n_x + hops) * block, block), block)
            target = pl.ds(pl.multiple_of((z * n_x + owner) * block, block), block)
            for g in range(9):
                pad_ref[target, 128 * g : 128 * g + 96] = w_ref[source, 96 * g : 96 * g + 96]
                at = {1: 864, 4: 896}.get(g)
                if at is None:
                    pad_ref[target, 128 * g + 96 : 128 * g + 128] = jnp.zeros((block, 32), BF)
                else:
                    pad_ref[target, 128 * g + 96 : 128 * g + 128] = w_ref[source, at : at + 32]

    acc[...] = jnp.zeros_like(acc)

    @pl.loop(0, n_y)
    def _(i):
        owner = lax.rem(place[1] - i + n_y, n_y)
        deep = pl.ds(pl.multiple_of(owner * depth, depth), depth)
        own_rows = pl.ds(pl.multiple_of(place[2] * rows, rows), rows)
        other_rows = pl.ds(pl.multiple_of((1 - place[2]) * rows, rows), rows)
        acc[own_rows, :] += mm(mine_ref[i], pad_ref[deep, :])
        acc[other_rows, :] += mm(theirs_ref[i], pad_ref[deep, :])

    outs = (a0_ref, a1_ref, a2_ref)
    shape = a0_ref.shape
    columns = lax.broadcasted_iota(jnp.int32, shape, 1)
    for k, d in enumerate(DILATIONS):
        left, own, right = (
            acc[:, 128 * (3 * k + j) : 128 * (3 * k + j) + 128].reshape(shape) for j in range(3)
        )
        outs[k][...] = (
            own
            + jnp.where(columns >= d, pltpu.roll(left, d, 1), 0.0)
            + jnp.where(columns < shape[1] - d, pltpu.roll(right, shape[1] - d, 1), 0.0)
        )
    masks = [slot_mask(shape[1:], slot) for slot in range(4)]

    def pack(ref, pieces, lane):
        for block in range(ref.shape[0]):
            value = jnp.zeros(shape[1:], F32)
            for slot, (source, r) in enumerate(pieces[4 * block : 4 * block + 4]):
                value = jnp.where(masks[slot], lane_roll(source[r], 32 * (slot - lane)), value)
            ref[block] = value.astype(BF)

    pack(p1, [(a0_ref, r) for r in range(6)] + [(a1_ref, r) for r in range(4, 8)], 2)
    pack(p2, [(a1_ref, r) for r in range(4)] + [(a2_ref, r) for r in range(2, 8)], 2)
    pack(p3, [(a2_ref, r) for r in range(2)], 2)
    pack(m1, [(a0_ref, r) for r in range(2, 8)] + [(a1_ref, r) for r in range(4)], 0)
    pack(m2, [(a1_ref, r) for r in range(4, 8)] + [(a2_ref, r) for r in range(6)], 0)
    pack(m3, [(a2_ref, r) for r in range(6, 8)], 0)


def spatial_kernel(
    table, a0, a1, a2, p1, p2, p3, m1, m2, m3, out_ref, payload_ref
):
    up, down, member = (Entries(table, name) for name in ("up", "down", "member"))
    own = (a0, a1, a2)
    shape = out_ref.shape[1:]
    masks = [slot_mask(shape, slot) for slot in range(4)]

    def piece(ref, i, k):
        return lane_roll(ref[i // 4].astype(F32), 32 * (k + 1 - i % 4))

    def plus_of(k, r):
        if k == 0:
            return lane_roll(a0[6 + r], -32) if r < 2 else piece(p1, r - 2, k)
        if k == 1:
            return piece(p1, 6 + r, k) if r < 4 else piece(p2, r - 4, k)
        return piece(p2, 4 + r, k) if r < 6 else piece(p3, r - 6, k)

    def minus_of(k, r):
        if k == 0:
            return piece(m1, r, k) if r < 6 else lane_roll(a0[r - 6], 32)
        if k == 1:
            return piece(m2, r, k) if r < 4 else piece(m1, 2 + r, k)
        return piece(m3, r, k) if r < 2 else piece(m2, 2 + r, k)

    sums = jnp.zeros((1, 128), F32)
    squares = jnp.zeros((1, 128), F32)
    pools = []
    for r in range(out_ref.shape[0]):
        total = jnp.where(masks[0], lane_roll(a0[r], 32), 0.0)
        for k in range(3):
            term = (
                lane_roll(own[k][r], 32 * k)
                + up[k, r] * minus_of(k, r)
                + down[k, r] * plus_of(k, r)
            )
            total = jnp.where(masks[k + 1], term, total)
        out_ref[r] = total
        sums = sums + column_sum(total)
        squares = squares + column_sum(total * total)
        pools.append(lane_roll(column_sum(a1[r]), 32))
    first = slot_mask((1, 128), 0)
    packed = [jnp.zeros((1, 128), F32), jnp.zeros((1, 128), F32)]
    for m in range(8):
        part = sum(member[r, m] * pools[r] for r in range(len(pools)))
        packed[m // 4] = packed[m // 4] + lane_roll(jnp.where(first, part, 0.0), 32 * (m % 4))
    payload = jnp.concatenate([sums, squares] + packed, axis=0)
    payload_ref[...] = jnp.broadcast_to(payload[None], payload_ref.shape)


def pool_rows_of(total, slot_rows):
    first = slot_mask((1, 128), 0)
    rows = []
    for m in range(8):
        row = total[slot_rows + m // 4 : slot_rows + m // 4 + 1]
        rows.append(jnp.where(first, lane_roll(row, -32 * (m % 4)), 0.0))
    return rows


def pool_norm(total, counts, gains):
    rows = pool_rows_of(total, 2)
    z = jnp.concatenate([rows[m] / counts[m] for m in range(8)], axis=0)
    mean = jnp.mean(z, axis=0, keepdims=True)
    inverse = lax.rsqrt(jnp.mean(jnp.square(z - mean), axis=0, keepdims=True) + EPSILON)
    normed = (z - mean) * inverse
    return normed, inverse, normed * gains[2:3] + gains[3:4]


def act_kernel(pixels, table, spatial_ref, landed_ref, gains_ref, out_ref):
    counts, member = Entries(table, "counts"), Entries(table, "member")
    total = jnp.sum(landed_ref[...], axis=0)
    gains = gains_ref[...]
    mean, inverse = norm_of(total, pixels)
    _, _, pre = pool_norm(total, counts, gains)
    act = silu(pre)
    columns = spatial_ref.shape[1]
    first_row = lax.broadcasted_iota(jnp.int32, (16, 128), 0) == 0
    for r in range(spatial_ref.shape[0]):
        normed = (spatial_ref[r] - mean) * inverse
        out_ref[r, 0:columns] = silu(normed * gains[0:1] + gains[1:2]).astype(BF)
        row = sum(member[r, m] * act[m : m + 1] for m in range(8))
        row = jnp.where(slot_mask((1, 128), 0), row, 0.0)
        out_ref[r, columns : columns + 16] = jnp.where(first_row, row, 0.0).astype(BF)


def proj_kernel(landed_ref, main_ref, pool_ref, low_ref, out_ref, payload_ref):
    columns = out_ref.shape[0]
    acc = jnp.zeros(out_ref.shape, F32)
    extra = jnp.zeros((16, out_ref.shape[1]), F32)
    for s in range(landed_ref.shape[0]):
        acc = acc + mm(landed_ref[s, 0:columns], main_ref[s])
        extra = extra + mm(landed_ref[s, columns : columns + 16], pool_ref[s])
    z = acc + extra[0:1]
    out_ref[...] = z
    payload = jnp.concatenate([column_sum(z), column_sum(z * z), low_ref[...]], axis=0)
    payload_ref[...] = jnp.broadcast_to(payload[None], payload_ref.shape)


def sum_kernel(landed_ref, out_ref):
    total = jnp.sum(landed_ref[...], axis=0)
    out_ref[...] = jnp.broadcast_to(total[None], out_ref.shape)


def half_lanes(value, index):
    return lane_roll(value, -64 * index)[:, 0:64]


def pieces_kernel(landed_ref, refine_ref, unite_ref, proj_ref, shrink_ref, rest_ref):
    total = landed_ref[0].astype(F32)
    for i in range(1, landed_ref.shape[0]):
        total = total + landed_ref[i].astype(F32)
    for ref, start in ((refine_ref, 0), (unite_ref, 20)):
        for t in range(9):
            for c in range(4):
                row = start + 5 * c + t // 2
                ref[t, c : c + 1] = half_lanes(total[row : row + 1], t % 2)
    rest_ref[...] = total[40:45].astype(BF)
    for i in range(proj_ref.shape[0]):
        row = 45 + i // 2
        proj_ref[i : i + 1] = half_lanes(total[row : row + 1], i % 2)
    shrink_ref[...] = total[55:56]


def landed_kernel(place, landed_ref, mine_ref, theirs_ref, low_ref, classes_ref):
    block = landed_ref.shape[1] - 8
    total = landed_ref[0, 0:block].astype(F32)
    for z in range(1, landed_ref.shape[0]):
        total = total + landed_ref[z, 0:block].astype(F32)
    first, second = total[0 : block // 2], total[block // 2 :]
    zero = place[2] == 0
    mine_ref[...] = jnp.where(zero, first, second)
    theirs_ref[...] = jnp.where(zero, second, first).astype(BF)
    rows = low_ref.shape[1] // 8
    for t in range(9):
        at = 128 * (t // 2)
        for z in range(rows):
            part = landed_ref[z, block : block + 8, at : at + 128].astype(F32)
            low_ref[t, 8 * z : 8 * z + 8] = half_lanes(part, t % 2)
    tail = landed_ref[rows, block : block + 8, 0:640].astype(F32)
    for i in range(classes_ref.shape[0]):
        at = 128 * (i % 10 // 2)
        part = tail[i // 10 : i // 10 + 1, at : at + 128]
        classes_ref[i : i + 1] = half_lanes(part, i % 2)


def joined_kernel(place, mine_ref, theirs_ref, atrous_ref, one_ref, pool_ref):
    zero = place[2] == 0
    lanes = lax.broadcasted_iota(jnp.int32, (mine_ref.shape[0], 128), 1)
    for g in range(8):
        mine = mine_ref[:, 128 * g : 128 * g + 128]
        theirs = theirs_ref[:, 128 * g : 128 * g + 128].astype(F32)
        first, second = jnp.where(zero, mine, theirs), jnp.where(zero, theirs, mine)
        for a in range(4):
            pair = jnp.where(lanes < 32, lane_roll(first, -32 * a), lane_roll(second, 32 - 32 * a))
            if a < 3:
                atrous_ref[g // 3, a, g % 3] = pair[:, 0:64]
            elif g in SPARE:
                atrous_ref[2, SPARE.index(g), 2] = pair[:, 0:64]
            elif g == 1:
                one_ref[...] = pair[:, 0:64]
            elif g == 4:
                pool_ref[...] = pair[:, 0:64]


def low_weight_kernel(raw_ref, out_ref):
    out_ref[...] = jnp.zeros_like(out_ref)
    rows = raw_ref.shape[2]
    first = lax.broadcasted_iota(jnp.int32, (rows, 128), 1) < 64
    for t in range(9):
        a, b = t // 3, t % 3
        for j in range(2):
            left = raw_ref[2 * j, t // 2].astype(F32)
            right = raw_ref[2 * j + 1, t // 2].astype(F32)
            if t % 2 == 0:
                right = pltpu.roll(right, 64, 1)
            else:
                left = pltpu.roll(left, 64, 1)
            value = jnp.where(first, left, right).astype(BF)
            out_ref[a, 64 * b : 64 * b + rows, 128 * j : 128 * j + 128] = value


def shared_weight_kernel(low_part, dec_ref, main_ref, pool_ref, shrink_ref, rows_ref):
    height = dec_ref.shape[0]
    n_s = main_ref.shape[0]
    for q in range(5):
        for j in range(2):
            at = 256 * q + 128 * j
            rows_ref[j, pl.ds(q, height, stride=5), :] = dec_ref[:, at : at + 128].astype(F32)
    for s in range(n_s):
        place = 64 * (s % (n_s // 2)) + 32 * (s // (n_s // 2))
        for branch in range(4):
            at = 256 * branch + place
            for j in range(2):
                main_ref[s, 32 * branch : 32 * branch + 32, 128 * j : 128 * j + 128] = rows_ref[
                    j, at : at + 32
                ].astype(BF)
        at = 1024 + place
        for j in range(2):
            pool_ref[s, 0:32, 128 * j : 128 * j + 128] = rows_ref[j, at : at + 32].astype(BF)
        pool_ref[s, 32:128] = jnp.zeros((96, 256), BF)
    lanes = lax.broadcasted_iota(jnp.int32, (height, 128), 1)
    value = jnp.zeros((height, 128), F32)
    for y in range(4):
        at = 256 * 5 + 128 * (y // 2)
        moved = lane_roll(dec_ref[:, at : at + 128].astype(F32), low_part * y - 64 * (y % 2))
        value = jnp.where((lanes >= low_part * y) & (lanes < low_part * (y + 1)), moved, value)
    shrink_ref[...] = value.astype(BF)


def unite_kernel(
    counts,
    table,
    own_ref,
    above_ref,
    below_ref,
    landed_ref,
    gain_ref,
    low_all_ref,
    low_gain_ref,
    columns_ref,
    up_w_ref,
    low_w_ref,
    z_ref,
    up_ref,
    act_ref,
    payload_ref,
    moments_ref,
    taps_ref,
    low_taps_ref,
    coarse_ref,
):
    blend, keep, inside = (Entries(table, name) for name in ("blend", "keep", "inside"))
    total = jnp.sum(landed_ref[...], axis=0)
    mean, inverse = norm_of(total, counts[0])
    mean_l, inverse_l = norm_of(total[2:4, 0:128], counts[1])
    moments_ref[0:1] = mean
    moments_ref[1:2] = inverse
    moments_ref[2:3] = total[2:3] / counts[1]
    moments_ref[3:4] = lax.rsqrt(
        total[3:4] / counts[1] - jnp.square(total[2:3] / counts[1]) + EPSILON
    )
    gain = gain_ref[...]
    low_gain = low_gain_ref[...]
    for k, ref in enumerate((above_ref, own_ref, below_ref)):
        pre = (ref[...] - mean) * inverse * gain[0:1] + gain[1:2]
        coarse_ref[k] = silu(pre).astype(BF).astype(F32)
    width = z_ref.shape[1]

    @pl.loop(0, 8)
    def _(f):
        row = (
            blend[f, 0] * coarse_ref[0] + blend[f, 1] * coarse_ref[1] + blend[f, 2] * coarse_ref[2]
        )
        high = row.astype(BF)
        rest = (row - high.astype(F32)).astype(BF)
        grown = mm(columns_ref[...], jnp.concatenate([high, rest], axis=0)) * inside[f]
        taps_ref[f] = grown.astype(BF)
        pre = (low_all_ref[f] - mean_l) * inverse_l * low_gain[0:1] + low_gain[1:2]
        act = silu(pre).astype(BF).astype(F32) * inside[f]
        pair = tap_rows(act, -1) + pltpu.roll(act, 64, 1)
        low_taps_ref[f] = jnp.concatenate([pair, tap_rows(act, 1)], axis=1).astype(BF)

        @pl.when((f >= 1) & (f <= 6))
        def _():
            up_ref[f - 1] = grown[width : 2 * width].astype(BF)
            act_ref[f - 1] = act.astype(BF)

    payload_ref[...] = jnp.zeros_like(payload_ref)

    @pl.loop(0, 6)
    def _(f):
        acc = jnp.zeros(z_ref.shape[1:], F32)
        for a in range(3):
            part = mm(low_taps_ref[f + a], low_w_ref[a])
            for b in range(3):
                t = 3 * a + b
                part = part + mm(
                    taps_ref[f + a, b * width : (b + 1) * width, :],
                    up_w_ref[:, 256 * t : 256 * t + 256],
                )
            acc = acc + keep[f, a] * part
        z_ref[f] = acc

        @pl.when((f >= 1) & (f <= 4))
        def _():
            both = jnp.concatenate([column_sum(acc), column_sum(acc * acc)], axis=0)
            payload_ref[...] += jnp.broadcast_to(both[None], payload_ref.shape)


def refine_kernel(
    counts,
    table,
    z_in_ref,
    landed_ref,
    gain_ref,
    w_ref,
    hidden_ref,
    z_ref,
    payload_ref,
    moments_ref,
    taps_ref,
):
    keep, inside = Entries(table, "keep"), Entries(table, "inside")
    total = jnp.sum(landed_ref[...], axis=0)
    mean, inverse = norm_of(total, counts[1])
    moments_ref[0:1] = mean
    moments_ref[1:2] = inverse
    gain = gain_ref[...]
    width = z_ref.shape[1]

    @pl.loop(0, 6)
    def _(f):
        pre = (z_in_ref[f] - mean) * inverse * gain[0:1] + gain[1:2]
        hidden = silu(pre).astype(BF).astype(F32) * inside[f + 1]
        hidden_ref[f] = hidden.astype(BF)
        for b in range(3):
            taps_ref[f, b * width : (b + 1) * width, :] = tap_rows(hidden, b - 1).astype(BF)

    payload_ref[...] = jnp.zeros_like(payload_ref)

    @pl.loop(0, 4)
    def _(f):
        acc = jnp.zeros(z_ref.shape[1:], F32)
        for a in range(3):
            part = None
            for b in range(3):
                t = 3 * a + b
                term = mm(
                    taps_ref[f + a, b * width : (b + 1) * width, :],
                    w_ref[:, 256 * t : 256 * t + 256],
                )
                part = term if part is None else part + term
            acc = acc + keep[f + 1, a] * part
        z_ref[f] = acc
        both = jnp.concatenate([column_sum(acc), column_sum(acc * acc)], axis=0)
        payload_ref[...] += jnp.broadcast_to(both[None], payload_ref.shape)


def classes_kernel(
    images,
    classes,
    counts,
    table,
    z_ref,
    landed_ref,
    gain_ref,
    labels_ref,
    w_ref,
    gp_ref,
    payload_ref,
    moments_ref,
    top_ref,
    bottom_ref,
    block_ref,
    part_ref,
):
    entries = Entries(table, "bias")
    total = jnp.sum(landed_ref[...], axis=0)
    mean, inverse = norm_of(total, counts[1])
    moments_ref[0:1] = mean
    moments_ref[1:2] = inverse
    gain = gain_ref[...]
    weight = w_ref[...]
    width = z_ref.shape[1]
    shape = (weight.shape[0], width)
    ids = lax.broadcasted_iota(jnp.int32, shape, 0)
    ones = jnp.ones((8, width), BF)
    bias = jnp.zeros(shape, F32)
    for i in range(classes):
        bias = jnp.where(ids == i, entries[i], bias)
    rows = [jnp.zeros((1, 256), F32) for _ in range(4)]
    part_ref[...] = jnp.zeros_like(part_ref)
    for f in range(4):
        normed = (z_ref[f] - mean) * inverse
        pre = normed * gain[0:1] + gain[1:2]
        gate = jax.nn.sigmoid(pre)
        refined = (pre * gate).astype(BF)
        logits = mm_nt(weight, refined) + bias
        valid = ids < classes
        logits = jnp.where(valid, logits, -1e30)
        highest = jnp.max(logits, axis=0, keepdims=True)
        exponent = jnp.exp(logits - highest)
        exp_total = jnp.sum(exponent, axis=0, keepdims=True)
        one_hot = ids == labels_ref[f : f + 1, :]
        picked = jnp.sum(jnp.where(one_hot, logits, 0.0), axis=0, keepdims=True)
        rows[3] = rows[3] + jnp.log(exp_total) + highest - picked
        share = exponent / exp_total - jnp.where(one_hot, 1.0, 0.0)
        grad = jnp.where(valid, share / images, 0.0).astype(BF)
        part_ref[...] += mm(grad, refined)
        counted = mm_nt(ones, grad)[0:1]
        rows[2] = rows[2] + jnp.concatenate(
            [counted, jnp.zeros((1, 256 - shape[0]), F32)], axis=1
        )
        gp = mm_tn(grad, weight) * (gate * (1.0 + pre * (1.0 - gate)))
        gp_ref[f] = gp
        rows[0] = rows[0] + column_sum(gp * normed)
        rows[1] = rows[1] + column_sum(gp)
        if f == 0:
            bottom_ref[0] = gp.astype(BF)
            bottom_ref[1] = normed.astype(BF)
        if f == 3:
            top_ref[0] = gp.astype(BF)
            top_ref[1] = normed.astype(BF)
    payload = jnp.concatenate(rows, axis=0)
    payload_ref[...] = jnp.broadcast_to(payload[None], payload_ref.shape)
    block_ref[...] = jnp.zeros_like(block_ref)
    first = lax.broadcasted_iota(jnp.int32, (1, 128), 1) < 64
    for i in range(0, classes, 2):
        for j in range(2):
            one, two = (part_ref[i + n : i + n + 1, 128 * j : 128 * j + 128] for n in range(2))
            at = 128 * (i % 10 // 2)
            for n, value in enumerate(
                (
                    jnp.where(first, one, pltpu.roll(two, 64, 1)),
                    jnp.where(first, pltpu.roll(one, 64, 1), two),
                )
            ):
                block_ref[2 * j + n, i // 10 : i // 10 + 1, at : at + 128] = value


def grad_z(gp, normed, scale, total, count):
    return (scale * (gp - (total[1:2] + normed * total[0:1]) / count)).astype(BF)


def store_taps(ref, f, values):
    width = values.shape[0]
    wide = values.astype(F32)
    for b in range(3):
        ref[f, b * width : (b + 1) * width, :] = tap_rows(wide, 1 - b).astype(BF)


def refine_back_kernel(
    counts,
    table,
    gp_ref,
    z_ref,
    above_ref,
    below_ref,
    landed_ref,
    moments_ref,
    gain_ref,
    w_ref,
    z1_ref,
    moments1_ref,
    gain1_ref,
    out_ref,
    taps_ref,
    payload_ref,
    top_ref,
    bottom_ref,
    total_ref,
    ends_ref,
):
    keep, inside = Entries(table, "keep_back"), Entries(table, "inside")
    total = jnp.sum(landed_ref[...], axis=0)
    total_ref[...] = total
    mean, inverse = moments_ref[0:1], moments_ref[1:2]
    scale = gain_ref[0:1] * inverse
    count = counts[1]
    for ref, at, f in ((above_ref, 0, 0), (below_ref, 1, 5)):
        edge = grad_z(ref[0].astype(F32), ref[1].astype(F32), scale, total, count)
        store_taps(ends_ref, at, edge.astype(F32) * inside[f + 1])

    @pl.loop(0, 4)
    def _(f):
        normed = (z_ref[f] - mean) * inverse
        store_taps(taps_ref, f, grad_z(gp_ref[f], normed, scale, total, count))

    width = out_ref.shape[1]
    mean1, inverse1 = moments1_ref[0:1], moments1_ref[1:2]
    gain1 = gain1_ref[...]
    payload_ref[...] = jnp.zeros_like(payload_ref)
    for g in range(4):
        acc = jnp.zeros(out_ref.shape[1:], F32)
        for a in range(3):
            source = g + 1 - a
            if source < 0:
                rows = ends_ref.at[0]
            elif source > 3:
                rows = ends_ref.at[1]
            else:
                rows = taps_ref.at[source]
            part = None
            for b in range(3):
                t = 3 * a + b
                term = mm_nt(
                    rows[b * width : (b + 1) * width, :], w_ref[:, 256 * t : 256 * t + 256]
                )
                part = term if part is None else part + term
            acc = acc + keep[g, a] * part
        normed = (z1_ref[g + 1] - mean1) * inverse1
        pre = normed * gain1[0:1] + gain1[1:2]
        gate = jax.nn.sigmoid(pre)
        gp = acc * (gate * (1.0 + pre * (1.0 - gate)))
        out_ref[g] = gp
        both = jnp.concatenate([column_sum(gp * normed), column_sum(gp)], axis=0)
        payload_ref[...] += jnp.broadcast_to(both[None], payload_ref.shape)
        if g == 0:
            bottom_ref[...] = gp.astype(BF)
        if g == 3:
            top_ref[...] = gp.astype(BF)


def unite_back_kernel(
    counts,
    table,
    gp_ref,
    z_ref,
    above_ref,
    below_ref,
    landed_ref,
    moments_ref,
    gain_ref,
    up_w_ref,
    low_w_ref,
    columns_ref,
    low_z_ref,
    moments0_ref,
    low_gain_ref,
    taps_ref,
    rows_ref,
    low_gp_ref,
    sums_ref,
    total_ref,
    ends_ref,
    flat_ref,
):
    keep, inside, blend = (Entries(table, name) for name in ("keep_back", "inside", "blend"))
    total = jnp.sum(landed_ref[...], axis=0)
    total_ref[...] = total
    mean, inverse = moments_ref[0:1], moments_ref[1:2]
    scale = gain_ref[0:1] * inverse
    count = counts[1]
    for ref, at, f in ((above_ref, 0, 0), (below_ref, 1, 5)):
        normed = (z_ref[f] - mean) * inverse
        edge = grad_z(ref[...].astype(F32), normed, scale, total, count)
        edge = edge.astype(F32) * inside[f + 1]
        store_taps(ends_ref, at, edge)
        flat_ref[5 * at] = edge.astype(BF)

    @pl.loop(0, 4)
    def _(f):
        normed = (z_ref[f + 1] - mean) * inverse
        edge = grad_z(gp_ref[f], normed, scale, total, count)
        store_taps(taps_ref, f, edge)
        flat_ref[f + 1] = edge

    width = gp_ref.shape[1]
    mean_l, inverse_l = moments0_ref[2:3, 0:128], moments0_ref[3:4, 0:128]
    low_gain = low_gain_ref[...]
    first = lax.broadcasted_iota(jnp.int32, (width, 128), 1) < 64
    rows_ref[...] = jnp.zeros_like(rows_ref)
    sums = [jnp.zeros((1, 128), F32), jnp.zeros((1, 128), F32)]
    for g in range(4):
        acc = jnp.zeros(gp_ref.shape[1:], F32)
        low = jnp.zeros((width, 256), F32)
        for a in range(3):
            source = g + 1 - a
            if source < 0:
                rows = ends_ref.at[0]
            elif source > 3:
                rows = ends_ref.at[1]
            else:
                rows = taps_ref.at[source]
            part = None
            for b in range(3):
                t = 3 * a + b
                term = mm_nt(
                    rows[b * width : (b + 1) * width, :], up_w_ref[:, 256 * t : 256 * t + 256]
                )
                part = term if part is None else part + term
            acc = acc + keep[g, a] * part
            low = low + keep[g, a] * mm_nt(flat_ref[source + 1], low_w_ref[a])
        pair, last = low[:, 0:128], low[:, 128:256]
        low_in = (
            tap_rows(jnp.where(first, pair, 0.0), 1)
            + jnp.where(first, pltpu.roll(pair, 64, 1), 0.0)
            + tap_rows(last, -1)
        )
        grown = mm(columns_ref[...], acc.astype(BF))
        for k in range(3):
            rows_ref[k] += blend[g + 2, k] * grown
        normed = (low_z_ref[g + 2] - mean_l) * inverse_l
        pre = normed * low_gain[0:1] + low_gain[1:2]
        gate = jax.nn.sigmoid(pre)
        gp = low_in * (gate * (1.0 + pre * (1.0 - gate)))
        low_gp_ref[g] = gp
        sums[0] = sums[0] + column_sum(gp * normed)
        sums[1] = sums[1] + column_sum(gp)
    both = jnp.concatenate(sums, axis=0)
    sums_ref[...] = jnp.concatenate([both, jnp.zeros_like(both)], axis=1)


def tap_gradients(keep, h_ref, taps_ref, store):
    width = taps_ref.shape[1] // 3
    channels = h_ref.shape[2]
    first = lax.broadcasted_iota(jnp.int32, (channels, 128), 1) < 64
    other = None
    for t in range(9):
        a, b = t // 3, t % 3
        acc = jnp.zeros((channels, 256), F32)
        for f in range(4):
            acc = acc + keep[f + 1, a] * mm_tn(
                h_ref[f + a], taps_ref[f, b * width : (b + 1) * width, :]
            )
        if t % 2 == 0 and t < 8:
            other = acc
            continue
        x, y = (other, acc) if t % 2 == 1 else (acc, jnp.zeros_like(acc))
        for j in range(2):
            left, right = x[:, 128 * j : 128 * j + 128], y[:, 128 * j : 128 * j + 128]
            store(2 * j, 128 * (t // 2), jnp.where(first, left, pltpu.roll(right, 64, 1)))
            store(2 * j + 1, 128 * (t // 2), jnp.where(first, pltpu.roll(left, 64, 1), right))


def store_rows(out_ref, rows_ref):
    height = out_ref.shape[1]

    def store(y, at, value):
        rows_ref[...] = value
        for i in range(4):
            out_ref[y, :, 640 * i + at : 640 * i + at + 128] = rows_ref[
                pl.ds(i, height, stride=4), :
            ].astype(BF)

    return store


def refine_weight_kernel(table, h_ref, taps_ref, out_ref, rows_ref):
    tap_gradients(Entries(table, "keep"), h_ref, taps_ref, store_rows(out_ref, rows_ref))


def unite_weight_kernel(table, h_ref, act_ref, taps_ref, classes_ref, out_ref, rows_ref):
    keep = Entries(table, "keep")
    tap_gradients(keep, h_ref, taps_ref, store_rows(out_ref, rows_ref))

    def store_low(y, at, value):
        out_ref[y, 0:48, 2560 + at : 2560 + at + 128] = value[0:48].astype(BF)

    tap_gradients(keep, act_ref, taps_ref, store_low)
    out_ref[:, 48:64, 2560:3200] = classes_ref[...].astype(BF)


def low_back_kernel(count, gp_ref, z_ref, total_ref, moments_ref, gain_ref, low_ref, out_ref, part_ref):
    mean, inverse = moments_ref[2:3, 0:128], moments_ref[3:4, 0:128]
    total = total_ref[2:4, 0:128]
    scale = gain_ref[0:1] * inverse
    used = out_ref.shape[1]
    part = jnp.zeros(part_ref.shape, F32)
    for f in range(out_ref.shape[0]):
        normed = (z_ref[f + 2] - mean) * inverse
        grad = grad_z(gp_ref[f], normed, scale, total, count).astype(F32)
        turned = jnp.transpose(grad)[0:used].astype(BF)
        out_ref[f] = turned
        part = part + mm_nt(turned, low_ref[f + 2])
    part_ref[...] = part


def proj_back_sums_kernel(own_ref, above_ref, below_ref, z_ref, moments_ref, gain_ref, low_ref, gp_ref, payload_ref):
    normed = (z_ref[...] - moments_ref[0:1]) * moments_ref[1:2]
    pre = normed * gain_ref[0:1] + gain_ref[1:2]
    gate = jax.nn.sigmoid(pre)
    grad = own_ref[...] + above_ref[...] + below_ref[...]
    gp = grad * (gate * (1.0 + pre * (1.0 - gate)))
    gp_ref[...] = gp
    payload = jnp.concatenate([column_sum(gp * normed), column_sum(gp), low_ref[...]], axis=0)
    payload_ref[...] = jnp.broadcast_to(payload[None], payload_ref.shape)


def proj_back_kernel(
    counts,
    gp_ref,
    z_ref,
    landed_sums_ref,
    moments_ref,
    gain_ref,
    landed_ref,
    main_ref,
    pool_ref,
    out_ref,
    weight_ref,
    total_ref,
    rows_ref,
):
    total = jnp.sum(landed_sums_ref[...], axis=0)
    total_ref[...] = total
    mean, inverse = moments_ref[0:1], moments_ref[1:2]
    normed = (z_ref[...] - mean) * inverse
    grad = grad_z(gp_ref[...], normed, gain_ref[0:1] * inverse, total, counts[0])
    columns = grad.shape[0]
    summed = column_sum(grad.astype(F32))
    high = summed.astype(BF).astype(F32)
    first = lax.broadcasted_iota(jnp.int32, (16, 256), 0) == 0
    high_rows = jnp.where(first, high, 0.0).astype(BF)
    low_rows = jnp.where(first, summed - high, 0.0).astype(BF)
    top = lax.broadcasted_iota(jnp.int32, (16, 128), 0)
    n_s = out_ref.shape[0]
    for s in range(n_s):
        out_ref[s, 0:columns] = mm_nt(grad, main_ref[s]).astype(BF)
        pool = mm_nt(high_rows, pool_ref[s]) + mm_nt(low_rows, pool_ref[s])
        pool_high = pool[0:1].astype(BF).astype(F32)
        pair = jnp.where(top == 0, pool_high, jnp.where(top == 1, pool[0:1] - pool_high, 0.0))
        out_ref[s, columns : columns + 16] = pair.astype(BF)
        place = 64 * (s % (n_s // 2)) + 32 * (s // (n_s // 2))
        main = mm_tn(landed_ref[s, 0:columns], grad)
        for branch in range(4):
            at = 256 * branch + place
            for j in range(2):
                rows_ref[j, at : at + 32] = main[
                    32 * branch : 32 * branch + 32, 128 * j : 128 * j + 128
                ]
        extra = landed_ref[s, columns : columns + 16]
        outer = mm_tn(extra, high_rows) + mm_tn(extra, low_rows)
        for j in range(2):
            rows_ref[j, 1024 + place : 1024 + place + 32] = outer[0:32, 128 * j : 128 * j + 128]
    half = rows_ref.shape[1] // 2
    left = lax.broadcasted_iota(jnp.int32, (half, 128), 1) < 64
    for j in range(2):
        even = rows_ref[j, pl.ds(0, half, stride=2), :]
        odd = rows_ref[j, pl.ds(1, half, stride=2), :]
        weight_ref[2 * j] = jnp.where(left, even, pltpu.roll(odd, 64, 1)).astype(BF)
        weight_ref[2 * j + 1] = jnp.where(left, pltpu.roll(even, 64, 1), odd).astype(BF)


def spatial_back_sums_kernel(
    pixels, table, back_ref, spatial_ref, landed_ref, gains_ref, gp_ref, payload_ref
):
    member = Entries(table, "member")
    total = jnp.sum(landed_ref[...], axis=0)
    gains = gains_ref[...]
    mean, inverse = norm_of(total, pixels)
    columns = spatial_ref.shape[1]
    rows = [jnp.zeros((1, 128), F32), jnp.zeros((1, 128), F32)]
    pools = []
    for r in range(spatial_ref.shape[0]):
        normed = (spatial_ref[r] - mean) * inverse
        pre = normed * gains[0:1] + gains[1:2]
        gate = jax.nn.sigmoid(pre)
        gp = back_ref[r, 0:columns].astype(F32) * (gate * (1.0 + pre * (1.0 - gate)))
        gp_ref[r] = gp
        rows[0] = rows[0] + column_sum(gp * normed)
        rows[1] = rows[1] + column_sum(gp)
        pools.append(column_sum(back_ref[r, columns : columns + 16].astype(F32)))
    first = slot_mask((1, 128), 0)
    packed = [jnp.zeros((1, 128), F32), jnp.zeros((1, 128), F32)]
    for m in range(8):
        part = sum(member[r, m] * pools[r] for r in range(len(pools)))
        packed[m // 4] = packed[m // 4] + lane_roll(jnp.where(first, part, 0.0), 32 * (m % 4))
    payload = jnp.concatenate(rows + packed, axis=0)
    payload_ref[...] = jnp.broadcast_to(payload[None], payload_ref.shape)


def spatial_back_kernel(
    pixels,
    table,
    gp_ref,
    spatial_ref,
    landed_ref,
    landed_back_ref,
    gains_ref,
    out_ref,
    pool_ref,
    gains_out_ref,
):
    counts = Entries(table, "counts")
    total = jnp.sum(landed_ref[...], axis=0)
    back = jnp.sum(landed_back_ref[...], axis=0)
    gains = gains_ref[...]
    mean, inverse = norm_of(total, pixels)
    scale = gains[0:1] * inverse
    for r in range(spatial_ref.shape[0]):
        normed = (spatial_ref[r] - mean) * inverse
        out_ref[r] = grad_z(gp_ref[r], normed, scale, back, pixels)
    normed, inverse_p, pre = pool_norm(total, counts, gains)
    gate = jax.nn.sigmoid(pre)
    gp = jnp.concatenate(pool_rows_of(back, 2), axis=0) * (gate * (1.0 + pre * (1.0 - gate)))
    gain_grad = column_sum(gp * normed)
    shift_grad = column_sum(gp)
    grad = gains[2:3] * inverse_p * (gp - (shift_grad + normed * gain_grad) / 8.0)
    pool_ref[...] = jnp.concatenate([grad[m : m + 1] / counts[m] for m in range(8)], axis=0)
    gains_out_ref[...] = jnp.concatenate([back[0:2], gain_grad, shift_grad], axis=0)


def spread_kernel(
    place,
    table,
    wide_ref,
    above_ref,
    below_ref,
    pool_ref,
    feats_ref,
    rest_ref,
    weight_ref,
    own_ref,
    spread_ref,
    reach_ref,
):
    keep, crowd = Entries(table, "group"), Entries(table, "crowd")
    height = wide_ref.shape[0]
    columns = wide_ref.shape[1]
    reach_ref[0:REACH] = above_ref[...]
    reach_ref[REACH : REACH + height] = wide_ref[...]
    reach_ref[REACH + height :] = below_ref[...]
    shape = (columns, 128)
    masks = [slot_mask(shape, slot) for slot in range(4)]
    ids = lax.broadcasted_iota(jnp.int32, shape, 0)

    @pl.loop(0, height)
    def _(r):
        own = reach_ref[REACH + r].astype(F32)
        start = pl.multiple_of(r * columns, columns)
        for k, d in enumerate(DILATIONS):
            mixed = jnp.zeros(shape, F32)
            for a in range(3):
                source = own if a == 1 else reach_ref[REACH + r - (a - 1) * d].astype(F32)
                moved = lane_roll(source, 32 * (a - k - 1)) * keep[3 * k + a, r]
                mixed = jnp.where(masks[a], moved, mixed)
            left = jnp.where(ids < columns - d, pltpu.roll(mixed, columns - d, 0), 0.0)
            right = jnp.where(ids >= d, pltpu.roll(mixed, d, 0), 0.0)
            if k == 0:
                mixed = jnp.where(masks[3], lane_roll(own, 96), mixed)
            if k == 1:
                window = sum(crowd[r, m] * pool_ref[m : m + 1] for m in range(8))
                window = lane_roll(window, 96)
                mixed = jnp.where(masks[3], window, mixed)
            for j, value in enumerate((left, mixed, right)):
                at = 128 * (3 * k + j)
                spread_ref[pl.ds(start, columns), at : at + 128] = value.astype(BF)

    n_y = feats_ref.shape[0] // 2
    block = feats_ref.shape[1] * 8 // height
    strip = 2 * block
    wide = feats_ref.shape[2]

    @pl.loop(0, n_y)
    def _(y):
        acc = jnp.zeros((wide, spread_ref.shape[1]), F32)
        for core in range(2):
            for x in range(spread_ref.shape[0] // strip):
                turn = lax.rem(place[0] - x + 4, 4)
                acc = acc + mm_tn(
                    feats_ref[core * n_y + y, pl.ds(pl.multiple_of(turn * block, block), block), :],
                    spread_ref[x * strip + core * block : x * strip + (core + 1) * block, :],
                )
        half = wide // 2
        last = acc[:, 1024:1152]
        fourth = slot_mask((wide, 128), 3)
        for g in range(8):
            piece = acc[:, 128 * g : 128 * g + 128]
            if g in SPARE:
                piece = jnp.where(fourth, lane_roll(last, 32 * (3 - SPARE.index(g))), piece)
            for i in range(2):
                weight_ref[2 * y + i, 0:half, 128 * g : 128 * g + 128] = piece[
                    half * i : half * (i + 1)
                ].astype(BF)

    rows, lanes = rest_ref.shape
    for z in range(weight_ref.shape[0]):
        weight_ref[z, 64 : 64 + rows, 0:lanes] = rest_ref[...]
        weight_ref[z, 64 : 64 + rows, lanes:] = jnp.zeros((rows, weight_ref.shape[2] - lanes), BF)

    own_ref[...] = spread_ref[pl.ds(pl.multiple_of(place[0] * strip, strip), strip), :]


def feature_kernel(place, spread_ref, w_ref, mine_ref, theirs_ref):
    n_y, block, depth = mine_ref.shape
    own = pl.multiple_of(place[2] * block, block)
    other = pl.multiple_of((1 - place[2]) * block, block)

    @pl.loop(0, n_y)
    def _(y):
        weight = w_ref[pl.ds(pl.multiple_of(y * depth, depth), depth), :]
        theirs_ref[y] = mm_nt(spread_ref[pl.ds(other, block), :], weight).astype(BF)
        mine_ref[y] = mm_nt(spread_ref[pl.ds(own, block), :], weight).astype(BF)


def feature_sum_kernel(place, mine_ref, theirs_ref, own_ref, sent_ref):
    n_y = mine_ref.shape[0]

    def total(y):
        return mine_ref[y].astype(F32) + theirs_ref[y].astype(F32)

    own_ref[...] = total(place[1])
    for step in range(1, n_y):
        sent_ref[step - 1] = total(lax.rem(place[1] + step, n_y)).astype(BF)


def on_device(
    features,
    low_level,
    labels,
    crop_rows,
    w_one,
    w_atrous,
    w_pool,
    w_proj,
    w_low,
    w_unite_up,
    w_unite_low,
    w_refine,
    w_classes,
    b_classes,
    gain_aspp,
    shift_aspp,
    gain_proj,
    shift_proj,
    gain_low,
    shift_low,
    gain_dec,
    shift_dec,
):
    n_y, n_z, n_x = lax.axis_size("y"), lax.axis_size("z"), lax.axis_size("x")
    core, yi, xi, zi = (lax.axis_index(a) for a in ("core", "y", "x", "z"))
    strip = lax.axis_index(STRIP)
    row = lax.axis_index(ALL)
    groups = lax.axis_size(ROWS)
    rows_in, columns, c_part = features.shape
    total_rows = rows_in * groups
    c_in = c_part * n_y
    fine_strip, c_low, fine_columns = low_level.shape
    fine_total = fine_strip * groups
    branch = w_proj.shape[1] * n_y
    o_part = w_one.shape[1]
    half = o_part // 2
    low_out = w_low.shape[1] * n_y
    classes = w_classes.shape[1]
    images = crop_rows.shape[0]
    pixels = float(total_rows * columns)
    fine_pixels = float(fine_total * fine_columns)
    tall = 2 * rows_in
    counts_static = (pixels, fine_pixels)

    atrous = w_atrous.transpose(0, 1, 3, 2, 4).reshape(w_one.shape[0], 27, o_part)
    own = jnp.concatenate([atrous, w_one[:, None], w_pool[:, None]], axis=1)
    paired = lax.all_to_all(own, "core", 2, 0, tiled=True)
    paired = paired.reshape(paired.shape[0], -1)
    first = jnp.concatenate([paired] + [hop(paired, "x", k) for k in range(1, n_x)])
    inputs = (
        features,
        low_level,
        w_proj,
        w_low,
        w_unite_up,
        w_unite_low,
        w_refine,
        w_classes,
        gain_proj,
        shift_proj,
        gain_low,
        shift_low,
        gain_dec,
        shift_dec,
    )
    first, inputs = lax.optimization_barrier((first, inputs))
    (
        features,
        low_level,
        w_proj,
        w_low,
        w_unite_up,
        w_unite_low,
        w_refine,
        w_classes,
        gain_proj,
        shift_proj,
        gain_low,
        shift_low,
        gain_dec,
        shift_dec,
    ) = inputs
    first = lax.all_gather(first, "z", axis=0, tiled=True)

    flat_feats = features.reshape(-1, c_part)
    feats = jnp.stack([flat_feats] + [hop(flat_feats, "y", k) for k in range(1, n_y)])
    feats_other = hop(feats, "core", 1)

    k_row = w_refine.shape[0]
    shard = jnp.concatenate(
        [
            w_unite_up.reshape(k_row, 9, o_part),
            w_refine.reshape(k_row, 9, o_part),
            w_proj.reshape(k_row, -1, o_part),
            jnp.pad(w_low, ((0, 0), (0, o_part - w_low.shape[1])))[:, None],
        ],
        axis=1,
    )
    low_raw = jnp.pad(w_unite_low.reshape(low_out, 9, o_part), ((0, 0), (0, 1), (0, 0)))
    low_raw = low_raw.reshape(low_out, 5, 2 * o_part).transpose(1, 0, 2)
    class_raw = jnp.pad(w_classes.T, ((0, 32 - classes), (0, 0)))
    lows = jnp.pad(jnp.stack([gain_low, shift_low]), ((0, 0), (0, o_part - gain_low.shape[0])))
    vectors = jnp.concatenate(
        [
            jnp.stack([gain_dec, shift_dec], axis=1).reshape(4, -1),
            jnp.stack([gain_proj, shift_proj]),
            lows,
        ]
    ).reshape(4, 128)
    parts = []
    for _ in range(3):
        part = lax.reduce_precision(vectors, 8, 7)
        parts.append(part.astype(BF))
        vectors = vectors - part
    sizes = [shard.size, low_raw.size, class_raw.size]
    sent = [shard, low_raw, class_raw, jnp.concatenate(parts)]
    sent = jnp.concatenate([block.reshape(-1, 128) for block in sent])
    sent = gathered(sent, "y").reshape(n_y, -1)
    shard = sent[:, : sizes[0]].reshape(n_y, k_row, 24, o_part)
    shard = shard.transpose(1, 2, 0, 3).reshape(k_row, -1)
    low_raw = sent[:, sizes[0] : sizes[0] + sizes[1]].reshape((n_y,) + low_raw.shape)
    triple = sent[:, sum(sizes) :].reshape(n_y, 3, 4, 128)
    classes_w = sent[:, sizes[0] + sizes[1] : sum(sizes)].reshape(n_y, 32, o_part)
    classes_w = classes_w.transpose(1, 0, 2).reshape(32, branch)
    shard = gathered(gathered(shard, "core"), "x").reshape(-1, shard.shape[1])
    strips = [(r * n_y, (r + 1) * n_y) for r in range(groups - 1)]
    route = strips + [(target + n_y - 1, source + n_y - 1) for source, target in strips]
    edge = jnp.where(yi == 0, low_level[-2:], low_level[:2])
    edge = lax.ppermute(edge, ALL, route)
    low_rows = jnp.concatenate([edge, low_level, edge], axis=0)
    low_rows = lax.dynamic_slice_in_dim(low_rows, yi * 4, 8, 0)
    labels_own = lax.dynamic_slice_in_dim(labels, yi * 4, 4, 0)

    place = jnp.stack([xi, yi, core]).astype(jnp.int32)
    wide_c = 4 * half
    edge10, edge2 = ((3, columns, wide_c), BF), ((1, columns, wide_c), BF)
    part = ((tall, columns, wide_c), F32)
    later = (triple, crop_rows, b_classes, gain_aspp, shift_aspp)
    later, shard = lax.optimization_barrier((later, shard))
    triple, crop_rows, b_classes, gain_aspp, shift_aspp = later
    ends, reached = [], jnp.int32(0)
    for m in range(images):
        reached = reached + crop_rows[m]
        ends.append(reached)
    fine, by_row, by_strip, by_group, at, offset, base, slope, crop = pair_entries(tall, n_x * tall)
    fine, by_row, by_strip, by_group, at, offset, crop = (
        v.astype(np.int32) for v in (fine, by_row, by_strip, by_group, at, offset, crop)
    )
    scale = 1 + 3 * fine
    first_id = by_row * (scale * row) + by_strip * (tall * strip) + by_group * (n_x * tall * zi) + at
    second_id = first_id + offset
    extent = scale * total_rows

    def image(ids):
        return sum((ids >= scale * end).astype(jnp.int32) for end in ends)

    first_image = image(first_id)
    valid = (first_id >= 0) & (first_id < extent) & (second_id >= 0) & (second_id < extent)
    same = (valid & (first_image == image(second_id))).astype(F32)
    pairs = jnp.where(crop >= 0, (first_image == crop).astype(F32), base + slope * same)
    counts = crop_rows.astype(F32) * float(columns)
    table = jnp.concatenate([pairs, counts, jnp.pad(b_classes, (0, 32 - classes))])
    columns_up, columns_back = column_matrices(columns)
    halves = jnp.stack([gain_aspp, shift_aspp])
    halves = lax.dynamic_slice_in_dim(halves, core * half, half, 2)
    gains_sp = jnp.concatenate(
        [
            halves[:, :4].reshape(2, -1),
            jnp.pad(halves[:, 4], ((0, 0), (0, 3 * half))),
        ]
    )
    vectors = jnp.sum(triple.astype(F32), axis=1).reshape(n_y, 8, o_part).transpose(1, 0, 2)
    lows = vectors[6:, :, : gain_low.shape[0]].reshape(2, low_out)
    vectors = vectors[:6].reshape(6, branch)
    gain_1, gain_2, gain_p = vectors[0:2], vectors[2:4], vectors[4:6]
    gain_l = jnp.pad(lows, ((0, 0), (0, 128 - low_out)))
    (low_w,) = run_kernel(low_weight_kernel, [], [low_raw], [((3, 256, branch), BF)])
    moved = (feats, feats_other, low_rows, shard, low_w, classes_w, table, gains_sp)
    moved += (gain_1, gain_2, gain_p, gain_l)
    first, moved = lax.optimization_barrier((first, moved))
    feats, feats_other, low_rows, shard, low_w, classes_w, table, gains_sp = moved[:8]
    gain_1, gain_2, gain_p, gain_l = moved[8:]
    dec = lax.all_gather(shard, "z", axis=0, tiled=True)
    padded_w, a0, a1, a2, p1, p2, p3, m1, m2, m3 = run_kernel(
        product_kernel,
        [place],
        [feats, feats_other, first],
        [((c_in, 9 * wide_c), BF), part, part, part, edge10, edge10, edge2, edge10, edge10, edge2],
        [((tall * columns, 9 * wide_c), F32)],
    )
    edges = [
        hop_open(p1, STRIP, -1),
        hop_open(p2, STRIP, -2),
        hop_open(p3, STRIP, -3),
        hop_open(m1, STRIP, 1),
        hop_open(m2, STRIP, 2),
        hop_open(m3, STRIP, 3),
    ]
    n_strips = n_z * n_x
    spatial, payload = run_kernel(
        spatial_kernel,
        [table],
        [a0, a1, a2] + edges,
        [part, ((n_strips, 4, wide_c), F32)],
    )
    landed_sp = lax.all_to_all(payload, STRIP, 0, 0, tiled=True)
    pieces_w = ((2 * n_y, 4 * half, branch), BF)
    main_w, pool_w, shrink = run_kernel(
        functools.partial(shared_weight_kernel, w_low.shape[1]),
        [],
        [Lanes(dec, 6 * branch, 3)],
        [pieces_w, pieces_w, ((c_low, 128), BF)],
        [((2, w_proj.shape[0] * groups, 128), F32)],
    )
    low_z = dot("fcv,co->fvo", low_rows, shrink)
    low_sums = jnp.stack(
        [jnp.sum(low_z[2:6], axis=(0, 1)), jnp.sum(jnp.square(low_z[2:6]), axis=(0, 1))]
    )
    low_sums = jnp.pad(low_sums, ((0, 0), (0, branch - 128)))
    (payload,) = run_kernel(
        functools.partial(act_kernel, pixels),
        [table],
        [spatial, landed_sp, gains_sp],
        [((tall, columns + 16, wide_c), BF)],
    )

    landed = lax.all_to_all(payload, GROUP, 0, 0, tiled=True)
    n_first = 2 * n_x * n_y
    proj_z, payload = run_kernel(
        proj_kernel,
        [],
        [landed, main_w, pool_w, low_sums],
        [((columns, branch), F32), ((n_first, 4, branch), F32)],
    )

    def exchanged(block, edges=()):
        block = lax.all_to_all(block, ("x", "core", "y"), 0, 0, tiled=True)
        if edges:
            block, edges = lax.optimization_barrier((block, edges))
            edges = (hop_open(edges[0], ALL, 1), hop_open(edges[1], ALL, -1))
        (block,) = run_kernel(sum_kernel, [], [block], [((n_z,) + block.shape[1:], F32)])
        block = lax.all_to_all(block, "z", 0, 0, tiled=True)
        return (block, *edges) if edges else block

    proj_above = hop_open(proj_z, ALL, 1)
    proj_below = hop_open(proj_z, ALL, -1)
    landed_p = exchanged(payload)


    fine = (fine_columns, branch)
    sums2, sums4 = ((n_first, 2, branch), F32), ((n_first, 4, branch), F32)
    united_z, united_up, low_act, payload, moments_0 = run_kernel(
        functools.partial(unite_kernel, counts_static),
        [table],
        [
            proj_z,
            proj_above,
            proj_below,
            landed_p,
            gain_p,
            low_z,
            gain_l,
            columns_up,
            Lanes(dec, 9 * branch, 0),
            low_w,
        ],
        [
            ((6,) + fine, F32),
            ((6,) + fine, BF),
            ((6, fine_columns, 128), BF),
            sums2,
            ((4, branch), F32),
        ],
        [
            ((8, 3 * fine_columns, branch), BF),
            ((8, fine_columns, 256), BF),
            ((3, columns, branch), F32),
        ],
    )
    features, _ = lax.optimization_barrier((features, united_z))
    digits = features.reshape(rows_in, columns, c_part // (n_x * o_part), n_x, o_part)
    digits = jnp.moveaxis(digits, 3, 0).reshape(n_x, rows_in * columns, -1)
    by_x = [lax.dynamic_index_in_dim(digits, xi, 0, keepdims=False)]
    for k in range(1, n_x):
        piece = lax.dynamic_index_in_dim(digits, (xi + k) % n_x, 0, keepdims=False)
        by_x.append(hop(piece, "x", k))
    by_x = jnp.concatenate(by_x)
    landed_1 = exchanged(payload)
    hidden, refine_z, payload, moments_1 = run_kernel(
        functools.partial(refine_kernel, counts_static),
        [table],
        [united_z, landed_1, gain_1, Lanes(dec, 9 * branch, 1)],
        [((6,) + fine, BF), ((4,) + fine, F32), sums2, ((2, branch), F32)],
        [((6, 3 * fine_columns, branch), BF)],
    )
    landed_2 = exchanged(payload)
    by_x, landed_2 = lax.optimization_barrier((by_x, landed_2))
    feats_x = lax.all_gather(by_x, GROUP, axis=0, tiled=False)
    edge = ((2,) + fine, BF)
    gp_2, payload, moments_2, top, bottom, class_block = run_kernel(
        functools.partial(classes_kernel, images, classes, counts_static),
        [table],
        [refine_z, landed_2, gain_2, labels_own, classes_w],
        [
            ((4,) + fine, F32),
            sums4,
            ((2, branch), F32),
            edge,
            edge,
            ((n_y, 16, 10 * o_part), F32),
        ],
        [((32, branch), F32)],
    )
    landed_g2, edge_above, edge_below = exchanged(payload, (top, bottom))
    edge = (fine, BF)
    gp_1, taps_2, payload, top, bottom, total_2 = run_kernel(
        functools.partial(refine_back_kernel, counts_static),
        [table],
        [
            gp_2,
            refine_z,
            edge_above,
            edge_below,
            landed_g2,
            moments_2,
            gain_2,
            Lanes(dec, 9 * branch, 1),
            united_z,
            moments_1,
            gain_1,
        ],
        [
            ((4,) + fine, F32),
            ((4, 3 * fine_columns, branch), BF),
            sums2,
            edge,
            edge,
            ((4, branch), F32),
        ],
        [((2, 3 * fine_columns, branch), BF)],
    )
    landed_g1, edge_above, edge_below = exchanged(payload, (top, bottom))
    grad_lanes = 5 * 2 * o_part
    (refine_part,) = run_kernel(
        refine_weight_kernel,
        [table],
        [hidden, taps_2],
        [((n_y, groups, k_row * grad_lanes), BF)],
        [((branch, 128), F32)],
    )
    taps_1, to_rows, gp_l, low_back, total_1 = run_kernel(
        functools.partial(unite_back_kernel, counts_static),
        [table],
        [
            gp_1,
            united_z,
            edge_above,
            edge_below,
            landed_g1,
            moments_1,
            gain_1,
            Lanes(dec, 9 * branch, 0),
            low_w,
            columns_back,
            low_z,
            moments_0,
            gain_l,
        ],
        [
            ((4, 3 * fine_columns, branch), BF),
            ((3, columns, branch), F32),
            ((4, fine_columns, 128), F32),
            ((2, branch), F32),
            ((2, branch), F32),
        ],
        [((2, 3 * fine_columns, branch), BF), ((6,) + fine, BF)],
    )
    to_above = hop_open(to_rows[0], ALL, -1)
    to_below = hop_open(to_rows[2], ALL, 1)
    gp_p, payload = run_kernel(
        proj_back_sums_kernel,
        [],
        [to_rows[1], to_above, to_below, proj_z, moments_0, gain_p, low_back],
        [((columns, branch), F32), sums4],
    )
    taps_late, payload = lax.optimization_barrier((taps_1, payload))
    (unite_part,) = run_kernel(
        unite_weight_kernel,
        [table],
        [united_up, low_act, taps_late, class_block],
        [((n_y, groups, (k_row + 1) * grad_lanes), BF)],
        [((branch, 128), F32)],
    )
    landed_gp = exchanged(payload)
    payload, proj_part, total_p = run_kernel(
        functools.partial(proj_back_kernel, counts_static),
        [],
        [gp_p, proj_z, landed_gp, moments_0, gain_p, landed, main_w, pool_w],
        [
            ((2 * n_y, columns + 16, wide_c), BF),
            ((n_y, w_proj.shape[0] * groups // 2, 2 * o_part), BF),
            ((4, branch), F32),
        ],
        [((2, w_proj.shape[0] * groups, 128), F32)],
    )
    back = lax.all_to_all(payload, GROUP, 0, 0, tiled=True)
    gp_sp, payload = run_kernel(
        functools.partial(spatial_back_sums_kernel, pixels),
        [table],
        [back, spatial, landed_sp, gains_sp],
        [part, ((n_strips, 4, wide_c), F32)],
    )
    grad_low_z, shrink_part = run_kernel(
        functools.partial(low_back_kernel, fine_pixels),
        [],
        [gp_l, low_z, total_p, moments_0, gain_l, low_rows],
        [((4, low_out, fine_columns), BF), ((low_out, c_low), F32)],
    )
    shrink_part, grad_low_z, proj_part, payload = lax.optimization_barrier(
        (shrink_part, grad_low_z, proj_part, payload)
    )
    landed_gsp = lax.all_to_all(payload, STRIP, 0, 0, tiled=True)
    grad_sp, pool_grad, gain_grads = run_kernel(
        functools.partial(spatial_back_kernel, pixels),
        [table],
        [gp_sp, spatial, landed_sp, landed_gsp, gains_sp],
        [((tall, columns, wide_c), BF), ((8, wide_c), F32), ((4, wide_c), F32)],
    )

    group_rows = n_x * tall
    grad_low_all = gathered(grad_low_z, "y").reshape(fine_strip, low_out, fine_columns)
    shrink_own = lax.dynamic_slice_in_dim(shrink, yi * (c_low // n_y), c_low // n_y, 0)
    grad_low_level = dot("fov,co->fcv", grad_low_all, shrink_own[:, :low_out])

    late = jnp.concatenate(
        [proj_part, shrink_part.reshape(n_y, -1, 2 * o_part).astype(BF)], axis=1
    )
    late = scattered(late, "y").astype(BF)
    n_proj = proj_part.shape[1]
    shrink_sum = late[n_proj:].reshape(-1, groups, w_low.shape[0]).transpose(1, 0, 2)
    pieces = [
        scattered(refine_part, "y").astype(BF),
        scattered(unite_part, "y").astype(BF),
        late[:n_proj].reshape(groups, -1),
        shrink_sum.reshape(groups, -1),
    ]
    filled = sum(piece.shape[1] for piece in pieces)
    pieces = jnp.concatenate(pieces + [jnp.zeros((groups, -filled % 1024), BF)], axis=1)
    pieces = pieces.reshape(groups, -1, 128)
    pieces = pieces.reshape(n_z * n_x, 2, -1, 128)
    mine = lax.dynamic_index_in_dim(pieces, core, 1, keepdims=False).astype(F32)
    theirs = hop(lax.dynamic_index_in_dim(pieces, 1 - core, 1, keepdims=False), "core", 1)
    pieces = (mine + theirs.astype(F32)).astype(BF)
    hops = [hop(grad_sp, "x", k) for k in range(1, n_x)]
    pieces, hops[0] = lax.optimization_barrier((pieces, hops[0]))
    wide = jnp.zeros((n_x,) + grad_sp.shape, BF)
    for k, block in enumerate([grad_sp] + hops):
        wide = lax.dynamic_update_index_in_dim(wide, block, (xi - k) % n_x, 0)
    wide = wide.reshape(group_rows, columns, wide_c)
    reach_above = hop_open(wide[group_rows - REACH :], "z", 1)
    reach_below = hop_open(wide[:REACH], "z", -1)
    pieces = lax.all_to_all(pieces, STRIP, 0, 0, tiled=True)
    taps9 = (9, k_row, o_part)
    grad_refine, grad_unite_up, grad_proj, shrink_sum, rest = run_kernel(
        pieces_kernel,
        [],
        [pieces],
        [(taps9, F32), (taps9, F32), (w_proj.shape, F32), ((1, 128), F32), ((5, 128), BF)],
    )
    grad_refine, grad_unite_up = (
        g.reshape(3, 3, k_row, o_part).transpose(2, 0, 1, 3) for g in (grad_refine, grad_unite_up)
    )
    grad_shrink = shrink_sum[0, : w_low.size].reshape(-1, w_low.shape[0]).T
    rest = gathered(gathered(rest, "core"), "x").reshape(2 * n_x, grad_lanes)
    own_lanes = (tall * columns, 9 * wide_c)
    aspp_part, spread = run_kernel(
        spread_kernel,
        [place, table],
        [wide, reach_above, reach_below, pool_grad, feats_x, rest],
        [((n_z, o_part + 2 * n_x, 8 * wide_c), BF), (own_lanes, BF)],
        [
            ((group_rows * columns, 9 * wide_c), BF),
            ((group_rows + 2 * REACH, columns, wide_c), BF),
        ],
    )
    halves = ((n_y, rows_in * columns, c_part), BF)
    mine, theirs = run_kernel(feature_kernel, [place], [spread, padded_w], [halves, halves])

    aspp_sum = lax.all_to_all(aspp_part, "z", 0, 0, tiled=True)
    half_rows = (half, 8 * wide_c)
    mine_w, theirs_w, grad_unite_low, grad_classes = run_kernel(
        landed_kernel,
        [place],
        [aspp_sum],
        [(half_rows, F32), (half_rows, BF), ((9, low_out, o_part), F32), ((classes, o_part), F32)],
    )
    grad_unite_low = grad_unite_low.reshape(3, 3, low_out, o_part).transpose(2, 0, 1, 3)
    grad_classes = grad_classes.T
    theirs_w = hop(theirs_w, "core", 1)
    grad_atrous, grad_one, grad_pool = run_kernel(
        joined_kernel,
        [place],
        [mine_w, theirs_w],
        [((3, 3, 3, half, o_part), F32), ((half, o_part), F32), ((half, o_part), F32)],
    )
    grad_atrous = grad_atrous.transpose(3, 0, 1, 2, 4)

    theirs = hop(theirs, "core", 1)
    flat_part = (rows_in * columns, c_part)
    grad_features, sent = run_kernel(
        feature_sum_kernel,
        [place],
        [mine, theirs],
        [(flat_part, F32), ((n_y - 1,) + flat_part, BF)],
    )
    for k in range(1, n_y):
        grad_features = grad_features + hop(sent[k - 1], "y", k).astype(F32)
    grad_features = grad_features.reshape(features.shape)

    grad_bias = total_2[2, :classes]
    loss_value = jnp.sum(total_2[3]) / images
    both = gathered(gain_grads, "core")
    both = both.reshape(2, 2, 2, 4, half)
    both = jnp.concatenate([both[:, 0], both[:, 1, :, :1]], axis=2)
    both = both.transpose(1, 2, 0, 3).reshape(2, 5, o_part)

    def own_channels(vector):
        size = vector.shape[-1] // n_y
        return lax.dynamic_slice_in_dim(vector, yi * size, size, vector.ndim - 1)

    return (
        loss_value,
        grad_features,
        grad_low_level,
        grad_one,
        grad_atrous,
        grad_pool,
        grad_proj,
        grad_shrink,
        grad_unite_up,
        grad_unite_low,
        grad_refine,
        grad_classes,
        grad_bias,
        both[0],
        both[1],
        own_channels(total_p[0]),
        own_channels(total_p[1]),
        own_channels(total_p[2, :low_out]),
        own_channels(total_p[3, :low_out]),
        own_channels(jnp.stack([total_1[0], total_2[0]])),
        own_channels(jnp.stack([total_1[1], total_2[1]])),
    )


def solution(mesh):
    torus = Mesh(mesh.devices.reshape(8, 4, 2, mesh.shape["ch"]), ALL)
    in_specs = (
        P(ROWS, None, "y"),
        P(ROWS, None, None),
        P(ROWS, None),
        P(),
        P(ROWS, "y"),
        P(ROWS, None, None, None, "y"),
        P(ROWS, "y"),
        P(ROWS, "y"),
        P(ROWS, "y"),
        P(ROWS, None, None, "y"),
        P(None, None, None, "y"),
        P(ROWS, None, None, "y"),
        P("y", None),
        P(),
        P(None, "y"),
        P(None, "y"),
        P("y"),
        P("y"),
        P("y"),
        P("y"),
        P(None, "y"),
        P(None, "y"),
    )
    out_specs = (
        P(),
        P(ROWS, None, "y"),
        P(ROWS, "y", None),
        P(ROWS, "y"),
        P(ROWS, None, None, None, "y"),
        P(ROWS, "y"),
        P(ROWS, "y"),
        P(ROWS, "y"),
        P(ROWS, None, None, "y"),
        P(None, None, None, "y"),
        P(ROWS, None, None, "y"),
        P("y", None),
        P(),
        P(None, "y"),
        P(None, "y"),
        P("y"),
        P("y"),
        P("y"),
        P("y"),
        P(None, "y"),
        P(None, "y"),
    )
    return jax.shard_map(
        on_device, mesh=torus, in_specs=in_specs, out_specs=out_specs, check_vma=False
    )
```
